32 devices in a mesh: dp: 4 (over z), expert: 2 (over y), tensor: 4 (over x, core).
Axes of the slice: x: 2, y: 2, z: 4, core: 2. Of those that a mesh axis runs over, the one named last changes fastest.
Arguments:
- tokens: bfloat16 [8192, 768], P(('dp', 'expert', 'tensor')), may hold values from -6 to 6
- cotangent: bfloat16 [8192, 768], P(('dp', 'expert', 'tensor')), may hold values from -6 to 6
- timesteps: int32 [32], P(('dp', 'expert')), may hold values from 0 to 999
- ada_weight: bfloat16 [768, 6, 768], P(None, None, 'tensor'), may hold values from -0.4375 to 0.4375
- ada_bias: float32 [6, 768], P(None, 'tensor'), may hold values from -1.5 to 1.5
- qkv_weight: bfloat16 [768, 3, 768], P(None, None, 'tensor'), may hold values from -0.21875 to 0.21875
- out_weight: bfloat16 [768, 768], P('tensor'), may hold values from -0.875 to 0.875
- router_weight: bfloat16 [768, 8], replicated, may hold values from -0.15625 to 0.15625
- shared_up: bfloat16 [768, 3072], P(None, 'tensor'), may hold values from -0.21875 to 0.21875
- shared_down: bfloat16 [3072, 768], P('tensor'), may hold values from -0.109375 to 0.109375
- expert_up: bfloat16 [8, 768, 3072], P('expert', None, 'tensor'), may hold values from -0.21875 to 0.21875
- expert_down: bfloat16 [8, 3072, 768], P('expert', 'tensor'), may hold values from -0.109375 to 0.109375
- routes: int32 [8192, 2], P(('dp', 'expert', 'tensor')), may hold values from 0 to 7, as said below
- places: int32 [8192, 2], P(('dp', 'expert', 'tensor')), may hold values from 0 to 80, as said below
Outputs:
- output: bfloat16 [8192, 768], P(('dp', 'expert', 'tensor'))
- grad_tokens: float32 [8192, 768], P(('dp', 'expert', 'tensor'))
- grad_ada_weight: float32 [768, 6, 768], P(None, None, 'tensor')
- grad_ada_bias: float32 [6, 768], P(None, 'tensor')
- grad_qkv_weight: float32 [768, 3, 768], P(None, None, 'tensor')
- grad_out_weight: float32 [768, 768], P('tensor')
- grad_router_weight: float32 [768, 8], replicated
- grad_shared_up: float32 [768, 3072], P(None, 'tensor')
- grad_shared_down: float32 [3072, 768], P('tensor')
- grad_expert_up: float32 [8, 768, 3072], P('expert', None, 'tensor')
- grad_expert_down: float32 [8, 3072, 768], P('expert', 'tensor')
- expert_counts: int32 [8], replicated
The draws below stay inside these ranges and needn't reach their ends.
Inputs may be any that keep to these rules, and one draw needn't show every extreme that they name: `routes`: each row names two different experts. places[p, k] is the smaller of 80 and the number of pairs (p', k') that come before (p, k), in the order of patches and then of k, within the same aligned block of 256 rows and name the same expert as routes[p, k]. Pairs with a place of 80 are dropped.
All inputs are finite; a program needn't handle non-finite values.
Results may differ from the reference program's by a relative error of at most 0.0165.
The reference program's roundings to bfloat16 on the way count: a program that leaves them out, or rounds other values in their place, can miss the bound.
Values may be sent and summed in bfloat16 or wider, within the bound.
No kernel may reach another device: no remote copies, remote signals or barrier semaphores. Data moves between devices by JAX's collectives and lax.ppermute only.
A program may use at most 192 MiB of HBM per device.

```python
import math
import jax
import jax.numpy as jnp
import numpy as np
from jax import lax

D = 768
HEADS = 12
HD = 64
FF = 3072
EXPERTS = 8
TOPK = 2
PATCHES = 256
TOK_DEV = 256
CAP = 80
TOKENS = 8192
IMAGES = 32


def route_pairs(key):
    order = jax.random.permutation(jax.random.fold_in(key, 11), EXPERTS)
    table = jnp.asarray(np.repeat(np.arange(8), np.array([4, 3, 2, 2, 2, 1, 1, 1])), jnp.int32)
    picked = jax.random.randint(jax.random.fold_in(key, 12), (TOKENS,), 0, 16)
    first_expert = order[table[picked]].astype(jnp.int32)
    stride = jax.random.randint(jax.random.fold_in(key, 13), (TOKENS,), 1, EXPERTS)
    second_expert = ((first_expert + stride) % EXPERTS).astype(jnp.int32)
    routes = jnp.stack([first_expert, second_expert], axis=1).astype(jnp.int32)
    blocks = TOKENS // TOK_DEV
    one_hot = (routes.reshape(blocks, TOK_DEV * 2, 1) == jnp.arange(EXPERTS, dtype=jnp.int32)[None, None, :]).astype(jnp.int32)
    before = jnp.cumsum(one_hot, axis=1) - one_hot
    places = jnp.sum(before * one_hot, axis=2).reshape(TOKENS, 2).astype(jnp.int32)
    places = jnp.minimum(places, CAP).astype(jnp.int32)
    return (routes, places)


def draw_routes(key, part):
    return route_pairs(key)[0]


def draw_places(key, part):
    return route_pairs(key)[1]


def touch_ends(drawn, stream_key, smallest, top_value):
    longest = drawn.shape.index(max(drawn.shape))
    spots = []
    for shift in (0, 1):
        where = [jax.random.randint(jax.random.fold_in(stream_key, axis), (), 0, length) for axis, length in enumerate(drawn.shape)]
        where[longest] = (where[longest] + shift) % drawn.shape[longest]
        spots.append(tuple(where))
    return drawn.at[spots[0]].set(smallest).at[spots[1]].set(top_value)


def block_levels(key, dims, shards, smallest, largest):
    def one(dim, shards_of):
        heights = jax.random.uniform(jax.random.fold_in(jax.random.fold_in(key, 6), dim), (shards_of,), jnp.float32, smallest / len(shards), largest / len(shards))
        return jnp.repeat(jnp.exp(heights), dims[dim] // shards_of).reshape((-1,) + (1,) * (len(dims) - dim - 1))

    factor_of = one(*shards[0])
    for cut in shards[1:]:
        factor_of = factor_of * one(*cut)
    return factor_of


def scatter_about(rng, extent, width, most, pieces=(), kind=jnp.bfloat16):
    level = block_levels(rng, extent, pieces, -0.22, 0.18) if pieces else 1.0
    result = jax.random.normal(rng, extent, jnp.float32) * width * level
    return jnp.minimum(jnp.maximum(result, -most), most).astype(kind)


def setup_inputs(seed: int = 0) -> dict:
    splits = jax.random.split(jax.random.key(seed), 15)
    tokens = scatter_about(splits[0], (TOKENS, D), 1.0, 6.0, ((0, 32),))
    cotangent = scatter_about(splits[1], (TOKENS, D), 1.0, 6.0, ((0, 32),))
    timesteps = touch_ends(jax.random.randint(splits[2], (IMAGES,), 0, 1000), jax.random.fold_in(splits[2], 1), 0, 999).astype(jnp.int32)
    ada_weight = scatter_about(splits[3], (D, 6, D), (D // 4) ** -0.5, 0.4375, ((2, 4),))
    ada_bias = scatter_about(splits[4], (6, D), 0.3, 1.5, ((1, 4),), jnp.float32)
    qkv_weight = scatter_about(splits[5], (D, 3, D), D ** -0.5, 0.21875, ((2, 4),))
    out_weight = scatter_about(splits[6], (D, D), (D // 16) ** -0.5, 0.875, ((0, 4),))
    router_weight = scatter_about(splits[7], (D, EXPERTS), (2 * D) ** -0.5, 0.15625)
    shared_up = scatter_about(splits[8], (D, FF), D ** -0.5, 0.21875, ((1, 4),))
    shared_down = scatter_about(splits[9], (FF, D), FF ** -0.5, 0.109375, ((0, 4),))
    expert_up = scatter_about(splits[10], (EXPERTS, D, FF), D ** -0.5, 0.21875, ((0, 2), (2, 4)))
    expert_down = scatter_about(splits[11], (EXPERTS, FF, D), FF ** -0.5, 0.109375, ((0, 2), (1, 4)))
    routes = draw_routes(jax.random.fold_in(splits[14], 71), 0)
    places = draw_places(jax.random.fold_in(splits[14], 71), 0)
    return dict(tokens=tokens, cotangent=cotangent, timesteps=timesteps, ada_weight=ada_weight, ada_bias=ada_bias, qkv_weight=qkv_weight, out_weight=out_weight, router_weight=router_weight, shared_up=shared_up, shared_down=shared_down, expert_up=expert_up, expert_down=expert_down, routes=routes, places=places)


HIGHEST_PRECISION = lax.Precision.HIGHEST

@jax.custom_vjp
def low(v):
    return lax.optimization_barrier(v.astype(jnp.bfloat16)).astype(jnp.float32)

@jax.custom_vjp
def low_back(v):
    return v

def low_keep(v):
    return (low(v), None)

def low_pass(kept, grad):
    return (grad,)

def back_keep(v):
    return (v, None)

def back_low(kept, grad):
    return (low(grad),)
low.defvjp(low_keep, low_pass)
low_back.defvjp(back_keep, back_low)

def low_both(values):
    return low_back(low(values))

def tanh_gelu(values):
    return jax.nn.gelu(values, approximate=True)

def normalize(values):
    center = lax.optimization_barrier(jnp.mean(values, axis=-1, keepdims=True))
    shifted = values - center
    return shifted * lax.rsqrt(lax.optimization_barrier(jnp.mean(shifted * shifted, axis=-1, keepdims=True)) + 1e-06)

def embedding(steps):
    half_width = D // 2
    freqs_all = jnp.exp(-math.log(10000.0) * jnp.arange(half_width, dtype=jnp.float32) / half_width)
    angles = steps.astype(jnp.float32)[:, None] * freqs_all[None, :]
    return jnp.concatenate([jnp.cos(angles), jnp.sin(angles)], axis=1)

def attend(block_in, qkv_w, out_w):
    number = block_in.shape[0]
    triple = jnp.einsum('bpd,dcf->bpcf', block_in, qkv_w, precision=HIGHEST_PRECISION)
    triple = low_both(triple).reshape(number, PATCHES, 3, HEADS, HD)
    queries = triple[:, :, 0]
    keys_all = triple[:, :, 1]
    values_all = triple[:, :, 2]
    scores = low_back(jnp.einsum('bphd,bqhd->bhpq', queries, keys_all, precision=HIGHEST_PRECISION) / math.sqrt(HD))
    soft_weights = jax.nn.softmax(scores, axis=-1)
    context = low_both(jnp.einsum('bhpq,bqhd->bphd', low(soft_weights), values_all, precision=HIGHEST_PRECISION))
    return low_back(jnp.einsum('bpf,fd->bpd', context.reshape(number, PATCHES, D), out_w, precision=HIGHEST_PRECISION))

def feed(inputs, weight_in, weight_out):
    pre_act = low_back(jnp.dot(inputs, weight_in, precision=HIGHEST_PRECISION))
    return low_back(jnp.dot(low(tanh_gelu(pre_act)), weight_out, precision=HIGHEST_PRECISION))

def pick_rows(block_rows, block_index):
    return block_rows[block_index]

def forward(stream_in, ada_w, ada_b, qkv_w, out_w, router_w, s_up, s_down, e_up, e_down, steps, routes, places):
    images = steps.shape[0]
    condition = low(jax.nn.silu(embedding(steps)))
    modulation = jnp.einsum('id,dcf->icf', condition, ada_w, precision=HIGHEST_PRECISION) + ada_b[None]
    shift_one, scale_one, gate_one, shift_two, scale_two, gate_two = [modulation[:, column, None, :] for column in range(6)]
    stream = stream_in.reshape(images, PATCHES, D)
    attn_in = low(normalize(stream) * (1.0 + scale_one) + shift_one)
    image_block = math.gcd(images, 16)
    attn_out = lax.map(jax.checkpoint(lambda block_in: attend(block_in, qkv_w, out_w)), attn_in.reshape(images // image_block, image_block, PATCHES, D)).reshape(images, PATCHES, D)
    residual = stream + gate_one * attn_out
    moe_in = low(normalize(residual) * (1.0 + scale_two) + shift_two).reshape(-1, D)
    logits = low_back(jnp.dot(moe_in, router_w, precision=HIGHEST_PRECISION))
    pair_hot = (routes[:, :, None] == jnp.arange(EXPERTS, dtype=jnp.int32)[None, None, :]).astype(jnp.float32)
    pair_gates = jax.nn.softmax(lax.optimization_barrier(jnp.sum(pair_hot * logits[:, None, :], axis=2)), axis=1)
    kept_pair = (places < CAP).astype(jnp.float32)
    total_rows = moe_in.shape[0]
    share_block = math.gcd(total_rows, 4096)
    shared_out = lax.map(jax.checkpoint(lambda row_block: feed(row_block, s_up, s_down)), moe_in.reshape(total_rows // share_block, share_block, D)).reshape(total_rows, D)
    blocks = total_rows // TOK_DEV
    slot_index = jnp.where(places < CAP, routes * CAP + places, EXPERTS * CAP).reshape(blocks, TOK_DEV * TOPK)
    owner_token = jnp.repeat(jnp.arange(TOK_DEV, dtype=jnp.int32), TOPK)

    def tables(slot_row):
        token_table = jnp.zeros((EXPERTS * CAP + 1,), jnp.int32).at[slot_row].set(owner_token)
        used_table = jnp.zeros((EXPERTS * CAP + 1,), jnp.float32).at[slot_row].set(1.0)
        return (token_table[:EXPERTS * CAP], used_table[:EXPERTS * CAP])
    slot_token, slot_used = jax.vmap(tables)(slot_index)
    buffers = jax.vmap(pick_rows)(moe_in.reshape(blocks, TOK_DEV, D), slot_token) * slot_used[:, :, None]
    buffers = buffers.reshape(blocks, EXPERTS, CAP, D).transpose(1, 0, 2, 3).reshape(EXPERTS, blocks * CAP, D)
    results = lax.map(jax.checkpoint(lambda member: feed(member[0], member[1], member[2])), (buffers, e_up, e_down))
    results = results.reshape(EXPERTS, blocks, CAP, D).transpose(1, 0, 2, 3).reshape(blocks, EXPERTS * CAP, D)
    safe_index = jnp.minimum(slot_index, EXPERTS * CAP - 1)
    pair_out = jax.vmap(pick_rows)(results, safe_index).reshape(total_rows, TOPK, D)
    moe_out = shared_out + lax.optimization_barrier(jnp.sum((kept_pair * pair_gates)[:, :, None] * pair_out, axis=1))
    return (residual + gate_two * moe_out.reshape(images, PATCHES, D)).reshape(total_rows, D)

def reference(tokens, cotangent, timesteps, ada_weight, ada_bias, qkv_weight, out_weight, router_weight, shared_up, shared_down, expert_up, expert_down, routes, places):
    floats = tuple((array.astype(jnp.float32) for array in (tokens, ada_weight, ada_bias, qkv_weight, out_weight, router_weight, shared_up, shared_down, expert_up, expert_down)))

    def run(*params):
        return forward(*params, timesteps, routes, places)
    output, pullback = jax.vjp(run, *floats)
    grads = pullback(cotangent.astype(jnp.float32))
    counts = lax.optimization_barrier(jnp.sum((routes[:, :, None] == jnp.arange(EXPERTS, dtype=jnp.int32)[None, None, :]).astype(jnp.int32), axis=(0, 1)))
    return (output.astype(jnp.bfloat16), grads[0], grads[1], grads[2], grads[3], grads[4], grads[5], grads[6], grads[7], grads[8], grads[9], counts)
```

```python
import functools
import math

import jax
import jax.numpy as jnp
from jax import lax
from jax.experimental import pallas as pl
from jax.experimental.pallas import tpu as pltpu
from jax.sharding import PartitionSpec as P

HD = 64
EXPERTS = 8
TOPK = 2
PATCHES = 256
CAP = 80
EXTRA = 16
EPSILON = 1e-06
GROUP = 8
FULL_LIMIT = 32 * 1024 * 1024

f32 = jnp.float32
bf16 = jnp.bfloat16
NN = (((1,), (0,)), ((), ()))
NT = (((1,), (1,)), ((), ()))
TN = (((0,), (0,)), ((), ()))
VMEM_LIMIT = 58 * 1024 * 1024


def mm(left, right, dims):
    return lax.dot_general(left, right, dims, preferred_element_type=f32)


def normalize(values):
    center = jnp.mean(values, axis=-1, keepdims=True)
    shifted = values - center
    inverse = lax.rsqrt(jnp.mean(shifted * shifted, axis=-1, keepdims=True) + EPSILON)
    return (shifted * inverse, inverse)


def normalize_back(normed, inverse, upstream):
    return inverse * (
        upstream
        - jnp.mean(upstream, axis=-1, keepdims=True)
        - normed * jnp.mean(upstream * normed, axis=-1, keepdims=True)
    )


def embedding(steps, model_width):
    half_width = model_width // 2
    freqs_all = jnp.exp(-math.log(10000.0) * jnp.arange(half_width, dtype=f32) / half_width)
    angles = steps.astype(f32)[:, None] * freqs_all[None, :]
    return jnp.concatenate([jnp.cos(angles), jnp.sin(angles)], axis=1)


def gelu_both(pre):
    const = math.sqrt(2.0 / math.pi)
    square = pre * pre
    tanh = jnp.tanh(const * pre * (1.0 + 0.044715 * square))
    half = 0.5 + 0.5 * tanh
    slope = half + 0.5 * pre * (1.0 - tanh * tanh) * (const * (1.0 + 3.0 * 0.044715 * square))
    return pre * half, slope


def whole(shape):
    return pl.BlockSpec(shape, lambda *_: (0,) * len(shape))


def pair_masks(rows):
    lane = lax.broadcasted_iota(jnp.int32, (rows, 2 * HD), 1)
    return (lane < HD, lane >= HD)


def head_probs(query, key):
    scores = mm(query, key, NT) * (1.0 / math.sqrt(HD))
    weights = jnp.exp(scores - jnp.max(scores, axis=-1, keepdims=True))
    return weights / jnp.sum(weights, axis=-1, keepdims=True)


def shard_rows(shards, part, local_width):
    return jnp.concatenate(
        [shard[part * local_width : (part + 1) * local_width, :] for shard in shards], axis=0
    )


def attention_kernel(
    local_width, tok_ref, mod_ref, cond_ref, router_ref, pairs_ref, w0, w1, w2, w3,
    attn_in_ref, qkv_ref, context_ref, attn_out_ref, ext_ref,
):
    shards = (w0, w1, w2, w3)
    rows, width = tok_ref.shape
    mod = mod_ref[...]
    stream = tok_ref[...].astype(f32)
    attn_in = (normalize(stream)[0] * (1.0 + mod[1:2]) + mod[0:1]).astype(bf16)
    attn_in_ref[...] = attn_in
    for part in range(3):
        qkv_ref[part] = mm(attn_in, shard_rows(shards, part, local_width), NT).astype(bf16)
    masks = pair_masks(rows)
    zero = jnp.zeros((rows, 2 * HD), bf16)
    for pair in range(width // (2 * HD)):
        cols = slice(pair * 2 * HD, (pair + 1) * 2 * HD)
        query, key, value = qkv_ref[0, :, cols], qkv_ref[1, :, cols], qkv_ref[2, :, cols]
        parts = []
        for mask in masks:
            probs = head_probs(jnp.where(mask, query, zero), key)
            parts.append(mm(probs.astype(bf16), value, NN))
        context_ref[:, cols] = jnp.where(masks[0], parts[0], parts[1]).astype(bf16)
    attn_out = mm(context_ref[...], shard_rows(shards, 3, local_width), NN)
    attn_out_ref[...] = attn_out
    residual = stream + mod[2:3] * attn_out
    moe_in = (normalize(residual)[0] * (1.0 + mod[4:5]) + mod[3:4]).astype(bf16)
    ext_ref[0:rows, :] = moe_in
    logits = mm(router_ref[...], moe_in, NT)
    pairs = pairs_ref[...]
    expert_id = lax.broadcasted_iota(jnp.int32, (EXPERTS, rows), 0)
    chosen = [
        jnp.sum(jnp.where(expert_id == pairs[k : k + 1], logits, 0.0), axis=0, keepdims=True)
        for k in range(TOPK)
    ]
    top = jnp.maximum(chosen[0], chosen[1])
    powers = [jnp.exp(value - top) for value in chosen]
    gates = [power / (powers[0] + powers[1]) for power in powers]
    high = [gate.astype(bf16).astype(f32) for gate in gates]
    rest = [gate - upper for gate, upper in zip(gates, high)]
    values = pairs.astype(f32)
    packed = (
        jnp.concatenate([values[0:1], values[1:2], values[2:3]], axis=1),
        jnp.concatenate([values[3:4], high[0], high[1]], axis=1),
        jnp.concatenate([rest[0], rest[1], jnp.zeros_like(rest[0])], axis=1),
        cond_ref[...],
    )
    row_id = lax.broadcasted_iota(jnp.int32, (EXTRA, width), 0)
    extra = jnp.zeros((EXTRA, width), f32)
    for index, line in enumerate(packed):
        extra = jnp.where(row_id == index, line, extra)
    ext_ref[rows : rows + EXTRA, :] = extra.astype(bf16)


def attention_forward(tokens, mod, cond, router_t, pairs, shards, local_width):
    rows, width = tokens.shape
    return pl.pallas_call(
        functools.partial(attention_kernel, local_width),
        out_shape=(
            jax.ShapeDtypeStruct((rows, width), bf16),
            jax.ShapeDtypeStruct((3, rows, width), bf16),
            jax.ShapeDtypeStruct((rows, width), bf16),
            jax.ShapeDtypeStruct((rows, width), f32),
            jax.ShapeDtypeStruct((rows + EXTRA, width), bf16),
        ),
        compiler_params=pltpu.CompilerParams(vmem_limit_bytes=VMEM_LIMIT),
        cost_estimate=pl.CostEstimate(flops=3 * 10**9, bytes_accessed=8 * 10**6, transcendentals=0),
        name="attention_forward",
    )(tokens, mod, cond, router_t, pairs, *shards)


def read_pairs(extra):
    info = extra.astype(f32)
    count = PATCHES
    routes = (info[0:1, 0:count], info[0:1, count : 2 * count])
    places = (info[0:1, 2 * count : 3 * count], info[1:2, 0:count])
    gates = (
        info[1:2, count : 2 * count] + info[2:3, 0:count],
        info[1:2, 2 * count : 3 * count] + info[2:3, count : 2 * count],
    )
    return routes, places, gates


def slot_hits(routes, places, base, slots):
    slot_id = lax.broadcasted_iota(jnp.int32, (slots, PATCHES), 0).astype(f32)
    return [
        slot_id == jnp.where(place < CAP, (route - base) * CAP + place, -1.0)
        for route, place in zip(routes, places)
    ]


def slot_gates(hits, gates):
    return jnp.sum(
        jnp.where(hits[0], gates[0], 0.0) + jnp.where(hits[1], gates[1], 0.0), axis=1, keepdims=True
    )


def dispatch_kernel(base_ref, ext_ref, cot_ref, rows_ref, cots_ref):
    members = rows_ref.shape[0]
    base = base_ref[0].astype(f32)
    for block in range(GROUP):
        routes, places, gates = read_pairs(ext_ref[block, PATCHES:, :])
        hits = slot_hits(routes, places, base, members * CAP)
        hot = (hits[0] | hits[1]).astype(bf16)
        picked = mm(hot, ext_ref[block, 0:PATCHES, :], NN).astype(bf16)
        scaled = (mm(hot, cot_ref[block], NN) * slot_gates(hits, gates)).astype(bf16)
        for member in range(members):
            span = slice(member * CAP, (member + 1) * CAP)
            rows_ref[member, block * CAP : (block + 1) * CAP, :] = picked[span]
            cots_ref[member, block * CAP : (block + 1) * CAP, :] = scaled[span]


def dispatch(base, ext, cot, members):
    blocks, _, width = ext.shape
    steps = blocks // GROUP
    out = jax.ShapeDtypeStruct((members, blocks * CAP, width), bf16)
    out_spec = pl.BlockSpec((members, GROUP * CAP, width), lambda c, b: (0, c, 0))
    return pl.pallas_call(
        dispatch_kernel,
        grid_spec=pltpu.PrefetchScalarGridSpec(
            num_scalar_prefetch=1,
            grid=(steps,),
            in_specs=[
                pl.BlockSpec((GROUP, PATCHES + EXTRA, width), lambda c, b: (c, 0, 0)),
                pl.BlockSpec((GROUP, PATCHES, width), lambda c, b: (c, 0, 0)),
            ],
            out_specs=(out_spec, out_spec),
        ),
        out_shape=(out, out),
        compiler_params=pltpu.CompilerParams(vmem_limit_bytes=VMEM_LIMIT),
        cost_estimate=pl.CostEstimate(
            flops=4 * blocks * members * CAP * PATCHES * width,
            bytes_accessed=blocks * 2 * 10**6,
            transcendentals=0,
        ),
        name="dispatch",
    )(base, ext, cot)


def expert_kernel(
    shared_ids, base_ref, ext_ref, cot_ref, sup_ref, sdown_ref, eup_ref, edown_ref,
    first_ref, second_ref, rows_s, cots_s, gate_s, dot_s, shared_s,
):
    chunk, step = pl.program_id(0), pl.program_id(1)
    members = rows_s.shape[0]
    width = cot_ref.shape[2]
    base = base_ref[0].astype(f32)

    def block_hits(block):
        routes, places, gates = read_pairs(ext_ref[block, PATCHES:, :])
        return slot_hits(routes, places, base, members * CAP), gates

    @pl.when(step == 0)
    def _():
        for block in range(GROUP):
            hits, gates = block_hits(block)
            hot = (hits[0] | hits[1]).astype(bf16)
            picked = mm(hot, ext_ref[block, 0:PATCHES, :], NN).astype(bf16)
            cots = mm(hot, cot_ref[block], NN).astype(bf16)
            gate = slot_gates(hits, gates)
            for member in range(members):
                span = slice(member * CAP, (member + 1) * CAP)
                rows_s[member, block * CAP : (block + 1) * CAP, :] = picked[span]
                cots_s[member, block * CAP : (block + 1) * CAP, :] = cots[span]
                gate_s[member, block * CAP : (block + 1) * CAP, :] = gate[span]

    @pl.when((step == 0) & (chunk == 0))
    def _():
        for place, block in enumerate(shared_ids):
            inputs, cots = ext_ref[block, 0:PATCHES, :], cot_ref[block]
            value, slope = gelu_both(mm(inputs, sup_ref[...], NN))
            pre_grad = (mm(cots, sdown_ref[...], NT) * slope).astype(bf16)
            shared_s[place, :, 0:width] = mm(value.astype(bf16), sdown_ref[...], NN)
            shared_s[place, :, width:] = mm(pre_grad, sup_ref[...], NT)

    @pl.when(step > 0)
    def _():
        member = step - 1
        total = GROUP * CAP
        tile = total // 2
        for part in range(2):
            span = slice(part * tile, (part + 1) * tile)
            inputs, cots, gate = rows_s[member, span, :], cots_s[member, span, :], gate_s[member, span, :]
            value, slope = gelu_both(mm(inputs, eup_ref[0], NN))
            act_grad = mm(cots, edown_ref[0], NT)
            dot_s[member, span, :] = jnp.sum(value * act_grad, axis=1, keepdims=True)
            active = (gate * value).astype(bf16)
            pre_grad = (gate * act_grad * slope).astype(bf16)
            rows_s[member, span, :] = mm(active, edown_ref[0], NN).astype(bf16)
            cots_s[member, span, :] = mm(pre_grad, eup_ref[0], NT).astype(bf16)

    @pl.when(step == members)
    def _():
        half = GROUP // 2
        for block in range(GROUP):
            out_ref, place = (first_ref, block) if block < half else (second_ref, block - half)
            hits, _ = block_hits(block)
            hot = (hits[0] | hits[1]).astype(bf16)
            span = slice(block * CAP, (block + 1) * CAP)
            dots = jnp.concatenate([dot_s[m, span, :] for m in range(members)], axis=0)
            sums = [jnp.sum(jnp.where(hit, dots, 0.0), axis=0, keepdims=True) for hit in hits]
            line = jnp.concatenate(sums + [jnp.zeros_like(sums[0])], axis=1)
            row_id = lax.broadcasted_iota(jnp.int32, (EXTRA, width), 0)
            out_ref[place, 2 * PATCHES :, :] = jnp.where(row_id == 0, line, 0.0).astype(bf16)
            for index, source in enumerate((rows_s, cots_s)):
                slots = jnp.concatenate([source[m, span, :] for m in range(members)], axis=0)
                total = mm(hot, slots, TN)
                if block in shared_ids:
                    where = shared_ids.index(block)
                    own = shared_s[where, :, index * width : (index + 1) * width]
                    total = total + jnp.where(chunk == 0, own, 0.0)
                out_ref[place, index * PATCHES : (index + 1) * PATCHES, :] = total.astype(bf16)


def experts_both(base, ext, cot, shared_up, shared_down, expert_up, expert_down, shared_ids):
    blocks, _, width = ext.shape
    members, _, hidden = expert_up.shape
    steps = blocks // GROUP
    half = GROUP // 2
    out = jax.ShapeDtypeStruct((steps * half, 2 * PATCHES + EXTRA, width), bf16)
    one = pl.Buffered(1)
    out_spec = pl.BlockSpec((half, 2 * PATCHES + EXTRA, width), lambda c, e, b: (c, 0, 0), pipeline_mode=one)
    return pl.pallas_call(
        functools.partial(expert_kernel, shared_ids),
        grid_spec=pltpu.PrefetchScalarGridSpec(
            num_scalar_prefetch=1,
            grid=(steps, members + 1),
            in_specs=[
                pl.BlockSpec((GROUP, PATCHES + EXTRA, width), lambda c, e, b: (c, 0, 0), pipeline_mode=one),
                pl.BlockSpec((GROUP, PATCHES, width), lambda c, e, b: (c, 0, 0), pipeline_mode=one),
                pl.BlockSpec((width, hidden), lambda c, e, b: (0, 0), pipeline_mode=one),
                pl.BlockSpec((hidden, width), lambda c, e, b: (0, 0), pipeline_mode=one),
                pl.BlockSpec((1, width, hidden), lambda c, e, b: (jnp.maximum(e - 1, 0), 0, 0)),
                pl.BlockSpec((1, hidden, width), lambda c, e, b: (jnp.maximum(e - 1, 0), 0, 0)),
            ],
            out_specs=(out_spec, out_spec),
            scratch_shapes=[
                pltpu.VMEM((members, GROUP * CAP, width), bf16),
                pltpu.VMEM((members, GROUP * CAP, width), bf16),
                pltpu.VMEM((members, GROUP * CAP, 1), f32),
                pltpu.VMEM((members, GROUP * CAP, 1), f32),
                pltpu.VMEM((len(shared_ids), PATCHES, 2 * width), f32),
            ],
        ),
        out_shape=(out, out),
        compiler_params=pltpu.CompilerParams(vmem_limit_bytes=VMEM_LIMIT),
        cost_estimate=pl.CostEstimate(flops=25 * 10**9, bytes_accessed=30 * 10**6, transcendentals=0),
        name="experts_both",
    )(base, ext, cot, shared_up, shared_down, expert_up, expert_down)


def grads_kernel(started, rows_ref, cots_ref, up_ref, down_ref, *refs):
    up_grad_ref, down_grad_ref = refs[-2:]
    width = up_ref.shape[1]
    inputs = rows_ref[...].reshape(-1, width)
    cots = cots_ref[...].reshape(-1, width)
    value, slope = gelu_both(mm(inputs, up_ref[0], NN))
    pre_grad = (mm(cots, down_ref[0], NT) * slope).astype(bf16)
    up_grad = mm(inputs, pre_grad, TN)
    down_grad = mm(value.astype(bf16), cots, TN)

    @pl.when(pl.program_id(1) == 0)
    def _():
        if started:
            up_grad_ref[0] = refs[0][0] + up_grad
            down_grad_ref[0] = refs[1][0] + down_grad
        else:
            up_grad_ref[0] = up_grad
            down_grad_ref[0] = down_grad

    @pl.when(pl.program_id(1) > 0)
    def _():
        up_grad_ref[0] += up_grad
        down_grad_ref[0] += down_grad


def weight_grads(rows, cots, up, down, before, row_spec, cot_spec, steps, count):
    members, width, hidden = up.shape
    up_spec = pl.BlockSpec((1, width, hidden), lambda e, t: (e, 0, 0))
    down_spec = pl.BlockSpec((1, hidden, width), lambda e, t: (e, 0, 0))
    started = before is not None
    return pl.pallas_call(
        functools.partial(grads_kernel, started),
        grid=(members, steps),
        in_specs=[row_spec, cot_spec, up_spec, down_spec] + ([up_spec, down_spec] if started else []),
        out_specs=(up_spec, down_spec),
        out_shape=(
            jax.ShapeDtypeStruct(up.shape, f32),
            jax.ShapeDtypeStruct(down.shape, f32),
        ),
        input_output_aliases={4: 0, 5: 1} if started else {},
        compiler_params=pltpu.CompilerParams(vmem_limit_bytes=VMEM_LIMIT),
        cost_estimate=pl.CostEstimate(
            flops=8 * count * width * hidden, bytes_accessed=count * width * 4, transcendentals=0
        ),
        name="weight_grads",
    )(rows, cots, up, down, *(before or ()))


def routed_grads(rows, cots, up, down, before):
    members, count, width = rows.shape
    tile = GROUP * CAP
    spec = pl.BlockSpec((1, tile, width), lambda e, t: (e, t, 0))
    return weight_grads(rows, cots, up, down, before, spec, spec, count // tile, members * count)


def shared_grads(ext, cot, up, down, before):
    blocks, _, width = ext.shape
    spec = pl.BlockSpec((4, PATCHES, width), lambda e, t: (t, 0, 0))
    return weight_grads(
        ext, cot, up[None], down[None], before, spec, spec, blocks // 4, blocks * PATCHES
    )


def backward_kernel(
    local_width, moe_ref, back_ref, dots_ref, tok_ref, cot_ref, mod_ref, router_ref, pairs_ref, attn_in_ref,
    qkv_ref, context_ref, attn_out_ref, ext_ref, w0, w1, w2, w3,
    output_ref, tok_grad_ref, small_ref, weights_ref, grad_s,
):
    shards = (w0, w1, w2, w3)
    rows, width = tok_ref.shape
    mod = mod_ref[...]
    stream = tok_ref[...].astype(f32)
    attn_out = attn_out_ref[...]
    residual = stream + mod[2:3] * attn_out
    second_norm, second_inv = normalize(residual)
    moe_out = moe_ref[...].astype(f32)
    upstream = cot_ref[...].astype(f32)
    output_ref[...] = (residual + mod[5:6] * moe_out).astype(bf16)
    gate_two_grad = jnp.sum(upstream * moe_out, axis=0, keepdims=True)
    routes, places, gates = read_pairs(ext_ref[rows:, :])
    dots = dots_ref[...].astype(f32)
    dots = (dots[0:1, 0:PATCHES], dots[0:1, PATCHES : 2 * PATCHES])
    mean_dot = gates[0] * dots[0] + gates[1] * dots[1]
    pairs = pairs_ref[...]
    expert_id = lax.broadcasted_iota(jnp.int32, (EXPERTS, rows), 0)
    logits_grad = jnp.zeros((EXPERTS, rows), f32)
    for k in range(TOPK):
        logits_grad += jnp.where(expert_id == pairs[k : k + 1], gates[k] * (dots[k] - mean_dot), 0.0)
    logits_grad = logits_grad.astype(bf16)
    moe_in_grad = back_ref[...].astype(f32) + mm(logits_grad, router_ref[...], TN)
    shift_two_grad = jnp.sum(moe_in_grad, axis=0, keepdims=True)
    scale_two_grad = jnp.sum(moe_in_grad * second_norm, axis=0, keepdims=True)
    residual_grad = upstream + normalize_back(
        second_norm, second_inv, moe_in_grad * (1.0 + mod[4:5])
    )
    gate_one_grad = jnp.sum(residual_grad * attn_out, axis=0, keepdims=True)
    attn_grad = (mod[2:3] * residual_grad).astype(bf16)
    out_grad = mm(context_ref[...], attn_grad, TN).astype(bf16)
    for index in range(len(shards)):
        weights_ref[index, 3 * local_width :, :] = out_grad[index * local_width : (index + 1) * local_width]
    context_grad = mm(attn_grad, shard_rows(shards, 3, local_width), NT).astype(bf16)
    masks = pair_masks(rows)
    zero = jnp.zeros((rows, 2 * HD), bf16)
    scale = 1.0 / math.sqrt(HD)
    for pair in range(width // (2 * HD)):
        cols = slice(pair * 2 * HD, (pair + 1) * 2 * HD)
        query, key, value = qkv_ref[0, :, cols], qkv_ref[1, :, cols], qkv_ref[2, :, cols]
        upper = context_grad[:, cols]
        sums = []
        for mask in masks:
            probs = head_probs(jnp.where(mask, query, zero), key)
            probs_grad = mm(jnp.where(mask, upper, zero), value, NT)
            value_grad = mm(probs.astype(bf16), upper, TN)
            score_grad = (
                probs * (probs_grad - jnp.sum(probs_grad * probs, axis=-1, keepdims=True))
            ).astype(bf16)
            sums.append((mm(score_grad, key, NN) * scale, mm(score_grad, query, TN) * scale, value_grad))
        for part in range(3):
            grad_s[part, :, cols] = jnp.where(masks[0], sums[0][part], sums[1][part]).astype(bf16)
    attn_in = attn_in_ref[...]
    attn_in_grad = jnp.zeros((rows, width), f32)
    for part in range(3):
        grad = grad_s[part]
        attn_in_grad += mm(grad, shard_rows(shards, part, local_width), NN)
        weight_grad = mm(grad, attn_in, TN).astype(bf16)
        for index in range(len(shards)):
            weights_ref[index, part * local_width : (part + 1) * local_width, :] = weight_grad[
                index * local_width : (index + 1) * local_width
            ]
    first_norm, first_inv = normalize(stream)
    shift_one_grad = jnp.sum(attn_in_grad, axis=0, keepdims=True)
    scale_one_grad = jnp.sum(attn_in_grad * first_norm, axis=0, keepdims=True)
    tok_grad_ref[...] = residual_grad + normalize_back(
        first_norm, first_inv, attn_in_grad * (1.0 + mod[1:2])
    )
    lines = (
        shift_one_grad, scale_one_grad, gate_one_grad, shift_two_grad, scale_two_grad, gate_two_grad,
    )
    row_id = lax.broadcasted_iota(jnp.int32, (8, width), 0)
    stacked = jnp.zeros((8, width), f32)
    for index, line in enumerate(lines):
        stacked = jnp.where(row_id == index, line, stacked)
    small_ref[0:8, :] = stacked
    small_ref[8:16, :] = mm(logits_grad, ext_ref[0:rows, :], NN)


def attention_backward(
    moe_out, moe_back, dots, tokens, cotangent, mod, router_t, pairs, attn_in, qkv, context, attn_out, ext,
    shards, local_width,
):
    rows, width = tokens.shape
    return pl.pallas_call(
        functools.partial(backward_kernel, local_width),
        out_shape=(
            jax.ShapeDtypeStruct((rows, width), bf16),
            jax.ShapeDtypeStruct((rows, width), f32),
            jax.ShapeDtypeStruct((16, width), f32),
            jax.ShapeDtypeStruct((len(shards), 4 * local_width, width), bf16),
        ),
        scratch_shapes=[pltpu.VMEM((3, rows, width), bf16)],
        compiler_params=pltpu.CompilerParams(vmem_limit_bytes=VMEM_LIMIT),
        cost_estimate=pl.CostEstimate(flops=6 * 10**9, bytes_accessed=16 * 10**6, transcendentals=0),
        name="attention_backward",
    )(
        moe_out, moe_back, dots, tokens, cotangent, mod, router_t, pairs, attn_in, qkv, context, attn_out,
        ext, *shards,
    )


class Links:
    def __init__(self, mesh):
        self.dp, self.expert, self.tensor = (mesh.shape[name] for name in ("dp", "expert", "tensor"))
        self.paired = self.expert == 2 and self.tensor == 4
        self.core = [(i, i ^ 1) for i in range(self.tensor)]
        self.side = [(i, i ^ 2) for i in range(self.tensor)]
        self.cross = [(i, i ^ 3) for i in range(self.tensor)]
        self.other = [(0, 1), (1, 0)]

    def to_core(self, value):
        return lax.ppermute(value, "tensor", self.core)

    def to_side(self, value):
        return lax.ppermute(value, "tensor", self.side)

    def to_other(self, value):
        return lax.ppermute(value, "expert", self.other)

    def tensor_blocks(self, block):
        if self.tensor != 4:
            raise NotImplementedError
        across = self.to_side(block)
        near = self.to_core(block)
        return (block, near, across, self.to_core(across))

    def plane(self, blocks):
        if self.paired:
            rows = blocks.shape[1]
            cut = (rows // 2 + 15) // 16 * 16
            side, other = self.to_side(blocks), self.to_other(blocks)
            upper = self.to_side(other[:, :cut])
            lower = self.to_other(side[:, cut:])
            corner = jnp.concatenate([upper, lower], axis=1)
            mine = jnp.concatenate([blocks, side, other, corner], axis=0)
            return jnp.concatenate([mine, self.to_core(mine)], axis=0)
        everything = lax.all_gather(blocks, ("expert", "tensor"), axis=0, tiled=True)
        return jnp.roll(everything, -lax.axis_index("expert") * self.tensor * blocks.shape[0], axis=0)

    def column(self, block):
        return jnp.stack(
            [
                lax.ppermute(block, "dp", [(i, (i + hop) % self.dp) for i in range(self.dp)])
                for hop in range(1, self.dp)
            ]
        )

    def plane_sum(self, first, second):
        if self.paired:
            here = first + self.to_core(second)
            rows = here.shape[1]
            cut = PATCHES
            from_side = self.to_side(here[1::2, :cut])
            from_other = self.to_other(here[2:, cut:])
            upper = here[0, :cut] + from_side[0]
            lower = here[0, cut:] + from_other[0]
            upper_next = here[2, :cut] + from_side[1]
            lower_next = here[1, cut:] + from_other[1]
            return upper + self.to_other(upper_next), lower + self.to_side(lower_next)
        half = GROUP // 2
        blocks = jnp.concatenate(
            [part.reshape((-1, half) + part.shape[1:]) for part in (first, second)], axis=1
        ).reshape((-1,) + first.shape[1:])
        blocks = jnp.roll(blocks, lax.axis_index("expert") * self.tensor, axis=0)
        total = lax.psum_scatter(blocks, ("expert", "tensor"), scatter_dimension=0, tiled=True)[0]
        return total[:PATCHES], total[PATCHES:]

    def sum_along(self, value, axis, size):
        rows = value.shape[0]
        share = rows // size
        if rows % (size * 16):
            return lax.psum(value, axis)
        me = lax.axis_index(axis)
        piece = lambda index: lax.dynamic_slice_in_dim(value, index * share, share, axis=0)
        total = piece(me).astype(f32)
        for hop in range(1, size):
            pairs = [(i, (i + hop) % size) for i in range(size)]
            total = total + lax.ppermute(piece((me + hop) % size), axis, pairs).astype(f32)
        total = total.astype(value.dtype)
        result = jnp.zeros_like(value)
        result = lax.dynamic_update_slice_in_dim(result, total, me * share, axis=0)
        for hop in range(1, size):
            pairs = [(i, (i + hop) % size) for i in range(size)]
            result = lax.dynamic_update_slice_in_dim(
                result, lax.ppermute(total, axis, pairs), (me - hop) % size * share, axis=0
            )
        return result


def local(
    links,
    tokens,
    cotangent,
    timesteps,
    ada_weight,
    ada_bias,
    qkv_weight,
    out_weight,
    router_weight,
    shared_up,
    shared_down,
    expert_up,
    expert_down,
    routes,
    places,
):
    rows, width = tokens.shape
    local_width = qkv_weight.shape[2]
    members = expert_up.shape[0]
    me = lax.axis_index("tensor")
    base = (lax.axis_index("expert") * members).astype(jnp.int32).reshape(1)

    weight = jnp.concatenate(
        [qkv_weight.transpose(1, 2, 0).reshape(3 * local_width, width), out_weight], axis=0
    )
    shards = links.tensor_blocks(weight)

    condition = jax.nn.silu(embedding(timesteps, width)).astype(bf16)
    mod_cols = jnp.einsum("id,dcf->icf", condition, ada_weight, preferred_element_type=f32) + ada_bias[None]
    mod = lax.all_to_all(mod_cols, "tensor", split_axis=0, concat_axis=2, tiled=True)[0]
    own_condition = lax.dynamic_slice_in_dim(condition.astype(f32), me, 1, axis=0)
    shared_cot = (mod[5][None] * cotangent.astype(f32)).astype(bf16)
    router_t = router_weight.T
    pairs = jnp.concatenate([routes.T, places.T], axis=0)

    attn_in, qkv, context, attn_out, ext = attention_forward(
        tokens, mod, own_condition, router_t, pairs, shards, local_width
    )
    cot_plane = links.plane(shared_cot[None])
    ext_plane = links.plane(ext[None])
    shared_ids = (0, 1, 4, 5) if links.paired else tuple(range(links.tensor))
    first, second = experts_both(
        base, ext_plane, cot_plane, shared_up, shared_down, expert_up, expert_down, shared_ids
    )
    upper, lower = links.plane_sum(first, second)
    slot_rows, slot_cots = dispatch(base, ext_plane, cot_plane, members)
    routed = routed_grads(slot_rows, slot_cots, expert_up, expert_down, None)
    shared = shared_grads(ext_plane, cot_plane, shared_up, shared_down, None)

    output, tokens_grad, small, weights_grad = attention_backward(
        upper, lower[:PATCHES], lower[PATCHES:], tokens, cotangent, mod, router_t, pairs,
        attn_in, qkv, context, attn_out, ext, shards, local_width,
    )

    total_blocks = links.dp * links.expert * links.tensor
    full = links.paired and total_blocks * rows * width * 2 <= FULL_LIMIT
    if full:
        cot_rest = links.plane(links.column(shared_cot))
        ext_rest = links.plane(links.column(ext))
        rest_rows, rest_cots = dispatch(base, ext_rest, cot_rest, members)
        routed = routed_grads(rest_rows, rest_cots, expert_up, expert_down, routed)
        shared = shared_grads(ext_rest, cot_rest, shared_up, shared_down, shared)
        small_all = jnp.concatenate([links.plane(small[None]), links.plane(links.column(small))], axis=0)
        extra_all = jnp.concatenate([ext_plane[:, PATCHES:], ext_rest[:, PATCHES:]], axis=0)
        condition_all = extra_all[:, 3]
        routes_all = extra_all[:, 0, : TOPK * PATCHES]
        near = weights_grad[0] + links.to_core(weights_grad[1])
        far = weights_grad[2] + links.to_core(weights_grad[3])
        dense = near + links.to_side(far)
        dense = links.sum_along(links.sum_along(dense, "expert", links.expert), "dp", links.dp)
    else:
        routed = lax.psum(routed, "dp")
        shared = lax.psum(shared, "dp")
        small_all = lax.all_gather(small, ("dp", "expert", "tensor"), axis=0)
        condition_all = lax.all_gather(own_condition[0], ("dp", "expert", "tensor"), axis=0).astype(bf16)
        routes_all = lax.all_gather(routes.reshape(-1), ("dp", "expert", "tensor"), axis=0)
        order = jnp.arange(links.tensor) ^ me
        dense = lax.psum_scatter(
            weights_grad[order], "tensor", scatter_dimension=0, tiled=True
        )[0]
        dense = lax.psum(dense, ("dp", "expert"))

    mod_grad = lax.dynamic_slice_in_dim(small_all[:, 0:6], me * local_width, local_width, axis=2)
    ada_grad = jnp.einsum(
        "id,icf->dcf", condition_all.astype(f32), mod_grad, precision=lax.Precision.HIGHEST
    )
    ada_bias_grad = jnp.sum(mod_grad, axis=0)
    router_grad = jnp.sum(small_all[:, 8:16], axis=0).T
    counts = jnp.sum(
        (routes_all[:, :, None] == jnp.arange(EXPERTS).astype(routes_all.dtype)).astype(jnp.int32),
        axis=(0, 1),
    )
    dense = dense.astype(f32)
    qkv_grad = dense[: 3 * local_width].reshape(3, local_width, width).transpose(2, 0, 1)
    return (
        output,
        tokens_grad,
        ada_grad,
        ada_bias_grad,
        qkv_grad,
        dense[3 * local_width :],
        router_grad,
        shared[0][0],
        shared[1][0],
        routed[0],
        routed[1],
        counts,
    )


def solution(mesh):
    rows = P(("dp", "expert", "tensor"), None)
    placed = (
        rows,
        rows,
        P(("dp", "expert")),
        P(None, None, "tensor"),
        P(None, "tensor"),
        P(None, None, "tensor"),
        P("tensor", None),
        P(),
        P(None, "tensor"),
        P("tensor", None),
        P("expert", None, "tensor"),
        P("expert", "tensor", None),
        rows,
        rows,
    )
    return jax.shard_map(
        functools.partial(local, Links(mesh)),
        mesh=mesh,
        in_specs=placed,
        out_specs=(
            rows,
            rows,
            P(None, None, "tensor"),
            P(None, "tensor"),
            P(None, None, "tensor"),
            P("tensor", None),
            P(),
            P(None, "tensor"),
            P("tensor", None),
            P("expert", None, "tensor"),
            P("expert", "tensor", None),
            P(),
        ),
        check_vma=False,
    )
```

```python
import functools
import math

import jax
import jax.numpy as jnp
from jax import lax
from jax.experimental import pallas as pl
from jax.experimental.pallas import tpu as pltpu
from jax.sharding import PartitionSpec as P

HD = 64
EXPERTS = 8
TOPK = 2
PATCHES = 256
CAP = 80
EXTRA = 16
EPSILON = 1e-06
HALF = 4
FULL_LIMIT = 32 * 1024 * 1024

f32 = jnp.float32
bf16 = jnp.bfloat16
NN = (((1,), (0,)), ((), ()))
NT = (((1,), (1,)), ((), ()))
TN = (((0,), (0,)), ((), ()))
TT = (((0,), (1,)), ((), ()))
VMEM_LIMIT = 58 * 1024 * 1024


def mm(left, right, dims):
    return lax.dot_general(left, right, dims, preferred_element_type=f32)


def normalize(values):
    center = jnp.mean(values, axis=-1, keepdims=True)
    shifted = values - center
    inverse = lax.rsqrt(jnp.mean(shifted * shifted, axis=-1, keepdims=True) + EPSILON)
    return (shifted * inverse, inverse)


def normalize_back(normed, inverse, upstream):
    return inverse * (
        upstream
        - jnp.mean(upstream, axis=-1, keepdims=True)
        - normed * jnp.mean(upstream * normed, axis=-1, keepdims=True)
    )


def embedding(steps, model_width):
    half_width = model_width // 2
    freqs_all = jnp.exp(-math.log(10000.0) * jnp.arange(half_width, dtype=f32) / half_width)
    angles = steps.astype(f32)[:, None] * freqs_all[None, :]
    return jnp.concatenate([jnp.cos(angles), jnp.sin(angles)], axis=1)


def gelu_both(pre):
    const = math.sqrt(2.0 / math.pi)
    square = pre * pre
    tanh = jnp.tanh(const * pre * (1.0 + 0.044715 * square))
    half = 0.5 + 0.5 * tanh
    value = pre * half
    return value, half + value * (1.0 - tanh) * (const + 3.0 * 0.044715 * const * square)


def params():
    return pltpu.CompilerParams(vmem_limit_bytes=VMEM_LIMIT)


def cost(flops, moved):
    return pl.CostEstimate(flops=int(flops), bytes_accessed=int(moved), transcendentals=0)


def copy_kernel(plan, count, *refs):
    sources, out, sems = refs[:count], refs[-2], refs[-1]
    copies = [
        pltpu.make_async_copy(sources[index].at[take], out.at[put], sems.at[order])
        for order, (index, take, put) in enumerate(plan)
    ]
    for copy in copies:
        copy.start()
    for copy in copies:
        copy.wait()


def assemble(shape, dtype, sources, plan, after=()):
    anywhere = pl.BlockSpec(memory_space=pl.ANY)
    operands = (*sources, *after)
    return pl.pallas_call(
        functools.partial(copy_kernel, plan, len(sources)),
        in_specs=[anywhere] * len(operands),
        out_specs=anywhere,
        out_shape=jax.ShapeDtypeStruct(shape, dtype),
        scratch_shapes=[pltpu.SemaphoreType.DMA((len(plan),))],
        compiler_params=params(),
        cost_estimate=cost(0, 2 * math.prod(shape) * jnp.dtype(dtype).itemsize),
        name="assemble",
    )(*operands)


def cotangent_kernel(mod_ref, cot_ref, after_ref, out_ref):
    out_ref[...] = (mod_ref[5:6] * cot_ref[...].astype(f32)).astype(bf16)


def moe_cotangent(mod, cotangent, after):
    vmem = pl.BlockSpec(memory_space=pltpu.VMEM)
    return pl.pallas_call(
        cotangent_kernel,
        in_specs=[vmem, vmem, pl.BlockSpec(memory_space=pl.ANY)],
        out_specs=vmem,
        out_shape=jax.ShapeDtypeStruct(cotangent.shape, bf16),
        compiler_params=params(),
        name="moe_cotangent",
    )(mod, cotangent, after)


def pair_masks(rows):
    lane = lax.broadcasted_iota(jnp.int32, (rows, 2 * HD), 1)
    return (lane < HD, lane >= HD)


def head_probs(query, key):
    scores = mm(query, key, NT) * (1.0 / math.sqrt(HD))
    weights = jnp.exp(scores - jnp.max(scores, axis=-1, keepdims=True))
    return weights / jnp.sum(weights, axis=-1, keepdims=True)


def shard_rows(shards, part, local_width):
    return jnp.concatenate(
        [shard[part * local_width : (part + 1) * local_width, :] for shard in shards], axis=0
    )


def attention_kernel(
    local_width, tok_ref, mod_ref, cond_ref, router_ref, pairs_ref, cot_ref, w0, w1, w2, w3,
    attn_in_ref, qkv_ref, context_ref, attn_out_ref, ext_ref, both_ref,
):
    shards = (w0, w1, w2, w3)
    rows, width = tok_ref.shape
    mod = mod_ref[...]
    stream = tok_ref[...].astype(f32)
    attn_in = (normalize(stream)[0] * (1.0 + mod[1:2]) + mod[0:1]).astype(bf16)
    attn_in_ref[...] = attn_in
    for part in range(3):
        qkv_ref[part] = mm(attn_in, shard_rows(shards, part, local_width), NT).astype(bf16)
    masks = pair_masks(rows)
    zero = jnp.zeros((rows, 2 * HD), bf16)
    for pair in range(width // (2 * HD)):
        cols = slice(pair * 2 * HD, (pair + 1) * 2 * HD)
        query, key, value = qkv_ref[0, :, cols], qkv_ref[1, :, cols], qkv_ref[2, :, cols]
        parts = []
        for mask in masks:
            probs = head_probs(jnp.where(mask, query, zero), key)
            parts.append(mm(probs.astype(bf16), value, NN))
        context_ref[:, cols] = jnp.where(masks[0], parts[0], parts[1]).astype(bf16)
    attn_out = mm(context_ref[...], shard_rows(shards, 3, local_width), NN)
    attn_out_ref[...] = attn_out
    residual = stream + mod[2:3] * attn_out
    moe_in = (normalize(residual)[0] * (1.0 + mod[4:5]) + mod[3:4]).astype(bf16)
    ext_ref[0:rows, :] = moe_in
    logits = mm(router_ref[...], moe_in, NT)
    pairs = pairs_ref[...]
    expert_id = lax.broadcasted_iota(jnp.int32, (EXPERTS, rows), 0)
    chosen = [
        jnp.sum(jnp.where(expert_id == pairs[k : k + 1], logits, 0.0), axis=0, keepdims=True)
        for k in range(TOPK)
    ]
    top = jnp.maximum(chosen[0], chosen[1])
    powers = [jnp.exp(value - top) for value in chosen]
    gates = [power / (powers[0] + powers[1]) for power in powers]
    high = [gate.astype(bf16).astype(f32) for gate in gates]
    rest = [gate - upper for gate, upper in zip(gates, high)]
    values = pairs.astype(f32)
    packed = (
        jnp.concatenate([values[0:1], values[1:2], values[2:3]], axis=1),
        jnp.concatenate([values[3:4], high[0], high[1]], axis=1),
        jnp.concatenate([rest[0], rest[1], jnp.zeros_like(rest[0])], axis=1),
        cond_ref[...],
    )
    row_id = lax.broadcasted_iota(jnp.int32, (EXTRA, width), 0)
    extra = jnp.zeros((EXTRA, width), f32)
    for index, line in enumerate(packed):
        extra = jnp.where(row_id == index, line, extra)
    ext_ref[rows : rows + EXTRA, :] = extra.astype(bf16)
    both_ref[0:rows, :] = cot_ref[...]
    both_ref[rows : 2 * rows, :] = moe_in
    both_ref[2 * rows :, :] = extra.astype(bf16)


def attention_forward(tokens, mod, cond, router_t, pairs, cot, shards, local_width):
    rows, width = tokens.shape
    return pl.pallas_call(
        functools.partial(attention_kernel, local_width),
        out_shape=(
            jax.ShapeDtypeStruct((rows, width), bf16),
            jax.ShapeDtypeStruct((3, rows, width), bf16),
            jax.ShapeDtypeStruct((rows, width), bf16),
            jax.ShapeDtypeStruct((rows, width), f32),
            jax.ShapeDtypeStruct((rows + EXTRA, width), bf16),
            jax.ShapeDtypeStruct((2 * rows + EXTRA, width), bf16),
        ),
        compiler_params=params(),
        cost_estimate=cost(5 * 10**9, 9 * 10**6),
        name="attention_forward",
    )(tokens, mod, cond, router_t, pairs, cot, *shards)


def read_pairs(extra):
    info = extra.astype(f32)
    count = PATCHES
    routes = (info[0:1, 0:count], info[0:1, count : 2 * count])
    places = (info[0:1, 2 * count : 3 * count], info[1:2, 0:count])
    gates = (
        info[1:2, count : 2 * count] + info[2:3, 0:count],
        info[1:2, 2 * count : 3 * count] + info[2:3, count : 2 * count],
    )
    return routes, places, gates


def slot_hits(routes, places, base, slots):
    slot_id = lax.broadcasted_iota(jnp.int32, (slots, PATCHES), 0).astype(f32)
    return [
        slot_id == jnp.where(place < CAP, (route - base) * CAP + place, -1.0)
        for route, place in zip(routes, places)
    ]


def slot_gates(hits, gates):
    return jnp.sum(
        jnp.where(hits[0], gates[0], 0.0) + jnp.where(hits[1], gates[1], 0.0), axis=1, keepdims=True
    )


class Blocks:
    def __init__(self, rows, rows_at, extra_at, cots, cots_at):
        self.rows, self.rows_at, self.extra_at, self.cots, self.cots_at = rows, rows_at, extra_at, cots, cots_at

    @classmethod
    def apart(cls, ext, cots):
        return cls(ext, 0, PATCHES // EXTRA, cots, 0)

    @classmethod
    def joined(cls, both):
        return cls(both, 1, 2 * PATCHES // EXTRA, both, 0)

    def operands(self):
        return [self.rows, self.rows, self.cots]

    def specs(self):
        width = self.rows.shape[2]
        places = ((PATCHES, self.rows_at), (EXTRA, self.extra_at), (PATCHES, self.cots_at))
        return [
            pl.BlockSpec((HALF, count, width), lambda *_, at=at: (0, at, 0)) for count, at in places
        ]

    def extra(self):
        return self.rows[:, self.extra_at * EXTRA : (self.extra_at + 1) * EXTRA]


def dispatch_kernel(base_ref, *refs):
    rows_ref, cots_ref = refs[-2:]
    members = rows_ref.shape[0]
    base = base_ref[0].astype(f32)
    for part in range(2):
        rows_in, extra_in, cots_in = refs[3 * part : 3 * part + 3]

        @pl.when(pl.program_id(0) == part)
        def _():
            for block in range(HALF):
                routes, places, gates = read_pairs(extra_in[block])
                hits = slot_hits(routes, places, base, members * CAP)
                hot = (hits[0] | hits[1]).astype(bf16)
                picked = mm(hot, rows_in[block], NN).astype(bf16)
                scaled = (mm(hot, cots_in[block], NN) * slot_gates(hits, gates)).astype(bf16)
                for member in range(members):
                    span = slice(member * CAP, (member + 1) * CAP)
                    rows_ref[member, block * CAP : (block + 1) * CAP, :] = picked[span]
                    cots_ref[member, block * CAP : (block + 1) * CAP, :] = scaled[span]


def dispatch(base, blocks, members):
    width = blocks[0].rows.shape[2]
    out = jax.ShapeDtypeStruct((members, 2 * HALF * CAP, width), bf16)
    out_spec = pl.BlockSpec((members, HALF * CAP, width), lambda c, b: (0, c, 0))
    return pl.pallas_call(
        dispatch_kernel,
        grid_spec=pltpu.PrefetchScalarGridSpec(
            num_scalar_prefetch=1,
            grid=(2,),
            in_specs=[spec for part in blocks for spec in part.specs()],
            out_specs=(out_spec, out_spec),
        ),
        out_shape=(out, out),
        compiler_params=params(),
        cost_estimate=cost(8 * 10**9, 16 * 10**6),
        name="dispatch",
    )(base, *[operand for part in blocks for operand in part.operands()])


def expert_kernel(
    shared_ids, base_ref, rows0, extra0, cots0, rows1, extra1, cots1, sup_ref, sdown_ref, eup_ref, edown_ref,
    first_ref, second_ref, rows_s, cots_s, gate_s, dot_s, shared_s,
):
    step = pl.program_id(0)
    members = rows_s.shape[0]
    width = sup_ref.shape[0]
    base = base_ref[0].astype(f32)
    halves = ((rows0, extra0, cots0), (rows1, extra1, cots1))
    total_rows = 2 * HALF * CAP

    def block_hits(block):
        routes, places, gates = read_pairs(halves[block // HALF][1][block % HALF])
        return slot_hits(routes, places, base, members * CAP), gates

    @pl.when(step == 0)
    def _():
        for block in range(2 * HALF):
            rows_in, _, cots_in = halves[block // HALF]
            hits, gates = block_hits(block)
            hot = (hits[0] | hits[1]).astype(bf16)
            picked = mm(hot, rows_in[block % HALF], NN).astype(bf16)
            cots = mm(hot, cots_in[block % HALF], NN).astype(bf16)
            gate = slot_gates(hits, gates)
            for member in range(members):
                span = slice(member * CAP, (member + 1) * CAP)
                rows_s[member, block * CAP : (block + 1) * CAP, :] = picked[span]
                cots_s[member, block * CAP : (block + 1) * CAP, :] = cots[span]
                gate_s[member, block * CAP : (block + 1) * CAP, :] = gate[span]
        for start in range(0, len(shared_ids), 2):
            pair = shared_ids[start : start + 2]
            inputs = jnp.concatenate([halves[b // HALF][0][b % HALF] for b in pair], axis=0)
            cots = jnp.concatenate([halves[b // HALF][2][b % HALF] for b in pair], axis=0)
            value, slope = gelu_both(mm(inputs, sup_ref[...], NN))
            pre_grad = (mm(cots, sdown_ref[...], NT) * slope).astype(bf16)
            result = mm(value.astype(bf16), sdown_ref[...], NN)
            back = mm(pre_grad, sup_ref[...], NT)
            for place in range(len(pair)):
                span = slice(place * PATCHES, (place + 1) * PATCHES)
                shared_s[start + place, :, 0:width] = result[span]
                shared_s[start + place, :, width:] = back[span]

    @pl.when(step > 0)
    def _():
        member = step - 1
        tile = total_rows // 2
        for part in range(2):
            span = slice(part * tile, (part + 1) * tile)
            inputs, cots, gate = rows_s[member, span, :], cots_s[member, span, :], gate_s[member, span, :]
            value, slope = gelu_both(mm(inputs, eup_ref[0], NN))
            act_grad = mm(cots, edown_ref[0], NT)
            dot_s[member, span, :] = jnp.sum(value * act_grad, axis=1, keepdims=True)
            active = (gate * value).astype(bf16)
            pre_grad = (gate * act_grad * slope).astype(bf16)
            rows_s[member, span, :] = mm(active, edown_ref[0], NN).astype(bf16)
            cots_s[member, span, :] = mm(pre_grad, eup_ref[0], NT).astype(bf16)

    @pl.when(step == members)
    def _():
        for block in range(2 * HALF):
            out_ref = (first_ref, second_ref)[block // HALF]
            place = block % HALF
            hits, _ = block_hits(block)
            hot = (hits[0] | hits[1]).astype(bf16)
            span = slice(block * CAP, (block + 1) * CAP)
            dots = jnp.concatenate([dot_s[m, span, :] for m in range(members)], axis=0)
            sums = [jnp.sum(jnp.where(hit, dots, 0.0), axis=0, keepdims=True) for hit in hits]
            line = jnp.concatenate(sums + [jnp.zeros_like(sums[0])], axis=1)
            row_id = lax.broadcasted_iota(jnp.int32, (EXTRA, width), 0)
            out_ref[place, 2 * PATCHES :, :] = jnp.where(row_id == 0, line, 0.0).astype(bf16)
            for index, source in enumerate((rows_s, cots_s)):
                slots = jnp.concatenate([source[m, span, :] for m in range(members)], axis=0)
                total = mm(hot, slots, TN)
                if block in shared_ids:
                    where = shared_ids.index(block)
                    total = total + shared_s[where, :, index * width : (index + 1) * width]
                out_ref[place, index * PATCHES : (index + 1) * PATCHES, :] = total.astype(bf16)


def experts_both(base, blocks, shared_up, shared_down, expert_up, expert_down, shared_ids):
    members, width, hidden = expert_up.shape
    out = jax.ShapeDtypeStruct((HALF, 2 * PATCHES + EXTRA, width), bf16)
    out_spec = pl.BlockSpec(out.shape, lambda e, b: (0, 0, 0))
    return pl.pallas_call(
        functools.partial(expert_kernel, shared_ids),
        grid_spec=pltpu.PrefetchScalarGridSpec(
            num_scalar_prefetch=1,
            grid=(members + 1,),
            in_specs=[spec for part in blocks for spec in part.specs()]
            + [
                pl.BlockSpec((width, hidden), lambda e, b: (0, 0)),
                pl.BlockSpec((hidden, width), lambda e, b: (0, 0)),
                pl.BlockSpec((1, width, hidden), lambda e, b: (jnp.maximum(e - 1, 0), 0, 0)),
                pl.BlockSpec((1, hidden, width), lambda e, b: (jnp.maximum(e - 1, 0), 0, 0)),
            ],
            out_specs=(out_spec, out_spec),
            scratch_shapes=[
                pltpu.VMEM((members, 2 * HALF * CAP, width), bf16),
                pltpu.VMEM((members, 2 * HALF * CAP, width), bf16),
                pltpu.VMEM((members, 2 * HALF * CAP, 1), f32),
                pltpu.VMEM((members, 2 * HALF * CAP, 1), f32),
                pltpu.VMEM((max(len(shared_ids), 1), PATCHES, 2 * width), f32),
            ],
        ),
        out_shape=(out, out),
        compiler_params=params(),
        cost_estimate=cost(30 * 10**9, 30 * 10**6),
        name="experts_both",
    )(
        base, *[operand for part in blocks for operand in part.operands()],
        shared_up, shared_down, expert_up, expert_down,
    )


def grads_kernel(count, tile, started, *refs):
    row_refs, cot_refs = refs[:count], refs[count : 2 * count]
    up_ref, down_ref = refs[2 * count : 2 * count + 2]
    up_grad_ref, down_grad_ref = refs[-2:]
    width = up_ref.shape[1]
    inputs = [ref[...].reshape(-1, width) for ref in row_refs]
    cots = [ref[...].reshape(-1, width) for ref in cot_refs]
    groups = max(1, count * inputs[0].shape[0] // tile)
    each = count // groups
    for group in range(groups):
        part = slice(group * each, (group + 1) * each)
        rows, cot = jnp.concatenate(inputs[part], axis=0), jnp.concatenate(cots[part], axis=0)
        value, slope = gelu_both(mm(up_ref[0], rows, TT))
        pre_grad = (mm(down_ref[0], cot, NT) * slope).astype(bf16)
        up_grad = mm(rows, pre_grad, TT)
        down_grad = mm(value.astype(bf16), cot, NN)
        if group == 0 and started:
            up_grad_ref[0] = refs[2 * count + 2][0] + up_grad
            down_grad_ref[0] = refs[2 * count + 3][0] + down_grad
        elif group == 0:
            up_grad_ref[0] = up_grad
            down_grad_ref[0] = down_grad
        else:
            up_grad_ref[0] += up_grad
            down_grad_ref[0] += down_grad


def weight_grads(rows, cots, specs, up, down, before, tile, total):
    members, width, hidden = up.shape
    up_spec = pl.BlockSpec((1, width, hidden), lambda e: (e, 0, 0))
    down_spec = pl.BlockSpec((1, hidden, width), lambda e: (e, 0, 0))
    started = before is not None
    count = len(rows)
    return pl.pallas_call(
        functools.partial(grads_kernel, count, tile, started),
        grid=(members,),
        in_specs=specs + [up_spec, down_spec] + ([up_spec, down_spec] if started else []),
        out_specs=(up_spec, down_spec),
        out_shape=(
            jax.ShapeDtypeStruct(up.shape, f32),
            jax.ShapeDtypeStruct(down.shape, f32),
        ),
        input_output_aliases={2 * count + 2: 0, 2 * count + 3: 1} if started else {},
        compiler_params=params(),
        cost_estimate=cost(12 * total * width * hidden, total * width * 4),
        name="weight_grads",
    )(*rows, *cots, up, down, *(before or ()))


def routed_grads(slots, up, down, before):
    members, count, width = slots[0][0].shape
    spec = pl.BlockSpec((1, count, width), lambda e: (e, 0, 0))
    rows, cots = [pair[0] for pair in slots], [pair[1] for pair in slots]
    specs = [spec] * (2 * len(slots))
    return weight_grads(
        rows, cots, specs, up, down, before, len(slots) * count, len(slots) * members * count
    )


def shared_grads(blocks, up, down, before):
    rows, cots = [part.rows for part in blocks], [part.cots for part in blocks]
    all_specs = [part.specs() for part in blocks]
    specs = [spec[0] for spec in all_specs] + [spec[2] for spec in all_specs]
    return weight_grads(
        rows, cots, specs, up[None], down[None], before, 2 * HALF * PATCHES, len(blocks) * HALF * PATCHES
    )


def backward_kernel(
    local_width, moe_ref, moe_more_ref, back_ref, back_more_ref, tok_ref, cot_ref, mod_ref, router_ref, pairs_ref, attn_in_ref,
    qkv_ref, context_ref, attn_out_ref, ext_ref, w0, w1, w2, w3,
    output_ref, tok_grad_ref, small_ref, near_ref, far_ref, grad_s,
):
    def put_weight_grad(first, grad):
        for index in range(len(shards)):
            out_ref = (near_ref, far_ref)[index % 2]
            out_ref[index // 2, first : first + local_width, :] = grad[
                index * local_width : (index + 1) * local_width
            ]

    shards = (w0, w1, w2, w3)
    rows, width = tok_ref.shape
    mod = mod_ref[...]
    stream = tok_ref[...].astype(f32)
    attn_out = attn_out_ref[...]
    residual = stream + mod[2:3] * attn_out
    second_norm, second_inv = normalize(residual)
    moe_out = moe_ref[...] + moe_more_ref[...].astype(f32)
    back = back_ref[...] + back_more_ref[...].astype(f32)
    upstream = cot_ref[...].astype(f32)
    output_ref[...] = (residual + mod[5:6] * moe_out).astype(bf16)
    gate_two_grad = jnp.sum(upstream * moe_out, axis=0, keepdims=True)
    routes, places, gates = read_pairs(ext_ref[rows:, :])
    dots = (back[rows : rows + 1, 0:PATCHES], back[rows : rows + 1, PATCHES : 2 * PATCHES])
    mean_dot = gates[0] * dots[0] + gates[1] * dots[1]
    pairs = pairs_ref[...]
    expert_id = lax.broadcasted_iota(jnp.int32, (EXPERTS, rows), 0)
    logits_grad = jnp.zeros((EXPERTS, rows), f32)
    for k in range(TOPK):
        logits_grad += jnp.where(expert_id == pairs[k : k + 1], gates[k] * (dots[k] - mean_dot), 0.0)
    logits_grad = logits_grad.astype(bf16)
    moe_in_grad = back[0:rows] + mm(logits_grad, router_ref[...], TN)
    shift_two_grad = jnp.sum(moe_in_grad, axis=0, keepdims=True)
    scale_two_grad = jnp.sum(moe_in_grad * second_norm, axis=0, keepdims=True)
    residual_grad = upstream + normalize_back(
        second_norm, second_inv, moe_in_grad * (1.0 + mod[4:5])
    )
    gate_one_grad = jnp.sum(residual_grad * attn_out, axis=0, keepdims=True)
    attn_grad = (mod[2:3] * residual_grad).astype(bf16)
    out_grad = mm(context_ref[...], attn_grad, TN).astype(bf16)
    put_weight_grad(3 * local_width, out_grad)
    context_grad = mm(attn_grad, shard_rows(shards, 3, local_width), NT).astype(bf16)
    masks = pair_masks(rows)
    zero = jnp.zeros((rows, 2 * HD), bf16)
    scale = 1.0 / math.sqrt(HD)
    for pair in range(width // (2 * HD)):
        cols = slice(pair * 2 * HD, (pair + 1) * 2 * HD)
        query, key, value = qkv_ref[0, :, cols], qkv_ref[1, :, cols], qkv_ref[2, :, cols]
        upper = context_grad[:, cols]
        sums = []
        for mask in masks:
            probs = head_probs(jnp.where(mask, query, zero), key)
            probs_grad = mm(jnp.where(mask, upper, zero), value, NT)
            value_grad = mm(probs.astype(bf16), upper, TN)
            score_grad = (
                probs * (probs_grad - jnp.sum(probs_grad * probs, axis=-1, keepdims=True))
            ).astype(bf16)
            sums.append((mm(score_grad, key, NN) * scale, mm(score_grad, query, TN) * scale, value_grad))
        for part in range(3):
            grad_s[part, :, cols] = jnp.where(masks[0], sums[0][part], sums[1][part]).astype(bf16)
    attn_in = attn_in_ref[...]
    attn_in_grad = jnp.zeros((rows, width), f32)
    for part in range(3):
        grad = grad_s[part]
        attn_in_grad += mm(grad, shard_rows(shards, part, local_width), NN)
        put_weight_grad(part * local_width, mm(grad, attn_in, TN).astype(bf16))
    first_norm, first_inv = normalize(stream)
    shift_one_grad = jnp.sum(attn_in_grad, axis=0, keepdims=True)
    scale_one_grad = jnp.sum(attn_in_grad * first_norm, axis=0, keepdims=True)
    tok_grad_ref[...] = residual_grad + normalize_back(
        first_norm, first_inv, attn_in_grad * (1.0 + mod[1:2])
    )
    lines = (
        shift_one_grad, scale_one_grad, gate_one_grad, shift_two_grad, scale_two_grad, gate_two_grad,
    )
    row_id = lax.broadcasted_iota(jnp.int32, (8, width), 0)
    stacked = jnp.zeros((8, width), f32)
    for index, line in enumerate(lines):
        stacked = jnp.where(row_id == index, line, stacked)
    small_ref[0:8, :] = stacked
    small_ref[8:16, :] = mm(logits_grad, ext_ref[0:rows, :], NN)


def attention_backward(
    moe, moe_more, back, back_more, tokens, cotangent, mod, router_t, pairs, attn_in, qkv, context, attn_out,
    ext, shards, local_width,
):
    rows, width = tokens.shape
    halves = jax.ShapeDtypeStruct((len(shards) // 2, 4 * local_width, width), bf16)
    return pl.pallas_call(
        functools.partial(backward_kernel, local_width),
        out_shape=(
            jax.ShapeDtypeStruct((rows, width), bf16),
            jax.ShapeDtypeStruct((rows, width), f32),
            jax.ShapeDtypeStruct((16, width), f32),
            halves,
            halves,
        ),
        scratch_shapes=[pltpu.VMEM((3, rows, width), bf16)],
        compiler_params=params(),
        cost_estimate=cost(10 * 10**9, 16 * 10**6),
        name="attention_backward",
    )(
        moe, moe_more, back, back_more, tokens, cotangent, mod, router_t, pairs, attn_in, qkv, context,
        attn_out, ext, *shards,
    )


def local_call(kernel, name, outs, operands, scalars=None, moved=4 * 10**6):
    count = 0 if scalars is None else 1
    vmem = pl.BlockSpec(memory_space=pltpu.VMEM)
    smem = pl.BlockSpec(memory_space=pltpu.SMEM)
    return pl.pallas_call(
        kernel,
        in_specs=[smem] * count + [vmem] * len(operands),
        out_specs=tuple(vmem for _ in outs),
        out_shape=tuple(jax.ShapeDtypeStruct(*out) for out in outs),
        compiler_params=params(),
        cost_estimate=cost(0, moved),
        name=name,
    )(*([] if scalars is None else [scalars]), *operands)


def plane_first_kernel(first, more, side, other, keep_upper, keep_lower):
    cut = PATCHES
    upper = lambda block: first[block, 0:cut, :].astype(f32) + more[block, 0:cut, :].astype(f32)
    lower = lambda block: first[block, cut:, :].astype(f32) + more[block, cut:, :].astype(f32)
    side[0], side[1] = upper(1).astype(bf16), upper(3).astype(bf16)
    other[0], other[1] = lower(2).astype(bf16), lower(3).astype(bf16)
    keep_upper[0], keep_upper[1] = upper(0), upper(2)
    keep_lower[0], keep_lower[1] = lower(0), lower(1)


def plane_second_kernel(keep_upper, keep_lower, side, other, upper, lower, upper_next, lower_next):
    upper[...] = keep_upper[0] + side[0].astype(f32)
    upper_next[...] = (keep_upper[1] + side[1].astype(f32)).astype(bf16)
    lower[...] = keep_lower[0] + other[0].astype(f32)
    lower_next[...] = (keep_lower[1] + other[1].astype(f32)).astype(bf16)


def span_of(index, size):
    return pl.ds(pl.multiple_of(index * size, size), size)


def dense_first_kernel(place, near, more, side, other, keep_upper, keep_lower):
    cut = near.shape[1] // 2
    half = cut // 2
    mine = place[0]
    side[...] = (near[1, 0:cut, :].astype(f32) + more[1, 0:cut, :].astype(f32)).astype(bf16)
    keep_upper[...] = near[0, 0:cut, :].astype(f32) + more[0, 0:cut, :].astype(f32)
    for index in range(2):
        for out, who in ((keep_lower, mine), (other, 1 - mine)):
            rows = pl.ds(pl.multiple_of(cut + who * half, half), half)
            total = near[index, rows, :].astype(f32) + more[index, rows, :].astype(f32)
            out[index] = total.astype(out.dtype)


def dense_second_kernel(place, keep_upper, keep_lower, from_side, from_other, side, other, upper, lower):
    half = upper.shape[0]
    mine = place[0]
    for out, who in ((upper, mine), (other, 1 - mine)):
        rows = span_of(who, half)
        out[...] = (keep_upper[rows, :] + from_side[rows, :].astype(f32)).astype(out.dtype)
    lower[...] = keep_lower[0] + from_other[0].astype(f32)
    side[...] = (keep_lower[1] + from_other[1].astype(f32)).astype(bf16)


def dense_third_kernel(size, place, upper, lower, from_side, from_other, own, sent, total):
    half = upper.shape[0]
    share = 2 * half // size
    total[0:half, :] = upper[...] + from_other[...].astype(f32)
    total[half:, :] = lower[...] + from_side[...].astype(f32)
    own[...] = total[span_of(place[1], share), :]
    for hop in range(1, size):
        sent[hop - 1] = total[span_of(lax.rem(place[1] + hop, size), share), :].astype(bf16)


def dense_fourth_kernel(own, *refs):
    out = refs[-1]
    total = own[...]
    for ref in refs[:-1]:
        total = total + ref[...].astype(f32)
    out[...] = total.astype(bf16)


def dense_fifth_kernel(size, place, own, *refs):
    out = refs[-1]
    share = own.shape[0]
    out[span_of(place[1], share), :] = own[...]
    for hop in range(1, size):
        out[span_of(lax.rem(place[1] + size - hop, size), share), :] = refs[hop - 1][...]


def dense_last_kernel(place, own, more, out):
    half = own.shape[0] // 2
    for ref, who in ((own, place[0]), (more, 1 - place[0])):
        for index in range(2):
            rows = pl.ds(pl.multiple_of(2 * half * index + who * half, half), half)
            out[rows, :] = ref[index * half : (index + 1) * half, :].astype(f32)


class Links:
    def __init__(self, mesh):
        self.dp, self.expert, self.tensor = (mesh.shape[name] for name in ("dp", "expert", "tensor"))
        self.paired = self.expert == 2 and self.tensor == 4
        self.core = [(i, i ^ 1) for i in range(self.tensor)]
        self.side = [(i, i ^ 2) for i in range(self.tensor)]
        self.other = [(0, 1), (1, 0)]

    def to_core(self, value):
        return lax.ppermute(value, "tensor", self.core)

    def to_side(self, value):
        return lax.ppermute(value, "tensor", self.side)

    def to_other(self, value):
        return lax.ppermute(value, "expert", self.other)

    def along(self, value, hop):
        return lax.ppermute(value, "dp", [(i, (i + hop) % self.dp) for i in range(self.dp)])

    def plane(self, block, after=()):
        rows, width = block.shape
        cut = (rows // 2 + 15) // 16 * 16
        side, other = self.to_side(block), self.to_other(block)
        upper, lower = self.to_side(other[:cut]), self.to_other(side[cut:])
        everything = slice(None)
        plan = [(index, everything, index) for index in range(3)]
        plan += [(3, everything, (3, pl.ds(0, cut))), (4, everything, (3, pl.ds(cut, rows - cut)))]
        mine = assemble((HALF, rows, width), block.dtype, (block, side, other, upper, lower), plan, after)
        return mine, self.to_core(mine)

    def everywhere(self, small):
        stack = jnp.stack([small] + [self.along(small, hop) for hop in range(1, self.dp)])
        side, other = self.to_side(stack), self.to_other(stack)
        chips = jnp.stack([stack, side, other, self.to_side(other)])
        cores = jnp.stack([chips, self.to_core(chips)])
        return cores.transpose((2, 0, 1) + tuple(range(3, cores.ndim)))

    def plane_sum(self, first, second):
        width = first.shape[2]
        low = first.shape[1] - PATCHES
        side, other, keep_upper, keep_lower = local_call(
            plane_first_kernel,
            "plane_first",
            [((2, PATCHES, width), bf16), ((2, low, width), bf16), ((2, PATCHES, width), f32), ((2, low, width), f32)],
            [first, self.to_core(second)],
        )
        upper, lower, upper_next, lower_next = local_call(
            plane_second_kernel,
            "plane_second",
            [((PATCHES, width), f32), ((low, width), f32), ((PATCHES, width), bf16), ((low, width), bf16)],
            [keep_upper, keep_lower, self.to_side(side), self.to_other(other)],
        )
        return upper, self.to_other(upper_next), lower, self.to_side(lower_next)

    def dense_sum(self, near, far):
        _, rows, width = near.shape
        cut, half, share = rows // 2, rows // 4, rows // 2 // self.dp
        place = jnp.stack([lax.axis_index("expert"), lax.axis_index("dp")]).astype(jnp.int32)
        side, other, keep_upper, keep_lower = local_call(
            dense_first_kernel,
            "dense_first",
            [((cut, width), bf16), ((2, half, width), bf16), ((cut, width), f32), ((2, half, width), f32)],
            [near, self.to_core(far)],
            place,
        )
        side, other, upper, lower = local_call(
            dense_second_kernel,
            "dense_second",
            [((half, width), bf16), ((half, width), bf16), ((half, width), f32), ((half, width), f32)],
            [keep_upper, keep_lower, self.to_side(side), self.to_other(other)],
            place,
        )
        own, sent, _ = local_call(
            functools.partial(dense_third_kernel, self.dp),
            "dense_third",
            [((share, width), f32), ((self.dp - 1, share, width), bf16), ((cut, width), f32)],
            [upper, lower, self.to_side(side), self.to_other(other)],
            place,
        )
        hops = range(1, self.dp)
        (total,) = local_call(
            dense_fourth_kernel,
            "dense_fourth",
            [((share, width), bf16)],
            [own] + [self.along(sent[hop - 1], hop) for hop in hops],
        )
        (column,) = local_call(
            functools.partial(dense_fifth_kernel, self.dp),
            "dense_fifth",
            [((cut, width), bf16)],
            [total] + [self.along(total, hop) for hop in hops],
            place,
        )
        (result,) = local_call(
            dense_last_kernel, "dense_last", [((rows, width), f32)], [column, self.to_other(column)], place
        )
        return result


def local(
    links,
    tokens,
    cotangent,
    timesteps,
    ada_weight,
    ada_bias,
    qkv_weight,
    out_weight,
    router_weight,
    shared_up,
    shared_down,
    expert_up,
    expert_down,
    routes,
    places,
):
    rows, width = tokens.shape
    local_width = qkv_weight.shape[2]
    members = expert_up.shape[0]
    me = lax.axis_index("tensor")
    base = (lax.axis_index("expert") * members).astype(jnp.int32).reshape(1)
    everyone = ("dp", "expert", "tensor")
    total_blocks = links.dp * links.expert * links.tensor
    full = links.paired and total_blocks * rows * width * 2 <= FULL_LIMIT

    weight = jnp.concatenate(
        [qkv_weight.transpose(1, 2, 0).reshape(3 * local_width, width), out_weight], axis=0
    )
    across = links.to_side(weight)
    shards = (weight, links.to_core(weight), across, links.to_core(across))

    condition = jax.nn.silu(embedding(timesteps, width)).astype(bf16)
    mod_cols = jnp.einsum("id,dcf->icf", condition, ada_weight, preferred_element_type=f32) + ada_bias[None]
    mod = lax.all_to_all(mod_cols, "tensor", split_axis=0, concat_axis=2, tiled=True)[0]
    own_condition = lax.dynamic_slice_in_dim(condition.astype(f32), me, 1, axis=0)
    shared_cot = moe_cotangent(mod, cotangent, across)
    router_t = router_weight.T
    pairs = jnp.concatenate([routes.T, places.T], axis=0)

    attn_in, qkv, context, attn_out, ext, both = attention_forward(
        tokens, mod, own_condition, router_t, pairs, shared_cot, shards, local_width
    )
    feed = (shared_up, shared_down, expert_up, expert_down)
    if links.paired:
        cots = links.plane(shared_cot)
        exts = links.plane(ext)
        planes = [tuple(Blocks.apart(*pair) for pair in zip(exts, cots))]
        first, second = experts_both(base, planes[0], *feed, (0, 1, 4, 5))
        upper, upper_more, lower, lower_more = links.plane_sum(first, second)
    else:
        shift = lax.axis_index("expert") * links.tensor
        gather = lambda block: jnp.roll(
            lax.all_gather(block, ("expert", "tensor"), axis=0), -shift, axis=0
        )
        all_ext, all_cot = gather(ext), gather(shared_cot)
        planes, sums = [], []
        for start in range(0, links.expert * links.tensor, 2 * HALF):
            spans = [slice(start + HALF * part, start + HALF * (part + 1)) for part in range(2)]
            planes.append(tuple(Blocks.apart(all_ext[span], all_cot[span]) for span in spans))
            shared_ids = tuple(range(links.tensor)) if start == 0 else ()
            sums += experts_both(base, planes[-1], *feed, shared_ids)
        blocks = jnp.roll(jnp.concatenate(sums, axis=0), shift, axis=0)
        total = lax.psum_scatter(blocks, ("expert", "tensor"), scatter_dimension=0, tiled=True)[0]
        upper, lower = total[:PATCHES].astype(f32), total[PATCHES:].astype(f32)
        upper_more, lower_more = jnp.zeros_like(total[:PATCHES]), jnp.zeros_like(total[PATCHES:])

    output, tokens_grad, small, near, far = attention_backward(
        upper, upper_more, lower, lower_more, tokens, cotangent, mod, router_t, pairs,
        attn_in, qkv, context, attn_out, ext, shards, local_width,
    )

    if full:
        hops = [links.plane(links.along(both, hop)) for hop in range(1, links.dp)]
        planes += [tuple(Blocks.joined(part) for part in parts) for parts in hops]
    slots = [dispatch(base, plane, members) for plane in planes]
    routed, shared = None, None
    for start in range(0, len(planes), 2):
        routed = routed_grads(slots[start : start + 2], expert_up, expert_down, routed)
        parts = [part for plane in planes[start : start + 2] for part in plane]
        shared = shared_grads(parts, shared_up, shared_down, shared)

    if full:
        small_all = links.everywhere(small).reshape(-1, 16, width)
        extra_all = jnp.concatenate([part.extra() for plane in planes for part in plane], axis=0)
        condition_all = extra_all[:, 3]
        routes_all = extra_all[:, 0, : TOPK * PATCHES]
        dense = links.dense_sum(near, far)
    else:
        routed = lax.psum(routed, "dp")
        shared = lax.psum(shared, "dp")
        small_all = lax.all_gather(small, everyone, axis=0)
        condition_all = lax.all_gather(own_condition[0], everyone, axis=0).astype(bf16)
        routes_all = lax.all_gather(routes.reshape(-1), everyone, axis=0)
        order = jnp.arange(links.tensor) ^ me
        grads = jnp.stack([near, far], axis=1).reshape((-1,) + near.shape[1:])[order]
        dense = lax.psum_scatter(grads, "tensor", scatter_dimension=0, tiled=True)[0]
        dense = lax.psum(dense, ("dp", "expert")).astype(f32)

    mod_grad = lax.dynamic_slice_in_dim(small_all[:, 0:6], me * local_width, local_width, axis=2)
    ada_grad = jnp.einsum(
        "id,icf->dcf", condition_all.astype(f32), mod_grad, precision=lax.Precision.HIGHEST
    )
    ada_bias_grad = jnp.sum(mod_grad, axis=0)
    router_grad = jnp.sum(small_all[:, 8:16], axis=0).T
    counts = jnp.sum(
        (routes_all[:, :, None] == jnp.arange(EXPERTS).astype(routes_all.dtype)).astype(jnp.int32),
        axis=(0, 1),
    )
    qkv_grad = dense[: 3 * local_width].reshape(3, local_width, width).transpose(2, 0, 1)
    return (
        output,
        tokens_grad,
        ada_grad,
        ada_bias_grad,
        qkv_grad,
        dense[3 * local_width :],
        router_grad,
        shared[0][0],
        shared[1][0],
        routed[0],
        routed[1],
        counts,
    )


def solution(mesh):
    rows = P(("dp", "expert", "tensor"), None)
    placed = (
        rows,
        rows,
        P(("dp", "expert")),
        P(None, None, "tensor"),
        P(None, "tensor"),
        P(None, None, "tensor"),
        P("tensor", None),
        P(),
        P(None, "tensor"),
        P("tensor", None),
        P("expert", None, "tensor"),
        P("expert", "tensor", None),
        rows,
        rows,
    )
    return jax.shard_map(
        functools.partial(local, Links(mesh)),
        mesh=mesh,
        in_specs=placed,
        out_specs=(
            rows,
            rows,
            P(None, None, "tensor"),
            P(None, "tensor"),
            P(None, None, "tensor"),
            P("tensor", None),
            P(),
            P(None, "tensor"),
            P("tensor", None),
            P("expert", None, "tensor"),
            P("expert", "tensor", None),
            P(),
        ),
        check_vma=False,
    )
```

```python
import functools
import math

import jax
import jax.numpy as jnp
from jax import lax
from jax.experimental import pallas as pl
from jax.experimental.pallas import tpu as pltpu
from jax.sharding import PartitionSpec as P

HD = 64
EXPERTS = 8
TOPK = 2
PATCHES = 256
CAP = 80
EXTRA = 16
EPSILON = 1e-06
HALF = 4
FULL_LIMIT = 32 * 1024 * 1024
VMEM_LIMIT = 58 * 1024 * 1024

f32 = jnp.float32
bf16 = jnp.bfloat16
NN = (((1,), (0,)), ((), ()))
NT = (((1,), (1,)), ((), ()))
TN = (((0,), (0,)), ((), ()))
TT = (((0,), (1,)), ((), ()))


def mm(left, right, dims):
    return lax.dot_general(left, right, dims, preferred_element_type=f32)


def normalize(values):
    center = jnp.mean(values, axis=-1, keepdims=True)
    shifted = values - center
    inverse = lax.rsqrt(jnp.mean(shifted * shifted, axis=-1, keepdims=True) + EPSILON)
    return (shifted * inverse, inverse)


def normalize_back(normed, inverse, upstream):
    return inverse * (
        upstream
        - jnp.mean(upstream, axis=-1, keepdims=True)
        - normed * jnp.mean(upstream * normed, axis=-1, keepdims=True)
    )


def embedding(steps, model_width):
    half_width = model_width // 2
    freqs_all = jnp.exp(-math.log(10000.0) * jnp.arange(half_width, dtype=f32) / half_width)
    angles = steps.astype(f32)[:, None] * freqs_all[None, :]
    return jnp.concatenate([jnp.cos(angles), jnp.sin(angles)], axis=1)


def gelu_both(pre):
    const = math.sqrt(2.0 / math.pi)
    square = pre * pre
    tanh = jnp.tanh(const * pre * (1.0 + 0.044715 * square))
    half = 0.5 + 0.5 * tanh
    value = pre * half
    return value, half + value * (1.0 - tanh) * (const + 3.0 * 0.044715 * const * square)


def launch(
    kernel, name, outs, operands, *, in_specs=None, out_specs=None, grid=(), scalars=(), scratch=(), aliases=None,
    after=(), flops=0, moved=0,
):
    lead = len(scalars)
    count = lead + len(operands)
    waits = len(after)
    on_chip = pl.BlockSpec(memory_space=pltpu.VMEM)
    anywhere = pl.BlockSpec(memory_space=pl.ANY)
    in_specs = list(in_specs or [on_chip] * len(operands)) + [anywhere] * waits
    out_specs = tuple(out_specs or [on_chip] * len(outs))

    def body(*refs):
        kernel(*refs[:count], *refs[count + waits :])

    if scalars and grid:
        shape = dict(
            grid_spec=pltpu.PrefetchScalarGridSpec(
                num_scalar_prefetch=lead, grid=grid, in_specs=in_specs, out_specs=out_specs, scratch_shapes=scratch
            )
        )
    else:
        in_specs = [pl.BlockSpec(memory_space=pltpu.SMEM)] * lead + in_specs
        shape = dict(grid=grid, in_specs=in_specs, out_specs=out_specs, scratch_shapes=scratch)
    return pl.pallas_call(
        body,
        out_shape=tuple(jax.ShapeDtypeStruct(*out) for out in outs),
        input_output_aliases=aliases or {},
        compiler_params=pltpu.CompilerParams(vmem_limit_bytes=VMEM_LIMIT),
        cost_estimate=pl.CostEstimate(flops=int(flops), bytes_accessed=int(moved), transcendentals=0),
        name=name,
        **shape,
    )(*scalars, *operands, *after)


def copy_kernel(plan, count, *refs):
    sources, out, sems = refs[:count], refs[-2], refs[-1]
    copies = [
        pltpu.make_async_copy(sources[index].at[take], out.at[put], sems.at[order])
        for order, (index, take, put) in enumerate(plan)
    ]
    for copy in copies:
        copy.start()
    for copy in copies:
        copy.wait()


def assemble(shape, dtype, sources, plan, after=()):
    size = math.prod(shape) * jnp.dtype(dtype).itemsize
    return launch(
        functools.partial(copy_kernel, plan, len(sources)), "assemble", [(shape, dtype)], sources,
        in_specs=[pl.BlockSpec(memory_space=pl.ANY)] * len(sources),
        scratch=[pltpu.SemaphoreType.DMA((len(plan),))], after=after, moved=2 * size,
    )[0]


def order_kernel(*refs):
    pass


def ordered(values, after):
    anywhere = [pl.BlockSpec(memory_space=pl.ANY)] * len(values)
    return launch(
        order_kernel, "ordered", [(value.shape, value.dtype) for value in values], values, in_specs=anywhere,
        out_specs=anywhere, aliases={index: index for index in range(len(values))}, after=after,
    )


def pair_masks(rows):
    lane = lax.broadcasted_iota(jnp.int32, (rows, 2 * HD), 1)
    return (lane < HD, lane >= HD)


def head_probs(query, key):
    scores = mm(query, key, NT) * (1.0 / math.sqrt(HD))
    weights = jnp.exp(scores - jnp.max(scores, axis=-1, keepdims=True))
    return weights / jnp.sum(weights, axis=-1, keepdims=True)


def shard_rows(shards, part, local_width):
    return jnp.concatenate(
        [shard[part * local_width : (part + 1) * local_width, :] for shard in shards], axis=0
    )


def attention_kernel(
    local_width, tok_ref, mod_ref, router_ref, pairs_ref, w0, w1, w2, w3,
    attn_in_ref, qkv_ref, context_ref, attn_out_ref, ext_ref,
):
    shards = (w0, w1, w2, w3)
    rows, width = tok_ref.shape
    mod = mod_ref[...]
    stream = tok_ref[...].astype(f32)
    attn_in = (normalize(stream)[0] * (1.0 + mod[1:2]) + mod[0:1]).astype(bf16)
    attn_in_ref[...] = attn_in
    for part in range(3):
        qkv_ref[part] = mm(attn_in, shard_rows(shards, part, local_width), NT).astype(bf16)
    masks = pair_masks(rows)
    zero = jnp.zeros((rows, 2 * HD), bf16)
    for pair in range(width // (2 * HD)):
        cols = slice(pair * 2 * HD, (pair + 1) * 2 * HD)
        query, key, value = qkv_ref[0, :, cols], qkv_ref[1, :, cols], qkv_ref[2, :, cols]
        parts = []
        for mask in masks:
            probs = head_probs(jnp.where(mask, query, zero), key)
            parts.append(mm(probs.astype(bf16), value, NN))
        context_ref[:, cols] = jnp.where(masks[0], parts[0], parts[1]).astype(bf16)
    attn_out = mm(context_ref[...], shard_rows(shards, 3, local_width), NN)
    attn_out_ref[...] = attn_out
    residual = stream + mod[2:3] * attn_out
    moe_in = (normalize(residual)[0] * (1.0 + mod[4:5]) + mod[3:4]).astype(bf16)
    ext_ref[0:rows, :] = moe_in
    logits = mm(router_ref[...], moe_in, NT)
    pairs = pairs_ref[...]
    expert_id = lax.broadcasted_iota(jnp.int32, (EXPERTS, rows), 0)
    chosen = [
        jnp.sum(jnp.where(expert_id == pairs[k : k + 1], logits, 0.0), axis=0, keepdims=True)
        for k in range(TOPK)
    ]
    top = jnp.maximum(chosen[0], chosen[1])
    powers = [jnp.exp(value - top) for value in chosen]
    gates = [power / (powers[0] + powers[1]) for power in powers]
    high = [gate.astype(bf16).astype(f32) for gate in gates]
    rest = [gate - upper for gate, upper in zip(gates, high)]
    values = pairs.astype(f32)
    packed = (
        jnp.concatenate([values[0:1], values[1:2], values[2:3]], axis=1),
        jnp.concatenate([values[3:4], high[0], high[1]], axis=1),
        jnp.concatenate([rest[0], rest[1], jnp.zeros_like(rest[0])], axis=1),
    )
    row_id = lax.broadcasted_iota(jnp.int32, (EXTRA, width), 0)
    extra = jnp.zeros((EXTRA, width), f32)
    for index, line in enumerate(packed):
        extra = jnp.where(row_id == index, line, extra)
    ext_ref[rows : rows + EXTRA, :] = extra.astype(bf16)


def attention_forward(tokens, mod, router_t, pairs, shards, local_width):
    rows, width = tokens.shape
    outs = [
        ((rows, width), bf16),
        ((3, rows, width), bf16),
        ((rows, width), bf16),
        ((rows, width), f32),
        ((rows + EXTRA, width), bf16),
    ]
    return launch(
        functools.partial(attention_kernel, local_width), "attention_forward", outs,
        [tokens, mod, router_t, pairs, *shards], flops=5 * 10**9, moved=9 * 10**6,
    )


def read_pairs(extra):
    info = extra.astype(f32)
    count = PATCHES
    routes = (info[0:1, 0:count], info[0:1, count : 2 * count])
    places = (info[0:1, 2 * count : 3 * count], info[1:2, 0:count])
    gates = (
        info[1:2, count : 2 * count] + info[2:3, 0:count],
        info[1:2, 2 * count : 3 * count] + info[2:3, count : 2 * count],
    )
    return routes, places, gates


def slot_hits(routes, places, base, slots):
    slot_id = lax.broadcasted_iota(jnp.int32, (slots, PATCHES), 0).astype(f32)
    return [
        slot_id == jnp.where(place < CAP, (route - base) * CAP + place, -1.0)
        for route, place in zip(routes, places)
    ]


def slot_gates(hits, gates):
    return jnp.sum(
        jnp.where(hits[0], gates[0], 0.0) + jnp.where(hits[1], gates[1], 0.0), axis=1, keepdims=True
    )


class Blocks:
    def __init__(self, rows, rows_at, extra_at, cots, cots_at):
        self.rows, self.rows_at, self.extra_at, self.cots, self.cots_at = rows, rows_at, extra_at, cots, cots_at

    @classmethod
    def apart(cls, ext, cots):
        return cls(ext, 0, PATCHES // EXTRA, cots, 0)

    def operands(self):
        return [self.rows, self.rows, self.cots]

    def specs(self, taken=HALF):
        width = self.rows.shape[2]
        places = ((PATCHES, self.rows_at), (EXTRA, self.extra_at), (PATCHES, self.cots_at))
        return [
            pl.BlockSpec((taken, count, width), lambda *_, at=at: (0, at, 0)) for count, at in places
        ]

    def extra(self):
        return self.rows[:, self.extra_at * EXTRA : (self.extra_at + 1) * EXTRA]


def dispatch_kernel(base_ref, *refs):
    rows_ref, cots_ref = refs[-2:]
    members = rows_ref.shape[0]
    base = base_ref[0].astype(f32)
    for part in range(2):
        rows_in, extra_in, cots_in = refs[3 * part : 3 * part + 3]

        @pl.when(pl.program_id(0) == part)
        def _():
            for block in range(HALF):
                dispatch_block(
                    base, members, rows_in[block], extra_in[block], cots_in[block], rows_ref, cots_ref, block
                )


def dispatch_block(base, members, rows, extra, cots, rows_ref, cots_ref, block):
    routes, places, gates = read_pairs(extra)
    hits = slot_hits(routes, places, base, members * CAP)
    hot = (hits[0] | hits[1]).astype(bf16)
    picked = mm(hot, rows, NN).astype(bf16)
    scaled = (mm(hot, cots, NN) * slot_gates(hits, gates)).astype(bf16)
    for member in range(members):
        span = slice(member * CAP, (member + 1) * CAP)
        rows_ref[member, block * CAP : (block + 1) * CAP, :] = picked[span]
        cots_ref[member, block * CAP : (block + 1) * CAP, :] = scaled[span]


def hops_kernel(place_ref, ext, cots, rows_ref, cots_ref):
    base = place_ref[0].astype(f32)
    for block in range(ext.shape[1]):
        dispatch_block(
            base, rows_ref.shape[0], ext[0, block, :PATCHES], ext[0, block, PATCHES:], cots[0, block], rows_ref,
            cots_ref, block,
        )


def plane_of(hop, place, planes):
    return lax.rem(place[2] + hop + 1, planes)


def dispatch_hops(place, ext, cots, members, after=()):
    planes, blocks, rows, width = ext.shape
    out = ((members, (planes - 1) * blocks * CAP, width), bf16)
    out_spec = pl.BlockSpec((members, blocks * CAP, width), lambda h, p: (0, h, 0))
    specs = [
        pl.BlockSpec((1, blocks, count, width), lambda h, p: (plane_of(h, p, planes), 0, 0, 0))
        for count in (rows, PATCHES)
    ]
    return launch(
        hops_kernel, "dispatch_hops", [out, out], [ext, cots], in_specs=specs, out_specs=[out_spec, out_spec],
        grid=(planes - 1,), scalars=[place], after=after, flops=24 * 10**9, moved=48 * 10**6,
    )


def dispatch(base, blocks, members, after=()):
    width = blocks[0].rows.shape[2]
    out = ((members, 2 * HALF * CAP, width), bf16)
    out_spec = pl.BlockSpec((members, HALF * CAP, width), lambda c, *_: (0, c, 0))
    return launch(
        dispatch_kernel, "dispatch", [out, out], [operand for part in blocks for operand in part.operands()],
        in_specs=[spec for part in blocks for spec in part.specs()], out_specs=[out_spec, out_spec],
        grid=(2,), scalars=[base], after=after, flops=8 * 10**9, moved=16 * 10**6,
    )


def expert_kernel(
    shared_ids, base_ref, rows0, extra0, cots0, rows1, extra1, cots1, sup_ref, sdown_ref, eup_ref, edown_ref,
    first_ref, second_ref, rows_s, cots_s, gate_s, dot_s, shared_s,
):
    step = pl.program_id(0)
    members = rows_s.shape[0]
    width = sup_ref.shape[0]
    base = base_ref[0].astype(f32)
    halves = ((rows0, extra0, cots0), (rows1, extra1, cots1))
    total_rows = 2 * HALF * CAP

    def block_hits(block):
        routes, places, gates = read_pairs(halves[block // HALF][1][block % HALF])
        return slot_hits(routes, places, base, members * CAP), gates

    @pl.when(step == 0)
    def _():
        for block in range(2 * HALF):
            rows_in, _, cots_in = halves[block // HALF]
            hits, gates = block_hits(block)
            hot = (hits[0] | hits[1]).astype(bf16)
            picked = mm(hot, rows_in[block % HALF], NN).astype(bf16)
            cots = mm(hot, cots_in[block % HALF], NN).astype(bf16)
            gate = slot_gates(hits, gates)
            for member in range(members):
                span = slice(member * CAP, (member + 1) * CAP)
                rows_s[member, block * CAP : (block + 1) * CAP, :] = picked[span]
                cots_s[member, block * CAP : (block + 1) * CAP, :] = cots[span]
                gate_s[member, block * CAP : (block + 1) * CAP, :] = gate[span]
        for start in range(0, len(shared_ids), 2):
            pair = shared_ids[start : start + 2]
            inputs = jnp.concatenate([halves[b // HALF][0][b % HALF] for b in pair], axis=0)
            cots = jnp.concatenate([halves[b // HALF][2][b % HALF] for b in pair], axis=0)
            value, slope = gelu_both(mm(inputs, sup_ref[...], NN))
            pre_grad = (mm(cots, sdown_ref[...], NT) * slope).astype(bf16)
            result = mm(value.astype(bf16), sdown_ref[...], NN)
            back = mm(pre_grad, sup_ref[...], NT)
            for place in range(len(pair)):
                span = slice(place * PATCHES, (place + 1) * PATCHES)
                shared_s[start + place, :, 0:width] = result[span]
                shared_s[start + place, :, width:] = back[span]

    @pl.when(step > 0)
    def _():
        member = step - 1
        tile = total_rows // 2
        for part in range(2):
            span = slice(part * tile, (part + 1) * tile)
            inputs, cots, gate = rows_s[member, span, :], cots_s[member, span, :], gate_s[member, span, :]
            value, slope = gelu_both(mm(inputs, eup_ref[0], NN))
            act_grad = mm(cots, edown_ref[0], NT)
            dot_s[member, span, :] = jnp.sum(value * act_grad, axis=1, keepdims=True)
            active = (gate * value).astype(bf16)
            pre_grad = (gate * act_grad * slope).astype(bf16)
            rows_s[member, span, :] = mm(active, edown_ref[0], NN).astype(bf16)
            cots_s[member, span, :] = mm(pre_grad, eup_ref[0], NT).astype(bf16)

    @pl.when(step == members)
    def _():
        for block in range(2 * HALF):
            out_ref = (first_ref, second_ref)[block // HALF]
            place = block % HALF
            hits, _ = block_hits(block)
            hot = (hits[0] | hits[1]).astype(bf16)
            span = slice(block * CAP, (block + 1) * CAP)
            dots = jnp.concatenate([dot_s[m, span, :] for m in range(members)], axis=0)
            sums = [jnp.sum(jnp.where(hit, dots, 0.0), axis=0, keepdims=True) for hit in hits]
            line = jnp.concatenate(sums + [jnp.zeros_like(sums[0])], axis=1)
            row_id = lax.broadcasted_iota(jnp.int32, (EXTRA, width), 0)
            out_ref[place, 2 * PATCHES :, :] = jnp.where(row_id == 0, line, 0.0).astype(bf16)
            for index, source in enumerate((rows_s, cots_s)):
                slots = jnp.concatenate([source[m, span, :] for m in range(members)], axis=0)
                total = mm(hot, slots, TN)
                if block in shared_ids:
                    where = shared_ids.index(block)
                    total = total + shared_s[where, :, index * width : (index + 1) * width]
                out_ref[place, index * PATCHES : (index + 1) * PATCHES, :] = total.astype(bf16)


def experts_both(base, blocks, shared_up, shared_down, expert_up, expert_down, shared_ids, after=()):
    members, width, hidden = expert_up.shape
    shape = (HALF, 2 * PATCHES + EXTRA, width)
    out_spec = pl.BlockSpec(shape, lambda e, b: (0, 0, 0))
    slots = (members, 2 * HALF * CAP)
    return launch(
        functools.partial(expert_kernel, shared_ids), "experts_both", [(shape, bf16)] * 2,
        [operand for part in blocks for operand in part.operands()]
        + [shared_up, shared_down, expert_up, expert_down],
        in_specs=[spec for part in blocks for spec in part.specs()]
        + [
            pl.BlockSpec((width, hidden), lambda e, b: (0, 0)),
            pl.BlockSpec((hidden, width), lambda e, b: (0, 0)),
            pl.BlockSpec((1, width, hidden), lambda e, b: (jnp.maximum(e - 1, 0), 0, 0)),
            pl.BlockSpec((1, hidden, width), lambda e, b: (jnp.maximum(e - 1, 0), 0, 0)),
        ],
        out_specs=[out_spec, out_spec],
        grid=(members + 1,),
        scalars=[base],
        after=after,
        scratch=[
            pltpu.VMEM((*slots, width), bf16),
            pltpu.VMEM((*slots, width), bf16),
            pltpu.VMEM((*slots, 1), f32),
            pltpu.VMEM((*slots, 1), f32),
            pltpu.VMEM((max(len(shared_ids), 1), PATCHES, 2 * width), f32),
        ], flops=30 * 10**9, moved=30 * 10**6,
    )


def grads_kernel(count, tile, started, low, *refs):
    row_refs, cot_refs = refs[:count], refs[count : 2 * count]
    up_ref, down_ref = refs[2 * count : 2 * count + 2]
    up_grad_ref, down_grad_ref = refs[-3:-1] if low else refs[-2:]
    width = up_ref.shape[1]
    inputs = [ref[...].reshape(-1, width) for ref in row_refs]
    cots = [ref[...].reshape(-1, width) for ref in cot_refs]
    groups = max(1, count * inputs[0].shape[0] // tile)
    each = count // groups
    for group in range(groups):
        part = slice(group * each, (group + 1) * each)
        rows, cot = jnp.concatenate(inputs[part], axis=0), jnp.concatenate(cots[part], axis=0)
        value, slope = gelu_both(mm(up_ref[0], rows, TT))
        pre_grad = (mm(down_ref[0], cot, NT) * slope).astype(bf16)
        up_grad = mm(rows, pre_grad, TT)
        down_grad = mm(value.astype(bf16), cot, NN)
        if group == 0 and started:
            up_grad_ref[0] = refs[2 * count + 2][0] + up_grad
            down_grad_ref[0] = refs[2 * count + 3][0] + down_grad
        elif group == 0:
            up_grad_ref[0] = up_grad
            down_grad_ref[0] = down_grad
        else:
            up_grad_ref[0] += up_grad
            down_grad_ref[0] += down_grad
    if low:
        refs[-1][0] = up_grad_ref[0].astype(bf16)
        refs[-1][1] = down_grad_ref[0].astype(bf16)


def weight_grads(rows, cots, specs, up, down, before, tile, total, low=False, after=(), scalars=(), span=None):
    members, width, hidden = up.shape
    start, stop = span or (0, members)
    up_spec = pl.BlockSpec((1, width, hidden), lambda e, *_: (e + start, 0, 0))
    down_spec = pl.BlockSpec((1, hidden, width), lambda e, *_: (e + start, 0, 0))
    started = before is not None
    count = len(rows)
    first = len(scalars) + 2 * count + 2
    low_spec = [pl.BlockSpec((2, width, hidden), lambda *_: (0, 0, 0))] if low else []
    kernel = functools.partial(grads_kernel, count, tile, started, low)
    return launch(
        (lambda place_ref, *refs: kernel(*refs)) if scalars else kernel, "weight_grads",
        [(up.shape, f32), (down.shape, f32)] + ([((2, width, hidden), bf16)] if low else []),
        [*rows, *cots, up, down, *(before or ())],
        in_specs=specs + [up_spec, down_spec] * (2 if started else 1), out_specs=[up_spec, down_spec] + low_spec,
        grid=(stop - start,), aliases={first: 0, first + 1: 1} if started else None, after=after, scalars=scalars,
        flops=12 * total * width * hidden, moved=total * width * 4,
    )


def routed_grads(slots, up, down, before, after=(), span=None):
    members, count, width = slots[0][0].shape
    start, stop = span or (0, members)
    spec = pl.BlockSpec((1, count, width), lambda e: (e + start, 0, 0))
    rows, cots = [pair[0] for pair in slots], [pair[1] for pair in slots]
    specs = [spec] * (2 * len(slots))
    each = len(slots) * count
    return weight_grads(
        rows, cots, specs, up, down, before, each, (stop - start) * each, after=after, span=span
    )


def shared_grads(blocks, taken, up, down, before, after=()):
    rows, cots = [part.rows for part in blocks], [part.cots for part in blocks]
    all_specs = [part.specs(taken) for part in blocks]
    specs = [spec[0] for spec in all_specs] + [spec[2] for spec in all_specs]
    total = len(blocks) * taken * PATCHES
    tile = total if total <= 8 * PATCHES else total // 2
    return weight_grads(rows, cots, specs, up[None], down[None], before, tile, total, after=after)


def shared_grads_hops(place, ext, cots, up, down, before, after=()):
    planes, blocks, _, width = ext.shape
    taken = blocks // 2
    specs = [
        pl.BlockSpec((1, taken, PATCHES, width), lambda e, p, hop=hop: (plane_of(hop, p, planes), p[1], 0, 0))
        for hop in range(planes - 1)
    ]
    total = (planes - 1) * taken * PATCHES
    return weight_grads(
        [ext] * len(specs), [cots] * len(specs), specs * 2, up[None], down[None], before, taken * PATCHES, total, True,
        after, [place],
    )


def shared_last_kernel(up, down, more, up_out, down_out):
    up_out[...] = up[0] + more[0].astype(f32)
    down_out[...] = down[0] + more[1].astype(f32)


def backward_kernel(
    local_width, moe_ref, moe_more_ref, back_ref, back_more_ref, cond_ref, tok_ref, cot_ref, mod_ref, router_ref, pairs_ref, attn_in_ref,
    qkv_ref, context_ref, attn_out_ref, ext_ref, w0, w1, w2, w3,
    output_ref, tok_grad_ref, small_ref, near_ref, far_ref, grad_s,
):
    def put_weight_grad(first, grad):
        for index in range(len(shards)):
            out_ref = (near_ref, far_ref)[index % 2]
            out_ref[index // 2, first : first + local_width, :] = grad[
                index * local_width : (index + 1) * local_width
            ]

    shards = (w0, w1, w2, w3)
    rows, width = tok_ref.shape
    mod = mod_ref[...]
    stream = tok_ref[...].astype(f32)
    attn_out = attn_out_ref[...]
    residual = stream + mod[2:3] * attn_out
    second_norm, second_inv = normalize(residual)
    moe_out = moe_ref[...] + moe_more_ref[...].astype(f32)
    back = back_ref[...] + back_more_ref[...].astype(f32)
    upstream = cot_ref[...].astype(f32)
    output_ref[...] = (residual + mod[5:6] * moe_out).astype(bf16)
    gate_two_grad = jnp.sum(upstream * moe_out, axis=0, keepdims=True)
    routes, places, gates = read_pairs(ext_ref[rows:, :])
    dots = (back[rows : rows + 1, 0:PATCHES], back[rows : rows + 1, PATCHES : 2 * PATCHES])
    mean_dot = gates[0] * dots[0] + gates[1] * dots[1]
    pairs = pairs_ref[...]
    expert_id = lax.broadcasted_iota(jnp.int32, (EXPERTS, rows), 0)
    logits_grad = jnp.zeros((EXPERTS, rows), f32)
    for k in range(TOPK):
        logits_grad += jnp.where(expert_id == pairs[k : k + 1], gates[k] * (dots[k] - mean_dot), 0.0)
    logits_grad = logits_grad.astype(bf16)
    moe_in_grad = back[0:rows] + mm(logits_grad, router_ref[...], TN)
    shift_two_grad = jnp.sum(moe_in_grad, axis=0, keepdims=True)
    scale_two_grad = jnp.sum(moe_in_grad * second_norm, axis=0, keepdims=True)
    residual_grad = upstream + normalize_back(
        second_norm, second_inv, moe_in_grad * (1.0 + mod[4:5])
    )
    gate_one_grad = jnp.sum(residual_grad * attn_out, axis=0, keepdims=True)
    attn_grad = (mod[2:3] * residual_grad).astype(bf16)
    out_grad = mm(context_ref[...], attn_grad, TN).astype(bf16)
    put_weight_grad(3 * local_width, out_grad)
    context_grad = mm(attn_grad, shard_rows(shards, 3, local_width), NT).astype(bf16)
    masks = pair_masks(rows)
    zero = jnp.zeros((rows, 2 * HD), bf16)
    scale = 1.0 / math.sqrt(HD)
    for pair in range(width // (2 * HD)):
        cols = slice(pair * 2 * HD, (pair + 1) * 2 * HD)
        query, key, value = qkv_ref[0, :, cols], qkv_ref[1, :, cols], qkv_ref[2, :, cols]
        upper = context_grad[:, cols]
        sums = []
        for mask in masks:
            probs = head_probs(jnp.where(mask, query, zero), key)
            probs_grad = mm(jnp.where(mask, upper, zero), value, NT)
            value_grad = mm(probs.astype(bf16), upper, TN)
            score_grad = (
                probs * (probs_grad - jnp.sum(probs_grad * probs, axis=-1, keepdims=True))
            ).astype(bf16)
            sums.append((mm(score_grad, key, NN) * scale, mm(score_grad, query, TN) * scale, value_grad))
        for part in range(3):
            grad_s[part, :, cols] = jnp.where(masks[0], sums[0][part], sums[1][part]).astype(bf16)
    attn_in = attn_in_ref[...]
    attn_in_grad = jnp.zeros((rows, width), f32)
    for part in range(3):
        grad = grad_s[part]
        attn_in_grad += mm(grad, shard_rows(shards, part, local_width), NN)
        put_weight_grad(part * local_width, mm(grad, attn_in, TN).astype(bf16))
    first_norm, first_inv = normalize(stream)
    shift_one_grad = jnp.sum(attn_in_grad, axis=0, keepdims=True)
    scale_one_grad = jnp.sum(attn_in_grad * first_norm, axis=0, keepdims=True)
    tok_grad_ref[...] = residual_grad + normalize_back(
        first_norm, first_inv, attn_in_grad * (1.0 + mod[1:2])
    )
    lines = (
        shift_one_grad, scale_one_grad, gate_one_grad, shift_two_grad, scale_two_grad, gate_two_grad,
        cond_ref[...],
    )
    row_id = lax.broadcasted_iota(jnp.int32, (8, width), 0)
    stacked = jnp.zeros((8, width), f32)
    for index, line in enumerate(lines):
        stacked = jnp.where(row_id == index, line, stacked)
    small_ref[0:8, :] = stacked
    small_ref[8:16, :] = mm(logits_grad, ext_ref[0:rows, :], NN)


def attention_backward(
    moe, moe_more, back, back_more, cond, tokens, cotangent, mod, router_t, pairs, attn_in, qkv, context,
    attn_out, ext, shards, local_width, after=(),
):
    rows, width = tokens.shape
    halves = ((len(shards) // 2, 4 * local_width, width), bf16)
    return launch(
        functools.partial(backward_kernel, local_width), "attention_backward",
        [((rows, width), bf16), ((rows, width), f32), ((16, width), f32), halves, halves],
        [
            moe, moe_more, back, back_more, cond, tokens, cotangent, mod, router_t, pairs, attn_in, qkv,
            context, attn_out, ext, *shards,
        ],
        scratch=[pltpu.VMEM((3, rows, width), bf16)], after=after, flops=10 * 10**9, moved=16 * 10**6,
    )


def plane_first_kernel(first, more, side, other, keep_upper, keep_lower):
    cut = PATCHES
    upper = lambda block: first[block, 0:cut, :].astype(f32) + more[block, 0:cut, :].astype(f32)
    lower = lambda block: first[block, cut:, :].astype(f32) + more[block, cut:, :].astype(f32)
    side[0], side[1] = upper(1).astype(bf16), upper(3).astype(bf16)
    other[0], other[1] = lower(2).astype(bf16), lower(3).astype(bf16)
    keep_upper[0], keep_upper[1] = upper(0), upper(2)
    keep_lower[0], keep_lower[1] = lower(0), lower(1)


def plane_second_kernel(keep_upper, keep_lower, side, other, upper, lower, upper_next, lower_next):
    upper[...] = keep_upper[0] + side[0].astype(f32)
    upper_next[...] = (keep_upper[1] + side[1].astype(f32)).astype(bf16)
    lower[...] = keep_lower[0] + other[0].astype(f32)
    lower_next[...] = (keep_lower[1] + other[1].astype(f32)).astype(bf16)


def span_of(index, size):
    return pl.ds(pl.multiple_of(index * size, size), size)


def dense_first_kernel(place, near, more, side, other, keep_upper, keep_lower):
    cut = near.shape[1] // 2
    half = cut // 2
    mine = place[0]
    side[...] = (near[1, 0:cut, :].astype(f32) + more[1, 0:cut, :].astype(f32)).astype(bf16)
    keep_upper[...] = near[0, 0:cut, :].astype(f32) + more[0, 0:cut, :].astype(f32)
    for index in range(2):
        for out, who in ((keep_lower, mine), (other, 1 - mine)):
            rows = pl.ds(pl.multiple_of(cut + who * half, half), half)
            total = near[index, rows, :].astype(f32) + more[index, rows, :].astype(f32)
            out[index] = total.astype(out.dtype)


def dense_second_kernel(place, keep_upper, keep_lower, from_side, from_other, side, other, upper, lower):
    half = upper.shape[0]
    mine = place[0]
    for out, who in ((upper, mine), (other, 1 - mine)):
        rows = span_of(who, half)
        out[...] = (keep_upper[rows, :] + from_side[rows, :].astype(f32)).astype(out.dtype)
    lower[...] = keep_lower[0] + from_other[0].astype(f32)
    side[...] = (keep_lower[1] + from_other[1].astype(f32)).astype(bf16)


def dense_third_kernel(size, place, upper, lower, from_side, from_other, own, *outs):
    sent, total = outs[:-1], outs[-1]
    half = upper.shape[0]
    share = 2 * half // size
    total[0:half, :] = upper[...] + from_other[...].astype(f32)
    total[half:, :] = lower[...] + from_side[...].astype(f32)
    own[...] = total[span_of(place[1], share), :]
    for hop in range(1, size):
        sent[hop - 1][...] = total[span_of(lax.rem(place[1] + hop, size), share), :].astype(bf16)


def dense_fourth_kernel(own, *refs):
    out = refs[-1]
    total = own[...]
    for ref in refs[:-1]:
        total = total + ref[...].astype(f32)
    out[...] = total.astype(bf16)


def dense_fifth_kernel(size, place, own, *refs):
    out = refs[-1]
    share = own.shape[0]
    out[span_of(place[1], share), :] = own[...]
    for hop in range(1, size):
        out[span_of(lax.rem(place[1] + size - hop, size), share), :] = refs[hop - 1][...]


def dense_last_kernel(place, own, more, qkv_out, out_out, total):
    half = own.shape[0] // 2
    for ref, who in ((own, place[0]), (more, 1 - place[0])):
        for index in range(2):
            rows = pl.ds(pl.multiple_of(2 * half * index + who * half, half), half)
            total[rows, :] = ref[index * half : (index + 1) * half, :].astype(f32)
    count = qkv_out.shape[0]
    qkv_out[...] = total[0:count, :]
    out_out[...] = total[count:, :]


class Links:
    def __init__(self, mesh):
        self.dp, self.expert, self.tensor = (mesh.shape[name] for name in ("dp", "expert", "tensor"))
        self.paired = self.expert == 2 and self.tensor == 4
        self.core = [(i, i ^ 1) for i in range(self.tensor)]
        self.side = [(i, i ^ 2) for i in range(self.tensor)]
        self.other = [(0, 1), (1, 0)]

    def to_core(self, value):
        return lax.ppermute(value, "tensor", self.core)

    def to_side(self, value):
        return lax.ppermute(value, "tensor", self.side)

    def to_other(self, value):
        return lax.ppermute(value, "expert", self.other)

    def along(self, value, hop):
        return lax.ppermute(value, "dp", [(i, (i + hop) % self.dp) for i in range(self.dp)])

    def plane_sum_first(self, first, more, after):
        width = first.shape[2]
        low = first.shape[1] - PATCHES
        return launch(
            plane_first_kernel, "plane_first",
            [((2, PATCHES, width), bf16), ((2, low, width), bf16), ((2, PATCHES, width), f32), ((2, low, width), f32)],
            [first, more], after=after, moved=10 * 10**6,
        )

    def plane_sum_second(self, keep_upper, keep_lower, side, other, after):
        _, low, width = keep_lower.shape
        return launch(
            plane_second_kernel, "plane_second",
            [((PATCHES, width), f32), ((low, width), f32), ((PATCHES, width), bf16), ((low, width), bf16)],
            [keep_upper, keep_lower, side, other], after=after, moved=6 * 10**6,
        )

    def dense_sum(self, near, far):
        _, rows, width = near.shape
        cut, half, share = rows // 2, rows // 4, rows // 2 // self.dp
        place = [jnp.stack([lax.axis_index("expert"), lax.axis_index("dp")]).astype(jnp.int32)]
        more = self.to_core(far)
        after = yield None
        side, other, keep_upper, keep_lower = launch(
            dense_first_kernel, "dense_first",
            [((cut, width), bf16), ((2, half, width), bf16), ((cut, width), f32), ((2, half, width), f32)],
            [near, more], scalars=place, after=after, moved=8 * 10**6,
        )
        from_side, from_other = self.to_side(side), self.to_other(other)
        after = yield keep_upper
        side, other, upper, lower = launch(
            dense_second_kernel, "dense_second",
            [((half, width), bf16), ((half, width), bf16), ((half, width), f32), ((half, width), f32)],
            [keep_upper, keep_lower, from_side, from_other], scalars=place, after=after, moved=5 * 10**6,
        )
        from_side, from_other = self.to_side(side), self.to_other(other)
        after = yield upper
        hops = range(1, self.dp)
        outs = launch(
            functools.partial(dense_third_kernel, self.dp), "dense_third",
            [((share, width), f32)] + [((share, width), bf16)] * len(hops),
            [upper, lower, from_side, from_other], scalars=place, scratch=[pltpu.VMEM((cut, width), f32)],
            after=after, moved=3 * 10**6,
        )
        moved = [self.along(outs[hop], hop) for hop in hops]
        after = yield outs[0]
        (total,) = launch(
            dense_fourth_kernel, "dense_fourth", [((share, width), bf16)], [outs[0], *moved], after=after,
            moved=10**6,
        )
        moved = [self.along(total, hop) for hop in hops]
        after = yield total
        (column,) = launch(
            functools.partial(dense_fifth_kernel, self.dp), "dense_fifth", [((cut, width), bf16)], [total, *moved],
            scalars=place, after=after, moved=10**6,
        )
        more = self.to_other(column)
        after = yield column
        yield launch(
            dense_last_kernel, "dense_last", [((rows * 3 // 4, width), f32), ((rows // 4, width), f32)],
            [column, more], scalars=place, scratch=[pltpu.VMEM((rows, width), f32)], after=after,
            moved=4 * 10**6,
        )


def local(
    links,
    tokens,
    cotangent,
    timesteps,
    ada_weight,
    ada_bias,
    qkv_weight,
    out_weight,
    router_weight,
    shared_up,
    shared_down,
    expert_up,
    expert_down,
    routes,
    places,
):
    rows, width = tokens.shape
    local_width = qkv_weight.shape[2]
    members = expert_up.shape[0]
    me = lax.axis_index("tensor")
    base = (lax.axis_index("expert") * members).astype(jnp.int32).reshape(1)
    everyone = ("dp", "expert", "tensor")
    total_blocks = links.dp * links.expert * links.tensor
    full = links.paired and total_blocks * rows * width * 2 <= FULL_LIMIT

    condition = jax.nn.silu(embedding(timesteps, width)).astype(bf16)
    mod_cols = jnp.einsum("id,dcf->icf", condition, ada_weight, preferred_element_type=f32) + ada_bias[None]
    mod = lax.all_to_all(mod_cols, "tensor", split_axis=0, concat_axis=2, tiled=True)[0]
    own_condition = lax.dynamic_slice_in_dim(condition.astype(f32), me, 1, axis=0)
    shared_cot = (mod[5][None] * cotangent.astype(f32)).astype(bf16)

    weight = jnp.concatenate(
        [qkv_weight.transpose(1, 2, 0).reshape(3 * local_width, width), out_weight], axis=0
    )
    across = links.to_side(weight)
    near_shard = links.to_core(weight)
    (across,) = ordered([across], [mod])
    shards = (weight, near_shard, across, links.to_core(across))
    router_t = router_weight.T
    pairs = jnp.concatenate([routes.T, places.T], axis=0)

    attn_in, qkv, context, attn_out, ext = attention_forward(
        tokens, mod, router_t, pairs, shards, local_width
    )
    feed = (shared_up, shared_down, expert_up, expert_down)
    backward = functools.partial(
        attention_backward, cond=own_condition, tokens=tokens, cotangent=cotangent, mod=mod, router_t=router_t,
        pairs=pairs, attn_in=attn_in, qkv=qkv, context=context, attn_out=attn_out, ext=ext, shards=shards,
        local_width=local_width,
    )
    whole = slice(None)
    if full:
        place = jnp.stack([base[0], *(lax.axis_index(axis) for axis in ("expert", "dp"))]).astype(jnp.int32)
        cots = lax.all_gather(shared_cot, everyone, axis=0)
        cot_side, cot_other = links.to_side(shared_cot), links.to_other(shared_cot)
        ext_side, ext_other = links.to_side(ext), links.to_other(ext)
        everything = lax.all_gather(ext, everyone, axis=0)
        cut = PATCHES // 2 + EXTRA
        ext_corner = (links.to_side(ext_other[:cut]), links.to_other(ext_side[cut:]))
        cot_corner = links.to_other(ordered([cot_side], [ext])[0])
        cot_mine = assemble(
            (HALF, PATCHES, width), bf16, [shared_cot, cot_side, cot_other, cot_corner],
            [(index, whole, index) for index in range(HALF)], after=[ext_side],
        )
        cot_near = links.to_core(cot_mine)
        ext_mine = assemble(
            (HALF, PATCHES + EXTRA, width), bf16, [ext, ext_side, ext_other, *ext_corner],
            [(index, whole, index) for index in range(3)]
            + [(3, whole, (3, pl.ds(0, cut))), (4, whole, (3, pl.ds(cut, PATCHES // 2)))],
        )
        ext_near = links.to_core(ext_mine)
        own = (Blocks.apart(ext_mine, cot_mine), Blocks.apart(ext_near, cot_near))
        first, second = experts_both(base, own, *feed, (0, 1, 4, 5))
        moved = links.to_core(second)
        slots = dispatch(base, own, members, after=[first])
        side, other, keep_upper, keep_lower = links.plane_sum_first(first, moved, after=[slots[0]])
        from_side, from_other = links.to_side(side), links.to_other(other)
        routed = routed_grads([slots], expert_up, expert_down, None, after=[side])
        upper, lower, upper_next, lower_next = links.plane_sum_second(
            keep_upper, keep_lower, from_side, from_other, after=[routed[0]]
        )
        upper_more, lower_more = links.to_other(upper_next), links.to_side(lower_next)
        shared = shared_grads(own, 2, shared_up, shared_down, None, after=[upper])
        output, tokens_grad, small, near, far = backward(
            upper, upper_more, lower, lower_more, after=[shared[0]]
        )
        dense = links.dense_sum(near, far)
        next(dense)
        small_all = lax.all_gather(small, everyone, axis=0)
        everything, cots = ordered([everything, cots], [small])
        everything, cots = (
            value.reshape(links.dp, links.expert * links.tensor, *value.shape[1:]) for value in (everything, cots)
        )
        slots = dispatch_hops(place, everything, cots, members)
        step = dense.send([slots[0]])
        *shared, sent = shared_grads_hops(place, everything, cots, shared_up, shared_down, shared, after=[step])
        step = dense.send([sent])
        middle = members // 2
        routed = routed_grads([slots], expert_up, expert_down, routed, after=[step], span=(0, middle))
        step = dense.send([routed[0]])
        shared_more = links.to_other(ordered([sent], [step])[0])
        routed = routed_grads([slots], expert_up, expert_down, routed, after=[step], span=(middle, members))
        step = dense.send([routed[0]])
        step = dense.send([step])
        shared = launch(
            shared_last_kernel, "shared_last", [(shared_up.shape, f32), (shared_down.shape, f32)],
            [*shared, shared_more], after=[step], moved=12 * 10**6,
        )
        qkv_grad, out_grad = dense.send([shared[0]])
        (small_all,) = ordered([small_all], [routed[0]])
        routes_all = everything[:, :, PATCHES, : TOPK * PATCHES].reshape(-1, TOPK * PATCHES)
    else:
        shift = lax.axis_index("expert") * links.tensor
        gather = lambda block: jnp.roll(
            lax.all_gather(block, ("expert", "tensor"), axis=0), -shift, axis=0
        )
        all_ext, all_cot = gather(ext), gather(shared_cot)
        planes, sums = [], []
        for start in range(0, links.expert * links.tensor, 2 * HALF):
            spans = [slice(start + HALF * part, start + HALF * (part + 1)) for part in range(2)]
            planes.append(tuple(Blocks.apart(all_ext[span], all_cot[span]) for span in spans))
            shared_ids = tuple(range(links.tensor)) if start == 0 else ()
            sums += experts_both(base, planes[-1], *feed, shared_ids)
        blocks = jnp.roll(jnp.concatenate(sums, axis=0), shift, axis=0)
        total = lax.psum_scatter(blocks, ("expert", "tensor"), scatter_dimension=0, tiled=True)[0]
        upper, lower = total[:PATCHES].astype(f32), total[PATCHES:].astype(f32)
        output, tokens_grad, small, near, far = backward(
            upper, jnp.zeros_like(total[:PATCHES]), lower, jnp.zeros_like(total[PATCHES:])
        )
        small_all = lax.all_gather(small, everyone, axis=0)
        slots = [dispatch(base, plane, members) for plane in planes]
        routed = None
        for start in range(0, len(planes), 2):
            routed = routed_grads(slots[start : start + 2], expert_up, expert_down, routed)
        shared = shared_grads(planes[0][:1], HALF, shared_up, shared_down, None)
        routed = lax.psum(routed, "dp")
        shared = lax.psum(tuple(part[0] for part in shared), ("dp", "expert"))
        routes_all = lax.all_gather(routes.reshape(-1), everyone, axis=0)
        turn = jnp.arange(links.tensor) ^ me
        grads = jnp.stack([near, far], axis=1).reshape((-1,) + near.shape[1:])[turn]
        dense = lax.psum_scatter(grads, "tensor", scatter_dimension=0, tiled=True)[0]
        dense = lax.psum(dense, ("dp", "expert")).astype(f32)
        qkv_grad, out_grad = dense[: 3 * local_width], dense[3 * local_width :]

    condition_all = small_all[:, 6].astype(bf16)
    mod_grad = lax.dynamic_slice_in_dim(small_all[:, 0:6], me * local_width, local_width, axis=2)
    ada_grad = jnp.einsum(
        "id,icf->dcf", condition_all.astype(f32), mod_grad, precision=lax.Precision.HIGHEST
    )
    ada_bias_grad = jnp.sum(mod_grad, axis=0)
    router_grad = jnp.sum(small_all[:, 8:16], axis=0).T
    counts = jnp.sum(
        (routes_all[:, :, None] == jnp.arange(EXPERTS).astype(routes_all.dtype)).astype(jnp.int32),
        axis=(0, 1),
    )
    qkv_grad = qkv_grad.reshape(3, local_width, width).transpose(2, 0, 1)
    return (
        output,
        tokens_grad,
        ada_grad,
        ada_bias_grad,
        qkv_grad,
        out_grad,
        router_grad,
        shared[0],
        shared[1],
        routed[0],
        routed[1],
        counts,
    )


def solution(mesh):
    rows = P(("dp", "expert", "tensor"), None)
    placed = (
        rows,
        rows,
        P(("dp", "expert")),
        P(None, None, "tensor"),
        P(None, "tensor"),
        P(None, None, "tensor"),
        P("tensor", None),
        P(),
        P(None, "tensor"),
        P("tensor", None),
        P("expert", None, "tensor"),
        P("expert", "tensor", None),
        rows,
        rows,
    )
    return jax.shard_map(
        functools.partial(local, Links(mesh)),
        mesh=mesh,
        in_specs=placed,
        out_specs=(
            rows,
            rows,
            P(None, None, "tensor"),
            P(None, "tensor"),
            P(None, None, "tensor"),
            P("tensor", None),
            P(),
            P(None, "tensor"),
            P("tensor", None),
            P("expert", None, "tensor"),
            P("expert", "tensor", None),
            P(),
        ),
        check_vma=False,
    )
```

```python
import functools
import math

import jax
import jax.numpy as jnp
from jax import lax
from jax.experimental import pallas as pl
from jax.experimental.pallas import tpu as pltpu
from jax.sharding import PartitionSpec as P

HD = 64
EXPERTS = 8
TOPK = 2
PATCHES = 256
CAP = 80
EXTRA = 16
EPSILON = 1e-06
HALF = 4
FULL_LIMIT = 32 * 1024 * 1024
VMEM_LIMIT = 58 * 1024 * 1024

f32 = jnp.float32
bf16 = jnp.bfloat16
NN = (((1,), (0,)), ((), ()))
NT = (((1,), (1,)), ((), ()))
TN = (((0,), (0,)), ((), ()))
TT = (((0,), (1,)), ((), ()))


def mm(left, right, dims):
    return lax.dot_general(left, right, dims, preferred_element_type=f32)


def normalize(values):
    center = jnp.mean(values, axis=-1, keepdims=True)
    shifted = values - center
    inverse = lax.rsqrt(jnp.mean(shifted * shifted, axis=-1, keepdims=True) + EPSILON)
    return (shifted * inverse, inverse)


def normalize_back(normed, inverse, upstream):
    return inverse * (
        upstream
        - jnp.mean(upstream, axis=-1, keepdims=True)
        - normed * jnp.mean(upstream * normed, axis=-1, keepdims=True)
    )


def embedding(steps, model_width):
    half_width = model_width // 2
    freqs_all = jnp.exp(-math.log(10000.0) * jnp.arange(half_width, dtype=f32) / half_width)
    angles = steps.astype(f32)[:, None] * freqs_all[None, :]
    return jnp.concatenate([jnp.cos(angles), jnp.sin(angles)], axis=1)


def gelu_both(pre):
    const = math.sqrt(2.0 / math.pi)
    square = pre * pre
    tanh = jnp.tanh(const * pre * (1.0 + 0.044715 * square))
    half = 0.5 + 0.5 * tanh
    value = pre * half
    return value, half + value * (1.0 - tanh) * (const + 3.0 * 0.044715 * const * square)


def launch(
    kernel, name, outs, operands, *, in_specs=None, out_specs=None, grid=(), scalars=(), scratch=(), aliases=None,
    after=(), flops=0, moved=0,
):
    lead = len(scalars)
    count = lead + len(operands)
    waits = len(after)
    on_chip = pl.BlockSpec(memory_space=pltpu.VMEM)
    anywhere = pl.BlockSpec(memory_space=pl.ANY)
    in_specs = list(in_specs or [on_chip] * len(operands)) + [anywhere] * waits
    out_specs = tuple(out_specs or [on_chip] * len(outs))

    def body(*refs):
        kernel(*refs[:count], *refs[count + waits :])

    if scalars and grid:
        shape = dict(
            grid_spec=pltpu.PrefetchScalarGridSpec(
                num_scalar_prefetch=lead, grid=grid, in_specs=in_specs, out_specs=out_specs, scratch_shapes=scratch
            )
        )
    else:
        in_specs = [pl.BlockSpec(memory_space=pltpu.SMEM)] * lead + in_specs
        shape = dict(grid=grid, in_specs=in_specs, out_specs=out_specs, scratch_shapes=scratch)
    return pl.pallas_call(
        body,
        out_shape=tuple(jax.ShapeDtypeStruct(*out) for out in outs),
        input_output_aliases=aliases or {},
        compiler_params=pltpu.CompilerParams(vmem_limit_bytes=VMEM_LIMIT),
        cost_estimate=pl.CostEstimate(flops=int(flops), bytes_accessed=int(moved), transcendentals=0),
        name=name,
        **shape,
    )(*scalars, *operands, *after)


def copy_kernel(plan, count, *refs):
    sources, out, sems = refs[:count], refs[-2], refs[-1]
    copies = [
        pltpu.make_async_copy(sources[index].at[take], out.at[put], sems.at[order])
        for order, (index, take, put) in enumerate(plan)
    ]
    for copy in copies:
        copy.start()
    for copy in copies:
        copy.wait()


def assemble(shape, dtype, sources, plan, after=()):
    size = math.prod(shape) * jnp.dtype(dtype).itemsize
    return launch(
        functools.partial(copy_kernel, plan, len(sources)), "assemble", [(shape, dtype)], sources,
        in_specs=[pl.BlockSpec(memory_space=pl.ANY)] * len(sources),
        scratch=[pltpu.SemaphoreType.DMA((len(plan),))], after=after, moved=2 * size,
    )[0]


def order_kernel(*refs):
    pass


def ordered(values, after):
    anywhere = [pl.BlockSpec(memory_space=pl.ANY)] * len(values)
    return launch(
        order_kernel, "ordered", [(value.shape, value.dtype) for value in values], values, in_specs=anywhere,
        out_specs=anywhere, aliases={index: index for index in range(len(values))}, after=after,
    )


def pair_masks(rows):
    lane = lax.broadcasted_iota(jnp.int32, (rows, 2 * HD), 1)
    return (lane < HD, lane >= HD)


def head_probs(query, key):
    scores = mm(query, key, NT) * (1.0 / math.sqrt(HD))
    weights = jnp.exp(scores - jnp.max(scores, axis=-1, keepdims=True))
    return weights / jnp.sum(weights, axis=-1, keepdims=True)


def shard_rows(shards, part, local_width):
    return jnp.concatenate(
        [shard[part * local_width : (part + 1) * local_width, :] for shard in shards], axis=0
    )


def attention_kernel(
    local_width, tok_ref, mod_ref, router_ref, pairs_ref, w0, w1, w2, w3,
    attn_in_ref, qkv_ref, context_ref, attn_out_ref, ext_ref,
):
    shards = (w0, w1, w2, w3)
    rows, width = tok_ref.shape
    mod = mod_ref[...]
    stream = tok_ref[...].astype(f32)
    attn_in = (normalize(stream)[0] * (1.0 + mod[1:2]) + mod[0:1]).astype(bf16)
    attn_in_ref[...] = attn_in
    for part in range(3):
        qkv_ref[part] = mm(attn_in, shard_rows(shards, part, local_width), NT).astype(bf16)
    masks = pair_masks(rows)
    zero = jnp.zeros((rows, 2 * HD), bf16)
    for pair in range(width // (2 * HD)):
        cols = slice(pair * 2 * HD, (pair + 1) * 2 * HD)
        query, key, value = qkv_ref[0, :, cols], qkv_ref[1, :, cols], qkv_ref[2, :, cols]
        parts = []
        for mask in masks:
            probs = head_probs(jnp.where(mask, query, zero), key)
            parts.append(mm(probs.astype(bf16), value, NN))
        context_ref[:, cols] = jnp.where(masks[0], parts[0], parts[1]).astype(bf16)
    attn_out = mm(context_ref[...], shard_rows(shards, 3, local_width), NN)
    attn_out_ref[...] = attn_out
    residual = stream + mod[2:3] * attn_out
    moe_in = (normalize(residual)[0] * (1.0 + mod[4:5]) + mod[3:4]).astype(bf16)
    ext_ref[0:rows, :] = moe_in
    logits = mm(router_ref[...], moe_in, NT)
    pairs = pairs_ref[...]
    expert_id = lax.broadcasted_iota(jnp.int32, (EXPERTS, rows), 0)
    chosen = [
        jnp.sum(jnp.where(expert_id == pairs[k : k + 1], logits, 0.0), axis=0, keepdims=True)
        for k in range(TOPK)
    ]
    top = jnp.maximum(chosen[0], chosen[1])
    powers = [jnp.exp(value - top) for value in chosen]
    gates = [power / (powers[0] + powers[1]) for power in powers]
    high = [gate.astype(bf16).astype(f32) for gate in gates]
    rest = [gate - upper for gate, upper in zip(gates, high)]
    values = pairs.astype(f32)
    packed = (
        jnp.concatenate([values[0:1], values[1:2], values[2:3]], axis=1),
        jnp.concatenate([values[3:4], high[0], high[1]], axis=1),
        jnp.concatenate([rest[0], rest[1], jnp.zeros_like(rest[0])], axis=1),
    )
    row_id = lax.broadcasted_iota(jnp.int32, (EXTRA, width), 0)
    extra = jnp.zeros((EXTRA, width), f32)
    for index, line in enumerate(packed):
        extra = jnp.where(row_id == index, line, extra)
    ext_ref[rows : rows + EXTRA, :] = extra.astype(bf16)


def attention_forward(tokens, mod, router_t, pairs, shards, local_width):
    rows, width = tokens.shape
    outs = [
        ((rows, width), bf16),
        ((3, rows, width), bf16),
        ((rows, width), bf16),
        ((rows, width), f32),
        ((rows + EXTRA, width), bf16),
    ]
    return launch(
        functools.partial(attention_kernel, local_width), "attention_forward", outs,
        [tokens, mod, router_t, pairs, *shards], flops=5 * 10**9, moved=9 * 10**6,
    )


def read_pairs(extra):
    info = extra.astype(f32)
    count = PATCHES
    routes = (info[0:1, 0:count], info[0:1, count : 2 * count])
    places = (info[0:1, 2 * count : 3 * count], info[1:2, 0:count])
    gates = (
        info[1:2, count : 2 * count] + info[2:3, 0:count],
        info[1:2, 2 * count : 3 * count] + info[2:3, count : 2 * count],
    )
    return routes, places, gates


def slot_hits(routes, places, base, slots):
    slot_id = lax.broadcasted_iota(jnp.int32, (slots, PATCHES), 0).astype(f32)
    return [
        slot_id == jnp.where(place < CAP, (route - base) * CAP + place, -1.0)
        for route, place in zip(routes, places)
    ]


def slot_gates(hits, gates):
    return jnp.sum(
        jnp.where(hits[0], gates[0], 0.0) + jnp.where(hits[1], gates[1], 0.0), axis=1, keepdims=True
    )


class Blocks:
    def __init__(self, rows, rows_at, extra_at, cots, cots_at):
        self.rows, self.rows_at, self.extra_at, self.cots, self.cots_at = rows, rows_at, extra_at, cots, cots_at

    @classmethod
    def apart(cls, ext, cots):
        return cls(ext, 0, PATCHES // EXTRA, cots, 0)

    def operands(self):
        return [self.rows, self.rows, self.cots]

    def specs(self, taken=HALF):
        width = self.rows.shape[2]
        places = ((PATCHES, self.rows_at), (EXTRA, self.extra_at), (PATCHES, self.cots_at))
        return [
            pl.BlockSpec((taken, count, width), lambda *_, at=at: (0, at, 0)) for count, at in places
        ]

    def extra(self):
        return self.rows[:, self.extra_at * EXTRA : (self.extra_at + 1) * EXTRA]


def dispatch_kernel(base_ref, *refs):
    rows_ref, cots_ref = refs[-2:]
    members = rows_ref.shape[0]
    base = base_ref[0].astype(f32)
    for part in range(2):
        rows_in, extra_in, cots_in = refs[3 * part : 3 * part + 3]

        @pl.when(pl.program_id(0) == part)
        def _():
            for block in range(HALF):
                dispatch_block(
                    base, members, rows_in[block], extra_in[block], cots_in[block], rows_ref, cots_ref, block
                )


def dispatch_block(base, members, rows, extra, cots, rows_ref, cots_ref, block):
    routes, places, gates = read_pairs(extra)
    hits = slot_hits(routes, places, base, members * CAP)
    hot = (hits[0] | hits[1]).astype(bf16)
    picked = mm(hot, rows, NN).astype(bf16)
    scaled = (mm(hot, cots, NN) * slot_gates(hits, gates)).astype(bf16)
    for member in range(members):
        span = slice(member * CAP, (member + 1) * CAP)
        rows_ref[member, block * CAP : (block + 1) * CAP, :] = picked[span]
        cots_ref[member, block * CAP : (block + 1) * CAP, :] = scaled[span]


def hops_kernel(base_ref, ext, cots, rows_ref, cots_ref):
    base = base_ref[0].astype(f32)
    for block in range(ext.shape[0]):
        dispatch_block(
            base, rows_ref.shape[0], ext[block, 0, :PATCHES], ext[block, 0, PATCHES:], cots[block, 0], rows_ref,
            cots_ref, block,
        )


def dispatch_hops(base, ext, cots, members, after=()):
    blocks, hops, rows, width = ext.shape
    out = ((members, hops * blocks * CAP, width), bf16)
    out_spec = pl.BlockSpec((members, blocks * CAP, width), lambda h, b: (0, h, 0))
    specs = [pl.BlockSpec((blocks, 1, count, width), lambda h, b: (0, h, 0, 0)) for count in (rows, PATCHES)]
    return launch(
        hops_kernel, "dispatch_hops", [out, out], [ext, cots], in_specs=specs, out_specs=[out_spec, out_spec],
        grid=(hops,), scalars=[base], after=after, flops=24 * 10**9, moved=48 * 10**6,
    )


def pick_kernel(place_ref, source, out):
    planes = source.shape[0]
    for hop in range(planes - 1):
        out[hop] = source[lax.rem(place_ref[2] + hop + 1, planes)]


def dispatch(base, blocks, members, after=()):
    width = blocks[0].rows.shape[2]
    out = ((members, 2 * HALF * CAP, width), bf16)
    out_spec = pl.BlockSpec((members, HALF * CAP, width), lambda c, *_: (0, c, 0))
    return launch(
        dispatch_kernel, "dispatch", [out, out], [operand for part in blocks for operand in part.operands()],
        in_specs=[spec for part in blocks for spec in part.specs()], out_specs=[out_spec, out_spec],
        grid=(2,), scalars=[base], after=after, flops=8 * 10**9, moved=16 * 10**6,
    )


def expert_kernel(
    shared_ids, base_ref, rows0, extra0, cots0, rows1, extra1, cots1, sup_ref, sdown_ref, eup_ref, edown_ref,
    first_ref, second_ref, rows_s, cots_s, gate_s, dot_s, shared_s,
):
    step = pl.program_id(0)
    members = rows_s.shape[0]
    width = sup_ref.shape[0]
    base = base_ref[0].astype(f32)
    halves = ((rows0, extra0, cots0), (rows1, extra1, cots1))
    total_rows = 2 * HALF * CAP

    def block_hits(block):
        routes, places, gates = read_pairs(halves[block // HALF][1][block % HALF])
        return slot_hits(routes, places, base, members * CAP), gates

    @pl.when(step == 0)
    def _():
        for block in range(2 * HALF):
            rows_in, _, cots_in = halves[block // HALF]
            hits, gates = block_hits(block)
            hot = (hits[0] | hits[1]).astype(bf16)
            picked = mm(hot, rows_in[block % HALF], NN).astype(bf16)
            cots = mm(hot, cots_in[block % HALF], NN).astype(bf16)
            gate = slot_gates(hits, gates)
            for member in range(members):
                span = slice(member * CAP, (member + 1) * CAP)
                rows_s[member, block * CAP : (block + 1) * CAP, :] = picked[span]
                cots_s[member, block * CAP : (block + 1) * CAP, :] = cots[span]
                gate_s[member, block * CAP : (block + 1) * CAP, :] = gate[span]
        for start in range(0, len(shared_ids), 2):
            pair = shared_ids[start : start + 2]
            inputs = jnp.concatenate([halves[b // HALF][0][b % HALF] for b in pair], axis=0)
            cots = jnp.concatenate([halves[b // HALF][2][b % HALF] for b in pair], axis=0)
            value, slope = gelu_both(mm(inputs, sup_ref[...], NN))
            pre_grad = (mm(cots, sdown_ref[...], NT) * slope).astype(bf16)
            result = mm(value.astype(bf16), sdown_ref[...], NN)
            back = mm(pre_grad, sup_ref[...], NT)
            for place in range(len(pair)):
                span = slice(place * PATCHES, (place + 1) * PATCHES)
                shared_s[start + place, :, 0:width] = result[span]
                shared_s[start + place, :, width:] = back[span]

    @pl.when(step > 0)
    def _():
        member = step - 1
        tile = total_rows // 2
        for part in range(2):
            span = slice(part * tile, (part + 1) * tile)
            inputs, cots, gate = rows_s[member, span, :], cots_s[member, span, :], gate_s[member, span, :]
            value, slope = gelu_both(mm(inputs, eup_ref[0], NN))
            act_grad = mm(cots, edown_ref[0], NT)
            dot_s[member, span, :] = jnp.sum(value * act_grad, axis=1, keepdims=True)
            active = (gate * value).astype(bf16)
            pre_grad = (gate * act_grad * slope).astype(bf16)
            rows_s[member, span, :] = mm(active, edown_ref[0], NN).astype(bf16)
            cots_s[member, span, :] = mm(pre_grad, eup_ref[0], NT).astype(bf16)

    @pl.when(step == members)
    def _():
        for block in range(2 * HALF):
            out_ref = (first_ref, second_ref)[block // HALF]
            place = block % HALF
            hits, _ = block_hits(block)
            hot = (hits[0] | hits[1]).astype(bf16)
            span = slice(block * CAP, (block + 1) * CAP)
            dots = jnp.concatenate([dot_s[m, span, :] for m in range(members)], axis=0)
            sums = [jnp.sum(jnp.where(hit, dots, 0.0), axis=0, keepdims=True) for hit in hits]
            line = jnp.concatenate(sums + [jnp.zeros_like(sums[0])], axis=1)
            row_id = lax.broadcasted_iota(jnp.int32, (EXTRA, width), 0)
            out_ref[place, 2 * PATCHES :, :] = jnp.where(row_id == 0, line, 0.0).astype(bf16)
            for index, source in enumerate((rows_s, cots_s)):
                slots = jnp.concatenate([source[m, span, :] for m in range(members)], axis=0)
                total = mm(hot, slots, TN)
                if block in shared_ids:
                    where = shared_ids.index(block)
                    total = total + shared_s[where, :, index * width : (index + 1) * width]
                out_ref[place, index * PATCHES : (index + 1) * PATCHES, :] = total.astype(bf16)


def experts_both(base, blocks, shared_up, shared_down, expert_up, expert_down, shared_ids, after=()):
    members, width, hidden = expert_up.shape
    shape = (HALF, 2 * PATCHES + EXTRA, width)
    out_spec = pl.BlockSpec(shape, lambda e, b: (0, 0, 0))
    slots = (members, 2 * HALF * CAP)
    return launch(
        functools.partial(expert_kernel, shared_ids), "experts_both", [(shape, bf16)] * 2,
        [operand for part in blocks for operand in part.operands()]
        + [shared_up, shared_down, expert_up, expert_down],
        in_specs=[spec for part in blocks for spec in part.specs()]
        + [
            pl.BlockSpec((width, hidden), lambda e, b: (0, 0)),
            pl.BlockSpec((hidden, width), lambda e, b: (0, 0)),
            pl.BlockSpec((1, width, hidden), lambda e, b: (jnp.maximum(e - 1, 0), 0, 0)),
            pl.BlockSpec((1, hidden, width), lambda e, b: (jnp.maximum(e - 1, 0), 0, 0)),
        ],
        out_specs=[out_spec, out_spec],
        grid=(members + 1,),
        scalars=[base],
        after=after,
        scratch=[
            pltpu.VMEM((*slots, width), bf16),
            pltpu.VMEM((*slots, width), bf16),
            pltpu.VMEM((*slots, 1), f32),
            pltpu.VMEM((*slots, 1), f32),
            pltpu.VMEM((max(len(shared_ids), 1), PATCHES, 2 * width), f32),
        ], flops=30 * 10**9, moved=30 * 10**6,
    )


def both_grads(inputs, cots, up, down):
    value, slope = gelu_both(mm(up, inputs, TT))
    pre_grad = (mm(down, cots, NT) * slope).astype(bf16)
    return mm(inputs, pre_grad, TT), mm(value.astype(bf16), cots, NN)


def grads_kernel(count, tile, started, *refs):
    row_refs, cot_refs = refs[:count], refs[count : 2 * count]
    up_ref, down_ref = refs[2 * count : 2 * count + 2]
    up_grad_ref, down_grad_ref = refs[-2:]
    width = up_ref.shape[1]
    inputs = [ref[...].reshape(-1, width) for ref in row_refs]
    cots = [ref[...].reshape(-1, width) for ref in cot_refs]
    groups = max(1, count * inputs[0].shape[0] // tile)
    each = count // groups
    for group in range(groups):
        part = slice(group * each, (group + 1) * each)
        rows, cot = jnp.concatenate(inputs[part], axis=0), jnp.concatenate(cots[part], axis=0)
        up_grad, down_grad = both_grads(rows, cot, up_ref[0], down_ref[0])
        if group == 0 and started:
            up_grad_ref[0] = refs[2 * count + 2][0] + up_grad
            down_grad_ref[0] = refs[2 * count + 3][0] + down_grad
        elif group == 0:
            up_grad_ref[0] = up_grad
            down_grad_ref[0] = down_grad
        else:
            up_grad_ref[0] += up_grad
            down_grad_ref[0] += down_grad


def shared_other_kernel(rows, cots, up, down, up_before, down_before, up_out, down_out, low_out):
    width = up.shape[0]
    grads = both_grads(rows[...].reshape(-1, width), cots[...].reshape(-1, width), up[...], down[...])
    step = pl.program_id(0)
    for grad, before, out in zip(grads, (up_before, down_before), (up_out, down_out)):

        @pl.when(step == 0)
        def _():
            out[...] = before[0] + grad

        @pl.when(step > 0)
        def _():
            out[...] += grad

    @pl.when(step == pl.num_programs(0) - 1)
    def _():
        low_out[0] = up_out[...].astype(bf16)
        low_out[1] = down_out[...].astype(bf16)


def weight_grads(rows, cots, specs, up, down, before, tile, total, after=(), span=None):
    members, width, hidden = up.shape
    start, stop = span or (0, members)
    up_spec = pl.BlockSpec((1, width, hidden), lambda e: (e + start, 0, 0))
    down_spec = pl.BlockSpec((1, hidden, width), lambda e: (e + start, 0, 0))
    started = before is not None
    count = len(rows)
    first = 2 * count + 2
    return launch(
        functools.partial(grads_kernel, count, tile, started), "weight_grads", [(up.shape, f32), (down.shape, f32)],
        [*rows, *cots, up, down, *(before or ())],
        in_specs=specs + [up_spec, down_spec] * (2 if started else 1), out_specs=[up_spec, down_spec],
        grid=(stop - start,), aliases={first: 0, first + 1: 1} if started else None, after=after,
        flops=12 * total * width * hidden, moved=total * width * 4,
    )


def routed_grads(slots, up, down, before, after=(), span=None):
    members, count, width = slots[0][0].shape
    start, stop = span or (0, members)
    spec = pl.BlockSpec((1, count, width), lambda e: (e + start, 0, 0))
    rows, cots = [pair[0] for pair in slots], [pair[1] for pair in slots]
    specs = [spec] * (2 * len(slots))
    each = len(slots) * count
    return weight_grads(
        rows, cots, specs, up, down, before, each, (stop - start) * each, after=after, span=span
    )


def shared_grads(blocks, taken, up, down, before, after=()):
    rows, cots = [part.rows for part in blocks], [part.cots for part in blocks]
    all_specs = [part.specs(taken) for part in blocks]
    specs = [spec[0] for spec in all_specs] + [spec[2] for spec in all_specs]
    total = len(blocks) * taken * PATCHES
    tile = total if total <= 8 * PATCHES else total // 2
    return weight_grads(rows, cots, specs, up[None], down[None], before, tile, total, after)


def shared_grads_other(ext, cots, hop, up, down, before, after=()):
    blocks, _, _, width = ext.shape
    steps = 2
    spec = pl.BlockSpec((blocks // steps, 1, PATCHES, width), lambda t: (t, hop, 0, 0))
    up_spec = pl.BlockSpec(up.shape, lambda t: (0, 0))
    down_spec = pl.BlockSpec(down.shape, lambda t: (0, 0))
    before_specs = [pl.BlockSpec((1, *part.shape), lambda t: (0, 0, 0)) for part in (up, down)]
    low = (2, *up.shape)
    total = blocks * PATCHES
    return launch(
        shared_other_kernel, "shared_grads_other", [(up.shape, f32), (down.shape, f32), (low, bf16)],
        [ext, cots, up, down, *before], in_specs=[spec, spec, up_spec, down_spec] + before_specs,
        out_specs=[up_spec, down_spec, pl.BlockSpec(low, lambda t: (0, 0, 0))],
        grid=(steps,), after=after, flops=12 * total * up.size, moved=total * width * 4,
    )


def shared_last_kernel(up, down, more, up_out, down_out):
    up_out[...] = up[...] + more[0].astype(f32)
    down_out[...] = down[...] + more[1].astype(f32)


def backward_kernel(
    local_width, moe_ref, moe_more_ref, back_ref, back_more_ref, cond_ref, tok_ref, cot_ref, mod_ref, router_ref, pairs_ref, attn_in_ref,
    qkv_ref, context_ref, attn_out_ref, ext_ref, w0, w1, w2, w3,
    output_ref, tok_grad_ref, small_ref, near_ref, far_ref, grad_s,
):
    def put_weight_grad(first, grad):
        for index in range(len(shards)):
            out_ref = (near_ref, far_ref)[index % 2]
            out_ref[index // 2, first : first + local_width, :] = grad[
                index * local_width : (index + 1) * local_width
            ]

    shards = (w0, w1, w2, w3)
    rows, width = tok_ref.shape
    mod = mod_ref[...]
    stream = tok_ref[...].astype(f32)
    attn_out = attn_out_ref[...]
    residual = stream + mod[2:3] * attn_out
    second_norm, second_inv = normalize(residual)
    moe_out = moe_ref[...] + moe_more_ref[...].astype(f32)
    back = back_ref[...] + back_more_ref[...].astype(f32)
    upstream = cot_ref[...].astype(f32)
    output_ref[...] = (residual + mod[5:6] * moe_out).astype(bf16)
    gate_two_grad = jnp.sum(upstream * moe_out, axis=0, keepdims=True)
    routes, places, gates = read_pairs(ext_ref[rows:, :])
    dots = (back[rows : rows + 1, 0:PATCHES], back[rows : rows + 1, PATCHES : 2 * PATCHES])
    mean_dot = gates[0] * dots[0] + gates[1] * dots[1]
    pairs = pairs_ref[...]
    expert_id = lax.broadcasted_iota(jnp.int32, (EXPERTS, rows), 0)
    logits_grad = jnp.zeros((EXPERTS, rows), f32)
    for k in range(TOPK):
        logits_grad += jnp.where(expert_id == pairs[k : k + 1], gates[k] * (dots[k] - mean_dot), 0.0)
    logits_grad = logits_grad.astype(bf16)
    moe_in_grad = back[0:rows] + mm(logits_grad, router_ref[...], TN)
    shift_two_grad = jnp.sum(moe_in_grad, axis=0, keepdims=True)
    scale_two_grad = jnp.sum(moe_in_grad * second_norm, axis=0, keepdims=True)
    residual_grad = upstream + normalize_back(
        second_norm, second_inv, moe_in_grad * (1.0 + mod[4:5])
    )
    gate_one_grad = jnp.sum(residual_grad * attn_out, axis=0, keepdims=True)
    attn_grad = (mod[2:3] * residual_grad).astype(bf16)
    out_grad = mm(context_ref[...], attn_grad, TN).astype(bf16)
    put_weight_grad(3 * local_width, out_grad)
    context_grad = mm(attn_grad, shard_rows(shards, 3, local_width), NT).astype(bf16)
    masks = pair_masks(rows)
    zero = jnp.zeros((rows, 2 * HD), bf16)
    scale = 1.0 / math.sqrt(HD)
    for pair in range(width // (2 * HD)):
        cols = slice(pair * 2 * HD, (pair + 1) * 2 * HD)
        query, key, value = qkv_ref[0, :, cols], qkv_ref[1, :, cols], qkv_ref[2, :, cols]
        upper = context_grad[:, cols]
        sums = []
        for mask in masks:
            probs = head_probs(jnp.where(mask, query, zero), key)
            probs_grad = mm(jnp.where(mask, upper, zero), value, NT)
            value_grad = mm(probs.astype(bf16), upper, TN)
            score_grad = (
                probs * (probs_grad - jnp.sum(probs_grad * probs, axis=-1, keepdims=True))
            ).astype(bf16)
            sums.append((mm(score_grad, key, NN) * scale, mm(score_grad, query, TN) * scale, value_grad))
        for part in range(3):
            grad_s[part, :, cols] = jnp.where(masks[0], sums[0][part], sums[1][part]).astype(bf16)
    attn_in = attn_in_ref[...]
    attn_in_grad = jnp.zeros((rows, width), f32)
    for part in range(3):
        grad = grad_s[part]
        attn_in_grad += mm(grad, shard_rows(shards, part, local_width), NN)
        put_weight_grad(part * local_width, mm(grad, attn_in, TN).astype(bf16))
    first_norm, first_inv = normalize(stream)
    shift_one_grad = jnp.sum(attn_in_grad, axis=0, keepdims=True)
    scale_one_grad = jnp.sum(attn_in_grad * first_norm, axis=0, keepdims=True)
    tok_grad_ref[...] = residual_grad + normalize_back(
        first_norm, first_inv, attn_in_grad * (1.0 + mod[1:2])
    )
    lines = (
        shift_one_grad, scale_one_grad, gate_one_grad, shift_two_grad, scale_two_grad, gate_two_grad,
        cond_ref[...],
    )
    row_id = lax.broadcasted_iota(jnp.int32, (8, width), 0)
    stacked = jnp.zeros((8, width), f32)
    for index, line in enumerate(lines):
        stacked = jnp.where(row_id == index, line, stacked)
    small_ref[0:8, :] = stacked
    small_ref[8:16, :] = mm(logits_grad, ext_ref[0:rows, :], NN)


def attention_backward(
    moe, moe_more, back, back_more, cond, tokens, cotangent, mod, router_t, pairs, attn_in, qkv, context,
    attn_out, ext, shards, local_width, after=(),
):
    rows, width = tokens.shape
    halves = ((len(shards) // 2, 4 * local_width, width), bf16)
    return launch(
        functools.partial(backward_kernel, local_width), "attention_backward",
        [((rows, width), bf16), ((rows, width), f32), ((16, width), f32), halves, halves],
        [
            moe, moe_more, back, back_more, cond, tokens, cotangent, mod, router_t, pairs, attn_in, qkv,
            context, attn_out, ext, *shards,
        ],
        scratch=[pltpu.VMEM((3, rows, width), bf16)], after=after, flops=10 * 10**9, moved=16 * 10**6,
    )


def take_all(copies):
    for copy in copies:
        copy.start()
    for copy in copies:
        copy.wait()


def plane_first_kernel(first, more, side, other, upper_s, lower_s, sems):
    cut = PATCHES
    low = first.shape[1] - cut
    copies = []
    for index, source in enumerate((first, more)):
        for place, (upper, lower) in enumerate(((1, 2), (3, 3))):
            at = 4 * index + 2 * place
            copies += [
                pltpu.make_async_copy(source.at[upper, pl.ds(0, cut)], upper_s.at[index, place], sems.at[at]),
                pltpu.make_async_copy(source.at[lower, pl.ds(cut, low)], lower_s.at[index, place], sems.at[at + 1]),
            ]
    take_all(copies)
    side[...] = (upper_s[0].astype(f32) + upper_s[1].astype(f32)).astype(bf16)
    other[...] = (lower_s[0].astype(f32) + lower_s[1].astype(f32)).astype(bf16)


def plane_second_kernel(first, more, side, other, upper, lower, upper_next, lower_next, upper_s, lower_s, sems):
    cut = PATCHES
    low = first.shape[1] - cut
    copies = []
    for index, source in enumerate((first, more)):
        for place, (up, down) in enumerate(((0, 0), (2, 1))):
            at = 4 * index + 2 * place
            copies += [
                pltpu.make_async_copy(source.at[up, pl.ds(0, cut)], upper_s.at[index, place], sems.at[at]),
                pltpu.make_async_copy(source.at[down, pl.ds(cut, low)], lower_s.at[index, place], sems.at[at + 1]),
            ]
    take_all(copies)
    uppers = [upper_s[0, p].astype(f32) + upper_s[1, p].astype(f32) + side[p].astype(f32) for p in range(2)]
    lowers = [lower_s[0, p].astype(f32) + lower_s[1, p].astype(f32) + other[p].astype(f32) for p in range(2)]
    upper[...] = uppers[0]
    upper_next[...] = uppers[1].astype(bf16)
    lower[...] = lowers[0]
    lower_next[...] = lowers[1].astype(bf16)


def span_of(index, size):
    return pl.ds(pl.multiple_of(index * size, size), size)


def dense_first_kernel(place, near, more, side, other, keep_upper, keep_lower):
    cut = near.shape[1] // 2
    half = cut // 2
    mine = place[0]
    side[...] = (near[1, 0:cut, :].astype(f32) + more[1, 0:cut, :].astype(f32)).astype(bf16)
    keep_upper[...] = near[0, 0:cut, :].astype(f32) + more[0, 0:cut, :].astype(f32)
    for index in range(2):
        for out, who in ((keep_lower, mine), (other, 1 - mine)):
            rows = pl.ds(pl.multiple_of(cut + who * half, half), half)
            total = near[index, rows, :].astype(f32) + more[index, rows, :].astype(f32)
            out[index] = total.astype(out.dtype)


def dense_second_kernel(place, keep_upper, keep_lower, from_side, from_other, side, other, upper, lower):
    half = upper.shape[0]
    mine = place[0]
    for out, who in ((upper, mine), (other, 1 - mine)):
        rows = span_of(who, half)
        out[...] = (keep_upper[rows, :] + from_side[rows, :].astype(f32)).astype(out.dtype)
    lower[...] = keep_lower[0] + from_other[0].astype(f32)
    side[...] = (keep_lower[1] + from_other[1].astype(f32)).astype(bf16)


def dense_third_kernel(size, place, upper, lower, from_side, from_other, own, *outs):
    sent, total = outs[:-1], outs[-1]
    half = upper.shape[0]
    share = 2 * half // size
    total[0:half, :] = upper[...] + from_other[...].astype(f32)
    total[half:, :] = lower[...] + from_side[...].astype(f32)
    own[...] = total[span_of(place[1], share), :]
    for hop in range(1, size):
        sent[hop - 1][...] = total[span_of(lax.rem(place[1] + hop, size), share), :].astype(bf16)


def dense_fourth_kernel(own, *refs):
    out = refs[-1]
    total = own[...]
    for ref in refs[:-1]:
        total = total + ref[...].astype(f32)
    out[...] = total.astype(bf16)


def dense_fifth_kernel(size, place, own, *refs):
    out = refs[-1]
    share = own.shape[0]
    out[span_of(place[1], share), :] = own[...]
    for hop in range(1, size):
        out[span_of(lax.rem(place[1] + size - hop, size), share), :] = refs[hop - 1][...]


def dense_last_kernel(place, own, more, qkv_out, out_out, total):
    half = own.shape[0] // 2
    for ref, who in ((own, place[0]), (more, 1 - place[0])):
        for index in range(2):
            rows = pl.ds(pl.multiple_of(2 * half * index + who * half, half), half)
            total[rows, :] = ref[index * half : (index + 1) * half, :].astype(f32)
    count = qkv_out.shape[0]
    qkv_out[...] = total[0:count, :]
    out_out[...] = total[count:, :]


class Links:
    def __init__(self, mesh):
        self.dp, self.expert, self.tensor = (mesh.shape[name] for name in ("dp", "expert", "tensor"))
        self.paired = self.expert == 2 and self.tensor == 4
        self.core = [(i, i ^ 1) for i in range(self.tensor)]
        self.side = [(i, i ^ 2) for i in range(self.tensor)]
        self.other = [(0, 1), (1, 0)]

    def to_core(self, value):
        return lax.ppermute(value, "tensor", self.core)

    def to_side(self, value):
        return lax.ppermute(value, "tensor", self.side)

    def to_other(self, value):
        return lax.ppermute(value, "expert", self.other)

    def to_next(self, value):
        return lax.ppermute(value, "dp", [(i, i ^ 1) for i in range(self.dp)])

    def along(self, value, hop):
        return lax.ppermute(value, "dp", [(i, (i + hop) % self.dp) for i in range(self.dp)])

    def column(self, block):
        copies = jnp.broadcast_to(block[None], (self.dp, *block.shape))
        return lax.all_to_all(copies, "dp", split_axis=0, concat_axis=0)

    def column_rest(self, column, place, after):
        planes, rows, width = column.shape
        (rest,) = launch(
            pick_kernel, "pick", [((planes - 1, rows, width), column.dtype)], [column], scalars=[place], after=after,
            moved=3 * 10**6,
        )
        return rest, lax.all_gather(rest, ("expert", "tensor"), axis=0)

    def plane_sum_first(self, first, more, after):
        width = first.shape[2]
        low = first.shape[1] - PATCHES
        return launch(
            plane_first_kernel, "plane_first", [((2, PATCHES, width), bf16), ((2, low, width), bf16)],
            [first, more], in_specs=[pl.BlockSpec(memory_space=pl.ANY)] * 2,
            scratch=[
                pltpu.VMEM((2, 2, PATCHES, width), bf16),
                pltpu.VMEM((2, 2, low, width), bf16),
                pltpu.SemaphoreType.DMA((8,)),
            ],
            after=after, moved=5 * 10**6,
        )

    def plane_sum_second(self, first, more, side, other, after):
        width = first.shape[2]
        low = first.shape[1] - PATCHES
        return launch(
            plane_second_kernel, "plane_second",
            [((PATCHES, width), f32), ((low, width), f32), ((PATCHES, width), bf16), ((low, width), bf16)],
            [first, more, side, other],
            in_specs=[pl.BlockSpec(memory_space=pl.ANY)] * 2 + [pl.BlockSpec(memory_space=pltpu.VMEM)] * 2,
            scratch=[
                pltpu.VMEM((2, 2, PATCHES, width), bf16),
                pltpu.VMEM((2, 2, low, width), bf16),
                pltpu.SemaphoreType.DMA((8,)),
            ],
            after=after, moved=7 * 10**6,
        )

    def dense_sum(self, near, far):
        _, rows, width = near.shape
        cut, half, share = rows // 2, rows // 4, rows // 2 // self.dp
        place = [jnp.stack([lax.axis_index("expert"), lax.axis_index("dp")]).astype(jnp.int32)]
        more = self.to_core(far)
        after = yield None
        side, other, keep_upper, keep_lower = launch(
            dense_first_kernel, "dense_first",
            [((cut, width), bf16), ((2, half, width), bf16), ((cut, width), f32), ((2, half, width), f32)],
            [near, more], scalars=place, after=after, moved=8 * 10**6,
        )
        from_side, from_other = self.to_side(side), self.to_other(other)
        after = yield keep_upper
        side, other, upper, lower = launch(
            dense_second_kernel, "dense_second",
            [((half, width), bf16), ((half, width), bf16), ((half, width), f32), ((half, width), f32)],
            [keep_upper, keep_lower, from_side, from_other], scalars=place, after=after, moved=5 * 10**6,
        )
        from_side, from_other = self.to_side(side), self.to_other(other)
        after = yield upper
        hops = range(1, self.dp)
        outs = launch(
            functools.partial(dense_third_kernel, self.dp), "dense_third",
            [((share, width), f32)] + [((share, width), bf16)] * len(hops),
            [upper, lower, from_side, from_other], scalars=place, scratch=[pltpu.VMEM((cut, width), f32)],
            after=after, moved=3 * 10**6,
        )
        moved = [self.along(outs[hop], hop) for hop in hops]
        after = yield outs[0]
        (total,) = launch(
            dense_fourth_kernel, "dense_fourth", [((share, width), bf16)], [outs[0], *moved], after=after,
            moved=10**6,
        )
        moved = [self.along(total, hop) for hop in hops]
        after = yield total
        (column,) = launch(
            functools.partial(dense_fifth_kernel, self.dp), "dense_fifth", [((cut, width), bf16)], [total, *moved],
            scalars=place, after=after, moved=10**6,
        )
        more = self.to_other(column)
        after = yield column
        yield launch(
            dense_last_kernel, "dense_last", [((rows * 3 // 4, width), f32), ((rows // 4, width), f32)],
            [column, more], scalars=place, scratch=[pltpu.VMEM((rows, width), f32)], after=after,
            moved=4 * 10**6,
        )


def local(
    links,
    tokens,
    cotangent,
    timesteps,
    ada_weight,
    ada_bias,
    qkv_weight,
    out_weight,
    router_weight,
    shared_up,
    shared_down,
    expert_up,
    expert_down,
    routes,
    places,
):
    rows, width = tokens.shape
    local_width = qkv_weight.shape[2]
    members = expert_up.shape[0]
    me = lax.axis_index("tensor")
    base = (lax.axis_index("expert") * members).astype(jnp.int32).reshape(1)
    everyone = ("dp", "expert", "tensor")
    total_blocks = links.dp * links.expert * links.tensor
    full = links.paired and links.dp == 4 and total_blocks * rows * width * 2 <= FULL_LIMIT

    condition = jax.nn.silu(embedding(timesteps, width)).astype(bf16)
    mod_cols = jnp.einsum("id,dcf->icf", condition, ada_weight, preferred_element_type=f32) + ada_bias[None]
    mod = lax.all_to_all(mod_cols, "tensor", split_axis=0, concat_axis=2, tiled=True)[0]
    own_condition = lax.dynamic_slice_in_dim(condition.astype(f32), me, 1, axis=0)
    shared_cot = (mod[5][None] * cotangent.astype(f32)).astype(bf16)

    weight = jnp.concatenate(
        [qkv_weight.transpose(1, 2, 0).reshape(3 * local_width, width), out_weight], axis=0
    )
    if full:
        (weight,) = ordered([weight], [shared_cot])
    across = links.to_side(weight)
    near_shard = links.to_core(weight)
    if full:
        place = jnp.stack([base[0], *(lax.axis_index(axis) for axis in ("expert", "dp"))]).astype(jnp.int32)
        cot_column = links.column(shared_cot)
        cot_other = links.to_other(shared_cot)
        across, cot_other = ordered([across, cot_other], [mod])
        cot_side = links.to_side(ordered([shared_cot], [across])[0])
        cot_corner = links.to_other(cot_side)
    else:
        (across,) = ordered([across], [mod])
    shards = (weight, near_shard, across, links.to_core(across))
    router_t = router_weight.T
    pairs = jnp.concatenate([routes.T, places.T], axis=0)

    whole = slice(None)
    attn_in, qkv, context, attn_out, ext = attention_forward(tokens, mod, router_t, pairs, shards, local_width)
    feed = (shared_up, shared_down, expert_up, expert_down)
    backward = functools.partial(
        attention_backward, cond=own_condition, tokens=tokens, cotangent=cotangent, mod=mod, router_t=router_t,
        pairs=pairs, attn_in=attn_in, qkv=qkv, context=context, attn_out=attn_out, ext=ext, shards=shards,
        local_width=local_width,
    )
    if full:
        ext_side, ext_other = links.to_side(ext), links.to_other(ext)
        cut = PATCHES // 2 + EXTRA
        ext_cuts = (ext_other[:cut], ext_side[cut:])
        ext_corner = (links.to_side(ext_cuts[0]), links.to_other(ext_cuts[1]))
        cot_mine = assemble(
            (HALF, PATCHES, width), bf16, [shared_cot, cot_side, cot_other, cot_corner],
            [(index, whole, index) for index in range(HALF)], after=ext_cuts,
        )
        cot_near = links.to_core(cot_mine)
        ext_column = links.column(ordered([ext], [ext_side, ext_other])[0])
        ext_mine = assemble(
            (HALF, PATCHES + EXTRA, width), bf16, [ext, ext_side, ext_other, *ext_corner],
            [(index, whole, index) for index in range(3)]
            + [(3, whole, (3, pl.ds(0, cut))), (4, whole, (3, pl.ds(cut, PATCHES // 2)))],
        )
        ext_near = links.to_core(ext_mine)
        own = (Blocks.apart(ext_mine, cot_mine), Blocks.apart(ext_near, cot_near))
        cot_rest, cots = links.column_rest(cot_column, place, [cot_mine])
        first, second = experts_both(base, own, *feed, (0, 1, 4, 5), after=[cot_rest])
        ext_rest, exts = links.column_rest(ext_column, place, [first])
        moved = links.to_core(second)
        slots = dispatch(base, own, members, after=[first, ext_rest])
        side, other = links.plane_sum_first(first, moved, after=[slots[0]])
        from_side, from_other = links.to_side(side), links.to_other(other)
        routed = routed_grads([slots], expert_up, expert_down, None, after=[side])
        upper, lower, upper_next, lower_next = links.plane_sum_second(
            first, moved, from_side, from_other, after=[routed[0]]
        )
        upper_more, lower_more = links.to_other(upper_next), links.to_side(lower_next)
        shared = shared_grads(own, HALF, shared_up, shared_down, None, after=[upper, cots])
        output, tokens_grad, small, near, far = backward(
            upper, upper_more, lower, lower_more, after=[shared[0]]
        )
        dense = links.dense_sum(near, far)
        next(dense)
        small_all = lax.all_gather(small, everyone, axis=0)
        *shared, sent = shared_grads_other(exts, cots, 1, shared_up, shared_down, shared, after=[small])
        shared_more = links.to_next(sent)
        step = dense.send([sent])
        slots = dispatch_hops(base, exts, cots, members, after=[step])
        step = dense.send([slots[0]])
        for span in ((0, 2), (2, 3)):
            routed = routed_grads([slots], expert_up, expert_down, routed, after=[step], span=span)
            step = dense.send([routed[0]])
        shared = launch(
            shared_last_kernel, "shared_last", [(shared_up.shape, f32), (shared_down.shape, f32)],
            [*shared, shared_more], after=[step], moved=12 * 10**6,
        )
        routed = routed_grads([slots], expert_up, expert_down, routed, after=[shared[0]], span=(3, members))
        step = dense.send([routed[0]])
        qkv_grad, out_grad = dense.send([step])
        (small_all,) = ordered([small_all], [routed[0]])
        routes_all = jnp.concatenate(
            [value[..., PATCHES, : TOPK * PATCHES].reshape(-1, TOPK * PATCHES) for value in (ext_mine, ext_near, exts)],
            axis=0,
        )
    else:
        shift = lax.axis_index("expert") * links.tensor
        gather = lambda block: jnp.roll(
            lax.all_gather(block, ("expert", "tensor"), axis=0), -shift, axis=0
        )
        all_ext, all_cot = gather(ext), gather(shared_cot)
        planes, sums = [], []
        for start in range(0, links.expert * links.tensor, 2 * HALF):
            spans = [slice(start + HALF * part, start + HALF * (part + 1)) for part in range(2)]
            planes.append(tuple(Blocks.apart(all_ext[span], all_cot[span]) for span in spans))
            shared_ids = tuple(range(links.tensor)) if start == 0 else ()
            sums += experts_both(base, planes[-1], *feed, shared_ids)
        blocks = jnp.roll(jnp.concatenate(sums, axis=0), shift, axis=0)
        total = lax.psum_scatter(blocks, ("expert", "tensor"), scatter_dimension=0, tiled=True)[0]
        upper, lower = total[:PATCHES].astype(f32), total[PATCHES:].astype(f32)
        output, tokens_grad, small, near, far = backward(
            upper, jnp.zeros_like(total[:PATCHES]), lower, jnp.zeros_like(total[PATCHES:])
        )
        small_all = lax.all_gather(small, everyone, axis=0)
        slots = [dispatch(base, plane, members) for plane in planes]
        routed = None
        for start in range(0, len(planes), 2):
            routed = routed_grads(slots[start : start + 2], expert_up, expert_down, routed)
        shared = shared_grads(planes[0][:1], HALF, shared_up, shared_down, None)
        routed = lax.psum(routed, "dp")
        shared = lax.psum(tuple(part[0] for part in shared), ("dp", "expert"))
        routes_all = lax.all_gather(routes.reshape(-1), everyone, axis=0)
        turn = jnp.arange(links.tensor) ^ me
        grads = jnp.stack([near, far], axis=1).reshape((-1,) + near.shape[1:])[turn]
        dense = lax.psum_scatter(grads, "tensor", scatter_dimension=0, tiled=True)[0]
        dense = lax.psum(dense, ("dp", "expert")).astype(f32)
        qkv_grad, out_grad = dense[: 3 * local_width], dense[3 * local_width :]

    condition_all = small_all[:, 6].astype(bf16)
    mod_grad = lax.dynamic_slice_in_dim(small_all[:, 0:6], me * local_width, local_width, axis=2)
    ada_grad = jnp.einsum(
        "id,icf->dcf", condition_all.astype(f32), mod_grad, precision=lax.Precision.HIGHEST
    )
    ada_bias_grad = jnp.sum(mod_grad, axis=0)
    router_grad = jnp.sum(small_all[:, 8:16], axis=0).T
    counts = jnp.sum(
        (routes_all[:, :, None] == jnp.arange(EXPERTS).astype(routes_all.dtype)).astype(jnp.int32),
        axis=(0, 1),
    )
    qkv_grad = qkv_grad.reshape(3, local_width, width).transpose(2, 0, 1)
    return (
        output,
        tokens_grad,
        ada_grad,
        ada_bias_grad,
        qkv_grad,
        out_grad,
        router_grad,
        shared[0],
        shared[1],
        routed[0],
        routed[1],
        counts,
    )


def solution(mesh):
    rows = P(("dp", "expert", "tensor"), None)
    placed = (
        rows,
        rows,
        P(("dp", "expert")),
        P(None, None, "tensor"),
        P(None, "tensor"),
        P(None, None, "tensor"),
        P("tensor", None),
        P(),
        P(None, "tensor"),
        P("tensor", None),
        P("expert", None, "tensor"),
        P("expert", "tensor", None),
        rows,
        rows,
    )
    return jax.shard_map(
        functools.partial(local, Links(mesh)),
        mesh=mesh,
        in_specs=placed,
        out_specs=(
            rows,
            rows,
            P(None, None, "tensor"),
            P(None, "tensor"),
            P(None, None, "tensor"),
            P("tensor", None),
            P(),
            P(None, "tensor"),
            P("tensor", None),
            P("expert", None, "tensor"),
            P("expert", "tensor", None),
            P(),
        ),
        check_vma=False,
    )
```

```python
import functools
import math

import jax
import jax.numpy as jnp
from jax import lax
from jax.experimental import pallas as pl
from jax.experimental.pallas import tpu as pltpu
from jax.sharding import PartitionSpec as P

HD = 64
EXPERTS = 8
TOPK = 2
PATCHES = 256
CAP = 80
EXTRA = 16
EPSILON = 1e-06
HALF = 4
FULL_LIMIT = 32 * 1024 * 1024
VMEM_LIMIT = 63 * 1024 * 1024

f32 = jnp.float32
bf16 = jnp.bfloat16
NN = (((1,), (0,)), ((), ()))
NT = (((1,), (1,)), ((), ()))
TN = (((0,), (0,)), ((), ()))
TT = (((0,), (1,)), ((), ()))


def mm(left, right, dims):
    return lax.dot_general(left, right, dims, preferred_element_type=f32)


def normalize(values):
    center = jnp.mean(values, axis=-1, keepdims=True)
    shifted = values - center
    inverse = lax.rsqrt(jnp.mean(shifted * shifted, axis=-1, keepdims=True) + EPSILON)
    return (shifted * inverse, inverse)


def normalize_back(normed, inverse, upstream):
    return inverse * (
        upstream
        - jnp.mean(upstream, axis=-1, keepdims=True)
        - normed * jnp.mean(upstream * normed, axis=-1, keepdims=True)
    )


def embedding(steps, model_width):
    half_width = model_width // 2
    freqs_all = jnp.exp(-math.log(10000.0) * jnp.arange(half_width, dtype=f32) / half_width)
    angles = steps.astype(f32)[:, None] * freqs_all[None, :]
    return jnp.concatenate([jnp.cos(angles), jnp.sin(angles)], axis=1)


def gelu_both(pre):
    const = math.sqrt(2.0 / math.pi)
    square = pre * pre
    tanh = jnp.tanh(const * pre * (1.0 + 0.044715 * square))
    half = 0.5 + 0.5 * tanh
    value = pre * half
    return value, half + value * (1.0 - tanh) * (const + 3.0 * 0.044715 * const * square)


def launch(
    kernel, name, outs, operands, *, in_specs=None, out_specs=None, grid=(), scalars=(), scratch=(), aliases=None,
    after=(), flops=0, moved=0,
):
    lead = len(scalars)
    count = lead + len(operands)
    waits = len(after)
    on_chip = pl.BlockSpec(memory_space=pltpu.VMEM)
    anywhere = pl.BlockSpec(memory_space=pl.ANY)
    in_specs = list(in_specs or [on_chip] * len(operands)) + [anywhere] * waits
    out_specs = tuple(out_specs or [on_chip] * len(outs))

    def body(*refs):
        kernel(*refs[:count], *refs[count + waits :])

    if scalars and grid:
        shape = dict(
            grid_spec=pltpu.PrefetchScalarGridSpec(
                num_scalar_prefetch=lead, grid=grid, in_specs=in_specs, out_specs=out_specs, scratch_shapes=scratch
            )
        )
    else:
        in_specs = [pl.BlockSpec(memory_space=pltpu.SMEM)] * lead + in_specs
        shape = dict(grid=grid, in_specs=in_specs, out_specs=out_specs, scratch_shapes=scratch)
    return pl.pallas_call(
        body,
        out_shape=tuple(jax.ShapeDtypeStruct(*out) for out in outs),
        input_output_aliases=aliases or {},
        compiler_params=pltpu.CompilerParams(vmem_limit_bytes=VMEM_LIMIT),
        cost_estimate=pl.CostEstimate(flops=int(flops), bytes_accessed=int(moved), transcendentals=0),
        name=name,
        **shape,
    )(*scalars, *operands, *after)


def copy_kernel(plan, count, *refs):
    sources, out, sems = refs[:count], refs[-2], refs[-1]
    copies = [
        pltpu.make_async_copy(sources[index].at[take], out.at[put], sems.at[order])
        for order, (index, take, put) in enumerate(plan)
    ]
    for copy in copies:
        copy.start()
    for copy in copies:
        copy.wait()


def assemble(shape, dtype, sources, plan, after=()):
    size = math.prod(shape) * jnp.dtype(dtype).itemsize
    return launch(
        functools.partial(copy_kernel, plan, len(sources)), "assemble", [(shape, dtype)], sources,
        in_specs=[pl.BlockSpec(memory_space=pl.ANY)] * len(sources),
        scratch=[pltpu.SemaphoreType.DMA((len(plan),))], after=after, moved=2 * size,
    )[0]


def order_kernel(*refs):
    pass


def ordered(values, after):
    anywhere = [pl.BlockSpec(memory_space=pl.ANY)] * len(values)
    return launch(
        order_kernel, "ordered", [(value.shape, value.dtype) for value in values], values, in_specs=anywhere,
        out_specs=anywhere, aliases={index: index for index in range(len(values))}, after=after,
    )


def pair_masks(rows):
    lane = lax.broadcasted_iota(jnp.int32, (rows, 2 * HD), 1)
    return (lane < HD, lane >= HD)


def head_probs(query, key):
    scores = mm(query, key, NT) * (1.0 / math.sqrt(HD))
    weights = jnp.exp(scores - jnp.max(scores, axis=-1, keepdims=True))
    return weights / jnp.sum(weights, axis=-1, keepdims=True)


def shard_rows(shards, part, local_width):
    return jnp.concatenate(
        [shard[part * local_width : (part + 1) * local_width, :] for shard in shards], axis=0
    )


def attention_kernel(
    local_width, tok_ref, mod_ref, router_ref, pairs_ref, w0, w1, w2, w3,
    attn_in_ref, qkv_ref, context_ref, attn_out_ref, ext_ref, column_ref,
):
    shards = (w0, w1, w2, w3)
    rows, width = tok_ref.shape
    mod = mod_ref[...]
    stream = tok_ref[...].astype(f32)
    attn_in = (normalize(stream)[0] * (1.0 + mod[1:2]) + mod[0:1]).astype(bf16)
    attn_in_ref[...] = attn_in
    for part in range(3):
        qkv_ref[part] = mm(attn_in, shard_rows(shards, part, local_width), NT).astype(bf16)
    masks = pair_masks(rows)
    zero = jnp.zeros((rows, 2 * HD), bf16)
    for pair in range(width // (2 * HD)):
        cols = slice(pair * 2 * HD, (pair + 1) * 2 * HD)
        query, key, value = qkv_ref[0, :, cols], qkv_ref[1, :, cols], qkv_ref[2, :, cols]
        parts = []
        for mask in masks:
            probs = head_probs(jnp.where(mask, query, zero), key)
            parts.append(mm(probs.astype(bf16), value, NN))
        context_ref[:, cols] = jnp.where(masks[0], parts[0], parts[1]).astype(bf16)
    attn_out = mm(context_ref[...], shard_rows(shards, 3, local_width), NN)
    attn_out_ref[...] = attn_out
    residual = stream + mod[2:3] * attn_out
    moe_in = (normalize(residual)[0] * (1.0 + mod[4:5]) + mod[3:4]).astype(bf16)
    ext_ref[0:rows, :] = moe_in
    logits = mm(router_ref[...], moe_in, NT)
    pairs = pairs_ref[...]
    expert_id = lax.broadcasted_iota(jnp.int32, (EXPERTS, rows), 0)
    chosen = [
        jnp.sum(jnp.where(expert_id == pairs[k : k + 1], logits, 0.0), axis=0, keepdims=True)
        for k in range(TOPK)
    ]
    top = jnp.maximum(chosen[0], chosen[1])
    powers = [jnp.exp(value - top) for value in chosen]
    gates = [power / (powers[0] + powers[1]) for power in powers]
    high = [gate.astype(bf16).astype(f32) for gate in gates]
    rest = [gate - upper for gate, upper in zip(gates, high)]
    values = pairs.astype(f32)
    packed = (
        jnp.concatenate([values[0:1], values[1:2], values[2:3]], axis=1),
        jnp.concatenate([values[3:4], high[0], high[1]], axis=1),
        jnp.concatenate([rest[0], rest[1], jnp.zeros_like(rest[0])], axis=1),
    )
    row_id = lax.broadcasted_iota(jnp.int32, (EXTRA, width), 0)
    extra = jnp.zeros((EXTRA, width), f32)
    for index, line in enumerate(packed):
        extra = jnp.where(row_id == index, line, extra)
    ext_ref[rows : rows + EXTRA, :] = extra.astype(bf16)
    for copy in range(column_ref.shape[0]):
        column_ref[copy] = ext_ref[...]


def attention_forward(tokens, mod, router_t, pairs, shards, local_width, copies):
    rows, width = tokens.shape
    outs = [
        ((rows, width), bf16),
        ((3, rows, width), bf16),
        ((rows, width), bf16),
        ((rows, width), f32),
        ((rows + EXTRA, width), bf16),
        ((copies, rows + EXTRA, width), bf16),
    ]
    return launch(
        functools.partial(attention_kernel, local_width), "attention_forward", outs,
        [tokens, mod, router_t, pairs, *shards], flops=5 * 10**9, moved=9 * 10**6,
    )


def read_pairs(extra):
    info = extra.astype(f32)
    count = PATCHES
    routes = (info[0:1, 0:count], info[0:1, count : 2 * count])
    places = (info[0:1, 2 * count : 3 * count], info[1:2, 0:count])
    gates = (
        info[1:2, count : 2 * count] + info[2:3, 0:count],
        info[1:2, 2 * count : 3 * count] + info[2:3, count : 2 * count],
    )
    return routes, places, gates


def slot_hits(routes, places, base, slots):
    slot_id = lax.broadcasted_iota(jnp.int32, (slots, PATCHES), 0).astype(f32)
    return [
        slot_id == jnp.where(place < CAP, (route - base) * CAP + place, -1.0)
        for route, place in zip(routes, places)
    ]


def slot_gates(hits, gates):
    return jnp.sum(
        jnp.where(hits[0], gates[0], 0.0) + jnp.where(hits[1], gates[1], 0.0), axis=1, keepdims=True
    )


class Blocks:
    def __init__(self, rows, rows_at, extra_at, cots, cots_at):
        self.rows, self.rows_at, self.extra_at, self.cots, self.cots_at = rows, rows_at, extra_at, cots, cots_at

    @classmethod
    def apart(cls, ext, cots):
        return cls(ext, 0, PATCHES // EXTRA, cots, 0)

    def operands(self):
        return [self.rows, self.rows, self.cots]

    def specs(self, taken=HALF):
        width = self.rows.shape[2]
        places = ((PATCHES, self.rows_at), (EXTRA, self.extra_at), (PATCHES, self.cots_at))
        return [
            pl.BlockSpec((taken, count, width), lambda *_, at=at: (0, at, 0)) for count, at in places
        ]

    def extra(self):
        return self.rows[:, self.extra_at * EXTRA : (self.extra_at + 1) * EXTRA]


def dispatch_kernel(base_ref, *refs):
    rows_ref, cots_ref = refs[-2:]
    members = rows_ref.shape[0]
    base = base_ref[0].astype(f32)
    for part in range(2):
        rows_in, extra_in, cots_in = refs[3 * part : 3 * part + 3]

        @pl.when(pl.program_id(0) == part)
        def _():
            for block in range(HALF):
                dispatch_block(
                    base, members, rows_in[block], extra_in[block], cots_in[block], rows_ref, cots_ref, block
                )


def dispatch_block(base, members, rows, extra, cots, rows_ref, cots_ref, block):
    routes, places, gates = read_pairs(extra)
    hits = slot_hits(routes, places, base, members * CAP)
    hot = (hits[0] | hits[1]).astype(bf16)
    picked = mm(hot, rows, NN).astype(bf16)
    scaled = (mm(hot, cots, NN) * slot_gates(hits, gates)).astype(bf16)
    for member in range(members):
        span = slice(member * CAP, (member + 1) * CAP)
        rows_ref[member, block * CAP : (block + 1) * CAP, :] = picked[span]
        cots_ref[member, block * CAP : (block + 1) * CAP, :] = scaled[span]


def hops_kernel(base_ref, ext, cots, rows_ref, cots_ref):
    base = base_ref[0].astype(f32)
    for block in range(ext.shape[0]):
        dispatch_block(
            base, rows_ref.shape[0], ext[block, 0, :PATCHES], ext[block, 0, PATCHES:], cots[block, 0], rows_ref,
            cots_ref, block,
        )


def dispatch_hops(base, ext, cots, members, after=()):
    blocks, hops, rows, width = ext.shape
    out = ((members, hops * blocks * CAP, width), bf16)
    out_spec = pl.BlockSpec((members, blocks * CAP, width), lambda h, b: (0, h, 0))
    specs = [pl.BlockSpec((blocks, 1, count, width), lambda h, b: (0, h, 0, 0)) for count in (rows, PATCHES)]
    return launch(
        hops_kernel, "dispatch_hops", [out, out], [ext, cots], in_specs=specs, out_specs=[out_spec, out_spec],
        grid=(hops,), scalars=[base], after=after, flops=24 * 10**9, moved=48 * 10**6,
    )


def pick_kernel(place_ref, source, out):
    planes = source.shape[0]
    for hop in range(planes - 1):
        out[hop] = source[lax.rem(place_ref[2] + hop + 1, planes)]


def dispatch(base, blocks, members, after=()):
    width = blocks[0].rows.shape[2]
    out = ((members, 2 * HALF * CAP, width), bf16)
    out_spec = pl.BlockSpec((members, HALF * CAP, width), lambda c, *_: (0, c, 0))
    return launch(
        dispatch_kernel, "dispatch", [out, out], [operand for part in blocks for operand in part.operands()],
        in_specs=[spec for part in blocks for spec in part.specs()], out_specs=[out_spec, out_spec],
        grid=(2,), scalars=[base], after=after, flops=8 * 10**9, moved=16 * 10**6,
    )


def expert_kernel(
    shared_ids, base_ref, rows0, extra0, cots0, rows1, extra1, cots1, sup_ref, sdown_ref, eup_ref, edown_ref,
    first_ref, second_ref, rows_s, cots_s, gate_s, dot_s, shared_s,
):
    step = pl.program_id(0)
    members = rows_s.shape[0]
    width = sup_ref.shape[0]
    base = base_ref[0].astype(f32)
    halves = ((rows0, extra0, cots0), (rows1, extra1, cots1))
    total_rows = 2 * HALF * CAP

    def hits_of(half, place):
        routes, places, gates = read_pairs(halves[half][1][place])
        return slot_hits(routes, places, base, members * CAP), gates

    def start_of(half, place):
        return pl.multiple_of((half * HALF + place) * CAP, CAP)

    def per_block(count, body, first=0):
        for half in range(2):
            lax.fori_loop(first, count, lambda place, _, half=half: (body(half, place), 0)[1], 0)

    @pl.when(step == 0)
    def _():
        def send(half, place):
            rows_in, _, cots_in = halves[half]
            hits, gates = hits_of(half, place)
            hot = (hits[0] | hits[1]).astype(bf16)
            picked = mm(hot, rows_in[place], NN).astype(bf16)
            cots = mm(hot, cots_in[place], NN).astype(bf16)
            gate = slot_gates(hits, gates)
            rows = pl.ds(start_of(half, place), CAP)
            for member in range(members):
                span = slice(member * CAP, (member + 1) * CAP)
                rows_s[member, rows, :] = picked[span]
                cots_s[member, rows, :] = cots[span]
                gate_s[member, rows, :] = gate[span]

        per_block(HALF, send)
        for start in range(0, len(shared_ids), 2):
            pair = shared_ids[start : start + 2]
            inputs = jnp.concatenate([halves[b // HALF][0][b % HALF] for b in pair], axis=0)
            cots = jnp.concatenate([halves[b // HALF][2][b % HALF] for b in pair], axis=0)
            value, slope = gelu_both(mm(inputs, sup_ref[...], NN))
            pre_grad = (mm(cots, sdown_ref[...], NT) * slope).astype(bf16)
            result = mm(value.astype(bf16), sdown_ref[...], NN)
            back = mm(pre_grad, sup_ref[...], NT)
            for place in range(len(pair)):
                span = slice(place * PATCHES, (place + 1) * PATCHES)
                shared_s[start + place, :, 0:width] = result[span]
                shared_s[start + place, :, width:] = back[span]

    @pl.when(step > 0)
    def _():
        member = step - 1
        tile = total_rows // 2

        for part in range(2):
            span = slice(part * tile, (part + 1) * tile)
            inputs, cots, gate = rows_s[member, span, :], cots_s[member, span, :], gate_s[member, span, :]
            value, slope = gelu_both(mm(inputs, eup_ref[0], NN))
            act_grad = mm(cots, edown_ref[0], NT)
            dot_s[member, span, :] = jnp.sum(value * act_grad, axis=1, keepdims=True)
            active = (gate * value).astype(bf16)
            pre_grad = (gate * act_grad * slope).astype(bf16)
            rows_s[member, span, :] = mm(active, edown_ref[0], NN).astype(bf16)
            cots_s[member, span, :] = mm(pre_grad, eup_ref[0], NT).astype(bf16)

    @pl.when(step == members)
    def _():
        per_half = [sum(1 for b in shared_ids if b // HALF == half) for half in range(2)]

        def combine(half, place, shared):
            out_ref = (first_ref, second_ref)[half]
            hits, _ = hits_of(half, place)
            hot = (hits[0] | hits[1]).astype(bf16)
            span = pl.ds(start_of(half, place), CAP)
            dots = jnp.concatenate([dot_s[m, span, :] for m in range(members)], axis=0)
            sums = [jnp.sum(jnp.where(hit, dots, 0.0), axis=0, keepdims=True) for hit in hits]
            line = jnp.concatenate(sums + [jnp.zeros_like(sums[0])], axis=1)
            row_id = lax.broadcasted_iota(jnp.int32, (EXTRA, width), 0)
            out_ref[place, 2 * PATCHES :, :] = jnp.where(row_id == 0, line, 0.0).astype(bf16)
            for index, source in enumerate((rows_s, cots_s)):
                slots = jnp.concatenate([source[m, span, :] for m in range(members)], axis=0)
                total = mm(hot, slots, TN)
                if shared:
                    where = half * per_half[0] + place
                    total = total + shared_s[where, :, index * width : (index + 1) * width]
                out_ref[place, index * PATCHES : (index + 1) * PATCHES, :] = total.astype(bf16)

        for half in range(2):
            for first, last, shared in ((0, per_half[half], True), (per_half[half], HALF, False)):
                if last > first:
                    lax.fori_loop(
                        first, last,
                        lambda place, _, half=half, shared=shared: (combine(half, place, shared), 0)[1], 0,
                    )


def experts_both(base, blocks, shared_up, shared_down, expert_up, expert_down, shared_ids, after=()):
    members, width, hidden = expert_up.shape
    shape = (HALF, 2 * PATCHES + EXTRA, width)
    out_spec = pl.BlockSpec(shape, lambda e, b: (0, 0, 0))
    slots = (members, 2 * HALF * CAP)
    return launch(
        functools.partial(expert_kernel, shared_ids), "experts_both", [(shape, bf16)] * 2,
        [operand for part in blocks for operand in part.operands()]
        + [shared_up, shared_down, expert_up, expert_down],
        in_specs=[spec for part in blocks for spec in part.specs()]
        + [
            pl.BlockSpec((width, hidden), lambda e, b: (0, 0)),
            pl.BlockSpec((hidden, width), lambda e, b: (0, 0)),
            pl.BlockSpec((1, width, hidden), lambda e, b: (jnp.maximum(e - 1, 0), 0, 0)),
            pl.BlockSpec((1, hidden, width), lambda e, b: (jnp.maximum(e - 1, 0), 0, 0)),
        ],
        out_specs=[out_spec, out_spec],
        grid=(members + 1,),
        scalars=[base],
        after=after,
        scratch=[
            pltpu.VMEM((*slots, width), bf16),
            pltpu.VMEM((*slots, width), bf16),
            pltpu.VMEM((*slots, 1), f32),
            pltpu.VMEM((*slots, 1), f32),
            pltpu.VMEM((max(len(shared_ids), 1), PATCHES, 2 * width), f32),
        ], flops=30 * 10**9, moved=30 * 10**6,
    )


def both_grads(inputs, cots, up, down):
    value, slope = gelu_both(mm(up, inputs, TT))
    pre_grad = (mm(down, cots, NT) * slope).astype(bf16)
    return mm(inputs, pre_grad, TT), mm(value.astype(bf16), cots, NN)


def grads_kernel(count, tile, started, *refs):
    row_refs, cot_refs = refs[:count], refs[count : 2 * count]
    up_ref, down_ref = refs[2 * count : 2 * count + 2]
    up_grad_ref, down_grad_ref = refs[-2:]
    width = up_ref.shape[1]
    inputs = [ref[...].reshape(-1, width) for ref in row_refs]
    cots = [ref[...].reshape(-1, width) for ref in cot_refs]
    groups = max(1, count * inputs[0].shape[0] // tile)
    each = count // groups
    for group in range(groups):
        part = slice(group * each, (group + 1) * each)
        rows, cot = jnp.concatenate(inputs[part], axis=0), jnp.concatenate(cots[part], axis=0)
        up_grad, down_grad = both_grads(rows, cot, up_ref[0], down_ref[0])
        if group == 0 and started:
            up_grad_ref[0] = refs[2 * count + 2][0] + up_grad
            down_grad_ref[0] = refs[2 * count + 3][0] + down_grad
        elif group == 0:
            up_grad_ref[0] = up_grad
            down_grad_ref[0] = down_grad
        else:
            up_grad_ref[0] += up_grad
            down_grad_ref[0] += down_grad


def shared_other_kernel(rows, cots, up, down, up_before, down_before, up_out, down_out, low_out):
    width = up.shape[0]
    grads = both_grads(rows[...].reshape(-1, width), cots[...].reshape(-1, width), up[...], down[...])
    step = pl.program_id(0)
    for grad, before, out in zip(grads, (up_before, down_before), (up_out, down_out)):

        @pl.when(step == 0)
        def _():
            out[...] = before[0] + grad

        @pl.when(step > 0)
        def _():
            out[...] += grad

    @pl.when(step == pl.num_programs(0) - 1)
    def _():
        low_out[0] = up_out[...].astype(bf16)
        low_out[1] = down_out[...].astype(bf16)


def weight_grads(rows, cots, specs, up, down, before, tile, total, after=(), span=None):
    members, width, hidden = up.shape
    start, stop = span or (0, members)
    up_spec = pl.BlockSpec((1, width, hidden), lambda e: (e + start, 0, 0))
    down_spec = pl.BlockSpec((1, hidden, width), lambda e: (e + start, 0, 0))
    started = before is not None
    count = len(rows)
    first = 2 * count + 2
    return launch(
        functools.partial(grads_kernel, count, tile, started), "weight_grads", [(up.shape, f32), (down.shape, f32)],
        [*rows, *cots, up, down, *(before or ())],
        in_specs=specs + [up_spec, down_spec] * (2 if started else 1), out_specs=[up_spec, down_spec],
        grid=(stop - start,), aliases={first: 0, first + 1: 1} if started else None, after=after,
        flops=12 * total * width * hidden, moved=total * width * 4,
    )


def routed_grads(slots, up, down, before, after=(), span=None):
    members, count, width = slots[0][0].shape
    start, stop = span or (0, members)
    spec = pl.BlockSpec((1, count, width), lambda e: (e + start, 0, 0))
    rows, cots = [pair[0] for pair in slots], [pair[1] for pair in slots]
    specs = [spec] * (2 * len(slots))
    each = len(slots) * count
    return weight_grads(
        rows, cots, specs, up, down, before, each, (stop - start) * each, after=after, span=span
    )


def shared_grads(blocks, taken, up, down, before, after=()):
    rows, cots = [part.rows for part in blocks], [part.cots for part in blocks]
    all_specs = [part.specs(taken) for part in blocks]
    specs = [spec[0] for spec in all_specs] + [spec[2] for spec in all_specs]
    total = len(blocks) * taken * PATCHES
    tile = total if total <= 8 * PATCHES else total // 2
    return weight_grads(rows, cots, specs, up[None], down[None], before, tile, total, after)


def shared_grads_other(ext, cots, hop, up, down, before, after=()):
    blocks, _, _, width = ext.shape
    steps = 2
    spec = pl.BlockSpec((blocks // steps, 1, PATCHES, width), lambda t: (t, hop, 0, 0))
    up_spec = pl.BlockSpec(up.shape, lambda t: (0, 0))
    down_spec = pl.BlockSpec(down.shape, lambda t: (0, 0))
    before_specs = [pl.BlockSpec((1, *part.shape), lambda t: (0, 0, 0)) for part in (up, down)]
    low = (2, *up.shape)
    total = blocks * PATCHES
    return launch(
        shared_other_kernel, "shared_grads_other", [(up.shape, f32), (down.shape, f32), (low, bf16)],
        [ext, cots, up, down, *before], in_specs=[spec, spec, up_spec, down_spec] + before_specs,
        out_specs=[up_spec, down_spec, pl.BlockSpec(low, lambda t: (0, 0, 0))],
        grid=(steps,), after=after, flops=12 * total * up.size, moved=total * width * 4,
    )


def shared_last_kernel(up, down, more, up_out, down_out):
    up_out[...] = up[...] + more[0].astype(f32)
    down_out[...] = down[...] + more[1].astype(f32)


def backward_kernel(
    local_width, moe_ref, moe_more_ref, back_ref, back_more_ref, cond_ref, tok_ref, cot_ref, mod_ref, router_ref, pairs_ref, attn_in_ref,
    qkv_ref, context_ref, attn_out_ref, ext_ref, w0, w1, w2, w3,
    output_ref, tok_grad_ref, small_ref, near_ref, far_ref, grad_s,
):
    def put_weight_grad(first, grad):
        for index in range(len(shards)):
            out_ref = (near_ref, far_ref)[index % 2]
            out_ref[index // 2, first : first + local_width, :] = grad[
                index * local_width : (index + 1) * local_width
            ]

    shards = (w0, w1, w2, w3)
    rows, width = tok_ref.shape
    mod = mod_ref[...]
    stream = tok_ref[...].astype(f32)
    attn_out = attn_out_ref[...]
    residual = stream + mod[2:3] * attn_out
    second_norm, second_inv = normalize(residual)
    moe_out = moe_ref[...] + moe_more_ref[...].astype(f32)
    back = back_ref[...] + back_more_ref[...].astype(f32)
    upstream = cot_ref[...].astype(f32)
    output_ref[...] = (residual + mod[5:6] * moe_out).astype(bf16)
    gate_two_grad = jnp.sum(upstream * moe_out, axis=0, keepdims=True)
    routes, places, gates = read_pairs(ext_ref[rows:, :])
    dots = (back[rows : rows + 1, 0:PATCHES], back[rows : rows + 1, PATCHES : 2 * PATCHES])
    mean_dot = gates[0] * dots[0] + gates[1] * dots[1]
    pairs = pairs_ref[...]
    expert_id = lax.broadcasted_iota(jnp.int32, (EXPERTS, rows), 0)
    logits_grad = jnp.zeros((EXPERTS, rows), f32)
    for k in range(TOPK):
        logits_grad += jnp.where(expert_id == pairs[k : k + 1], gates[k] * (dots[k] - mean_dot), 0.0)
    logits_grad = logits_grad.astype(bf16)
    moe_in_grad = back[0:rows] + mm(logits_grad, router_ref[...], TN)
    shift_two_grad = jnp.sum(moe_in_grad, axis=0, keepdims=True)
    scale_two_grad = jnp.sum(moe_in_grad * second_norm, axis=0, keepdims=True)
    residual_grad = upstream + normalize_back(
        second_norm, second_inv, moe_in_grad * (1.0 + mod[4:5])
    )
    gate_one_grad = jnp.sum(residual_grad * attn_out, axis=0, keepdims=True)
    attn_grad = (mod[2:3] * residual_grad).astype(bf16)
    out_grad = mm(context_ref[...], attn_grad, TN).astype(bf16)
    put_weight_grad(3 * local_width, out_grad)
    context_grad = mm(attn_grad, shard_rows(shards, 3, local_width), NT).astype(bf16)
    masks = pair_masks(rows)
    zero = jnp.zeros((rows, 2 * HD), bf16)
    scale = 1.0 / math.sqrt(HD)
    for pair in range(width // (2 * HD)):
        cols = slice(pair * 2 * HD, (pair + 1) * 2 * HD)
        query, key, value = qkv_ref[0, :, cols], qkv_ref[1, :, cols], qkv_ref[2, :, cols]
        upper = context_grad[:, cols]
        sums = []
        for mask in masks:
            probs = head_probs(jnp.where(mask, query, zero), key)
            probs_grad = mm(jnp.where(mask, upper, zero), value, NT)
            value_grad = mm(probs.astype(bf16), upper, TN)
            score_grad = (
                probs * (probs_grad - jnp.sum(probs_grad * probs, axis=-1, keepdims=True))
            ).astype(bf16)
            sums.append((mm(score_grad, key, NN) * scale, mm(score_grad, query, TN) * scale, value_grad))
        for part in range(3):
            grad_s[part, :, cols] = jnp.where(masks[0], sums[0][part], sums[1][part]).astype(bf16)
    attn_in = attn_in_ref[...]
    attn_in_grad = jnp.zeros((rows, width), f32)
    for part in range(3):
        grad = grad_s[part]
        attn_in_grad += mm(grad, shard_rows(shards, part, local_width), NN)
        put_weight_grad(part * local_width, mm(grad, attn_in, TN).astype(bf16))
    first_norm, first_inv = normalize(stream)
    shift_one_grad = jnp.sum(attn_in_grad, axis=0, keepdims=True)
    scale_one_grad = jnp.sum(attn_in_grad * first_norm, axis=0, keepdims=True)
    tok_grad_ref[...] = residual_grad + normalize_back(
        first_norm, first_inv, attn_in_grad * (1.0 + mod[1:2])
    )
    lines = (
        shift_one_grad, scale_one_grad, gate_one_grad, shift_two_grad, scale_two_grad, gate_two_grad,
        cond_ref[...],
    )
    row_id = lax.broadcasted_iota(jnp.int32, (8, width), 0)
    stacked = jnp.zeros((8, width), f32)
    for index, line in enumerate(lines):
        stacked = jnp.where(row_id == index, line, stacked)
    small_ref[0:8, :] = stacked
    small_ref[8:16, :] = mm(logits_grad, ext_ref[0:rows, :], NN)


def attention_backward(
    moe, moe_more, back, back_more, cond, tokens, cotangent, mod, router_t, pairs, attn_in, qkv, context,
    attn_out, ext, shards, local_width, after=(),
):
    rows, width = tokens.shape
    halves = ((len(shards) // 2, 4 * local_width, width), bf16)
    return launch(
        functools.partial(backward_kernel, local_width), "attention_backward",
        [((rows, width), bf16), ((rows, width), f32), ((16, width), f32), halves, halves],
        [
            moe, moe_more, back, back_more, cond, tokens, cotangent, mod, router_t, pairs, attn_in, qkv,
            context, attn_out, ext, *shards,
        ],
        scratch=[pltpu.VMEM((3, rows, width), bf16)], after=after, flops=10 * 10**9, moved=16 * 10**6,
    )


def take_all(copies):
    for copy in copies:
        copy.start()
    for copy in copies:
        copy.wait()


def plane_first_kernel(first, more, side, other, upper_s, lower_s, sems):
    cut = PATCHES
    low = first.shape[1] - cut
    copies = []
    for index, source in enumerate((first, more)):
        for place, (upper, lower) in enumerate(((1, 2), (3, 3))):
            at = 4 * index + 2 * place
            copies += [
                pltpu.make_async_copy(source.at[upper, pl.ds(0, cut)], upper_s.at[index, place], sems.at[at]),
                pltpu.make_async_copy(source.at[lower, pl.ds(cut, low)], lower_s.at[index, place], sems.at[at + 1]),
            ]
    take_all(copies)
    side[...] = (upper_s[0].astype(f32) + upper_s[1].astype(f32)).astype(bf16)
    other[...] = (lower_s[0].astype(f32) + lower_s[1].astype(f32)).astype(bf16)


def plane_second_kernel(first, more, side, other, upper, lower, upper_next, lower_next, upper_s, lower_s, sems):
    cut = PATCHES
    low = first.shape[1] - cut
    copies = []
    for index, source in enumerate((first, more)):
        for place, (up, down) in enumerate(((0, 0), (2, 1))):
            at = 4 * index + 2 * place
            copies += [
                pltpu.make_async_copy(source.at[up, pl.ds(0, cut)], upper_s.at[index, place], sems.at[at]),
                pltpu.make_async_copy(source.at[down, pl.ds(cut, low)], lower_s.at[index, place], sems.at[at + 1]),
            ]
    take_all(copies)
    uppers = [upper_s[0, p].astype(f32) + upper_s[1, p].astype(f32) + side[p].astype(f32) for p in range(2)]
    lowers = [lower_s[0, p].astype(f32) + lower_s[1, p].astype(f32) + other[p].astype(f32) for p in range(2)]
    upper[...] = uppers[0]
    upper_next[...] = uppers[1].astype(bf16)
    lower[...] = lowers[0]
    lower_next[...] = lowers[1].astype(bf16)


def span_of(index, size):
    return pl.ds(pl.multiple_of(index * size, size), size)


def dense_first_kernel(place, near, more, side, other, keep_upper, keep_lower):
    cut = near.shape[1] // 2
    half = cut // 2
    mine = place[0]
    side[...] = (near[1, 0:cut, :].astype(f32) + more[1, 0:cut, :].astype(f32)).astype(bf16)
    keep_upper[...] = near[0, 0:cut, :].astype(f32) + more[0, 0:cut, :].astype(f32)
    for index in range(2):
        for out, who in ((keep_lower, mine), (other, 1 - mine)):
            rows = pl.ds(pl.multiple_of(cut + who * half, half), half)
            total = near[index, rows, :].astype(f32) + more[index, rows, :].astype(f32)
            out[index] = total.astype(out.dtype)


def dense_second_kernel(place, keep_upper, keep_lower, from_side, from_other, side, other, upper, lower):
    half = upper.shape[0]
    mine = place[0]
    for out, who in ((upper, mine), (other, 1 - mine)):
        rows = span_of(who, half)
        out[...] = (keep_upper[rows, :] + from_side[rows, :].astype(f32)).astype(out.dtype)
    lower[...] = keep_lower[0] + from_other[0].astype(f32)
    side[...] = (keep_lower[1] + from_other[1].astype(f32)).astype(bf16)


def dense_third_kernel(size, place, upper, lower, from_side, from_other, own, *outs):
    sent, total = outs[:-1], outs[-1]
    half = upper.shape[0]
    share = 2 * half // size
    total[0:half, :] = upper[...] + from_other[...].astype(f32)
    total[half:, :] = lower[...] + from_side[...].astype(f32)
    own[...] = total[span_of(place[1], share), :]
    for hop in range(1, size):
        sent[hop - 1][...] = total[span_of(lax.rem(place[1] + hop, size), share), :].astype(bf16)


def dense_fourth_kernel(own, *refs):
    out = refs[-1]
    total = own[...]
    for ref in refs[:-1]:
        total = total + ref[...].astype(f32)
    out[...] = total.astype(bf16)


def dense_fifth_kernel(size, place, own, *refs):
    out = refs[-1]
    share = own.shape[0]
    out[span_of(place[1], share), :] = own[...]
    for hop in range(1, size):
        out[span_of(lax.rem(place[1] + size - hop, size), share), :] = refs[hop - 1][...]


def dense_last_kernel(place, own, more, qkv_out, out_out, total):
    half = own.shape[0] // 2
    for ref, who in ((own, place[0]), (more, 1 - place[0])):
        for index in range(2):
            rows = pl.ds(pl.multiple_of(2 * half * index + who * half, half), half)
            total[rows, :] = ref[index * half : (index + 1) * half, :].astype(f32)
    count = qkv_out.shape[0]
    qkv_out[...] = total[0:count, :]
    out_out[...] = total[count:, :]


class Links:
    def __init__(self, mesh):
        self.dp, self.expert, self.tensor = (mesh.shape[name] for name in ("dp", "expert", "tensor"))
        self.paired = self.expert == 2 and self.tensor == 4
        self.core = [(i, i ^ 1) for i in range(self.tensor)]
        self.side = [(i, i ^ 2) for i in range(self.tensor)]
        self.other = [(0, 1), (1, 0)]

    def to_core(self, value):
        return lax.ppermute(value, "tensor", self.core)

    def to_side(self, value):
        return lax.ppermute(value, "tensor", self.side)

    def to_other(self, value):
        return lax.ppermute(value, "expert", self.other)

    def to_next(self, value):
        return lax.ppermute(value, "dp", [(i, i ^ 1) for i in range(self.dp)])

    def along(self, value, hop):
        return lax.ppermute(value, "dp", [(i, (i + hop) % self.dp) for i in range(self.dp)])

    def column(self, copies):
        return lax.all_to_all(copies, "dp", split_axis=0, concat_axis=0)

    def column_rest(self, column, place, after):
        planes, rows, width = column.shape
        (rest,) = launch(
            pick_kernel, "pick", [((planes - 1, rows, width), column.dtype)], [column], scalars=[place], after=after,
            moved=3 * 10**6,
        )
        return rest, lax.all_gather(rest, ("expert", "tensor"), axis=0)

    def plane_sum_first(self, first, more, after):
        width = first.shape[2]
        low = first.shape[1] - PATCHES
        return launch(
            plane_first_kernel, "plane_first", [((2, PATCHES, width), bf16), ((2, low, width), bf16)],
            [first, more], in_specs=[pl.BlockSpec(memory_space=pl.ANY)] * 2,
            scratch=[
                pltpu.VMEM((2, 2, PATCHES, width), bf16),
                pltpu.VMEM((2, 2, low, width), bf16),
                pltpu.SemaphoreType.DMA((8,)),
            ],
            after=after, moved=5 * 10**6,
        )

    def plane_sum_second(self, first, more, side, other, after):
        width = first.shape[2]
        low = first.shape[1] - PATCHES
        return launch(
            plane_second_kernel, "plane_second",
            [((PATCHES, width), f32), ((low, width), f32), ((PATCHES, width), bf16), ((low, width), bf16)],
            [first, more, side, other],
            in_specs=[pl.BlockSpec(memory_space=pl.ANY)] * 2 + [pl.BlockSpec(memory_space=pltpu.VMEM)] * 2,
            scratch=[
                pltpu.VMEM((2, 2, PATCHES, width), bf16),
                pltpu.VMEM((2, 2, low, width), bf16),
                pltpu.SemaphoreType.DMA((8,)),
            ],
            after=after, moved=7 * 10**6,
        )

    def dense_sum(self, near, far):
        _, rows, width = near.shape
        cut, half, share = rows // 2, rows // 4, rows // 2 // self.dp
        place = [jnp.stack([lax.axis_index("expert"), lax.axis_index("dp")]).astype(jnp.int32)]
        more = self.to_core(far)
        after = yield None
        side, other, keep_upper, keep_lower = launch(
            dense_first_kernel, "dense_first",
            [((cut, width), bf16), ((2, half, width), bf16), ((cut, width), f32), ((2, half, width), f32)],
            [near, more], scalars=place, after=after, moved=8 * 10**6,
        )
        from_side, from_other = self.to_side(side), self.to_other(other)
        after = yield keep_upper
        side, other, upper, lower = launch(
            dense_second_kernel, "dense_second",
            [((half, width), bf16), ((half, width), bf16), ((half, width), f32), ((half, width), f32)],
            [keep_upper, keep_lower, from_side, from_other], scalars=place, after=after, moved=5 * 10**6,
        )
        from_side, from_other = self.to_side(side), self.to_other(other)
        after = yield upper
        hops = range(1, self.dp)
        outs = launch(
            functools.partial(dense_third_kernel, self.dp), "dense_third",
            [((share, width), f32)] + [((share, width), bf16)] * len(hops),
            [upper, lower, from_side, from_other], scalars=place, scratch=[pltpu.VMEM((cut, width), f32)],
            after=after, moved=3 * 10**6,
        )
        moved = [self.along(outs[hop], hop) for hop in hops]
        after = yield outs[0]
        (total,) = launch(
            dense_fourth_kernel, "dense_fourth", [((share, width), bf16)], [outs[0], *moved], after=after,
            moved=10**6,
        )
        moved = [self.along(total, hop) for hop in hops]
        after = yield total
        (column,) = launch(
            functools.partial(dense_fifth_kernel, self.dp), "dense_fifth", [((cut, width), bf16)], [total, *moved],
            scalars=place, after=after, moved=10**6,
        )
        more = self.to_other(column)
        after = yield column
        yield launch(
            dense_last_kernel, "dense_last", [((rows * 3 // 4, width), f32), ((rows // 4, width), f32)],
            [column, more], scalars=place, scratch=[pltpu.VMEM((rows, width), f32)], after=after,
            moved=4 * 10**6,
        )


def local(
    links,
    tokens,
    cotangent,
    timesteps,
    ada_weight,
    ada_bias,
    qkv_weight,
    out_weight,
    router_weight,
    shared_up,
    shared_down,
    expert_up,
    expert_down,
    routes,
    places,
):
    rows, width = tokens.shape
    local_width = qkv_weight.shape[2]
    members = expert_up.shape[0]
    me = lax.axis_index("tensor")
    base = (lax.axis_index("expert") * members).astype(jnp.int32).reshape(1)
    everyone = ("dp", "expert", "tensor")
    total_blocks = links.dp * links.expert * links.tensor
    full = links.paired and links.dp == 4 and total_blocks * rows * width * 2 <= FULL_LIMIT

    condition = jax.nn.silu(embedding(timesteps, width)).astype(bf16)
    mod_cols = jnp.einsum("id,dcf->icf", condition, ada_weight, preferred_element_type=f32) + ada_bias[None]
    mod = lax.all_to_all(mod_cols, "tensor", split_axis=0, concat_axis=2, tiled=True)[0]
    own_condition = lax.dynamic_slice_in_dim(condition.astype(f32), me, 1, axis=0)
    shared_cot = (mod[5][None] * cotangent.astype(f32)).astype(bf16)

    weight = jnp.concatenate(
        [qkv_weight.transpose(1, 2, 0).reshape(3 * local_width, width), out_weight], axis=0
    )
    if full:
        (weight,) = ordered([weight], [shared_cot])
    across = links.to_side(weight)
    near_shard = links.to_core(weight)
    if full:
        place = jnp.stack([base[0], *(lax.axis_index(axis) for axis in ("expert", "dp"))]).astype(jnp.int32)
        cot_column = links.column(jnp.broadcast_to(shared_cot[None], (links.dp, *shared_cot.shape)))
        cot_other = links.to_other(shared_cot)
        across, cot_other = ordered([across, cot_other], [mod])
        cot_side = links.to_side(ordered([shared_cot], [across])[0])
        cot_corner = links.to_other(cot_side)
    else:
        (across,) = ordered([across], [mod])
    shards = (weight, near_shard, across, links.to_core(across))
    router_t = router_weight.T
    pairs = jnp.concatenate([routes.T, places.T], axis=0)

    whole = slice(None)
    attn_in, qkv, context, attn_out, ext, ext_copies = attention_forward(
        tokens, mod, router_t, pairs, shards, local_width, links.dp if full else 1
    )
    feed = (shared_up, shared_down, expert_up, expert_down)
    backward = functools.partial(
        attention_backward, cond=own_condition, tokens=tokens, cotangent=cotangent, mod=mod, router_t=router_t,
        pairs=pairs, attn_in=attn_in, qkv=qkv, context=context, attn_out=attn_out, ext=ext, shards=shards,
        local_width=local_width,
    )
    if full:
        ext_side, ext_other = links.to_side(ext), links.to_other(ext)
        cut = PATCHES // 2 + EXTRA
        ext_cuts = (ext_other[:cut], ext_side[cut:])
        ext_corner = (links.to_side(ext_cuts[0]), links.to_other(ext_cuts[1]))
        cot_mine = assemble(
            (HALF, PATCHES, width), bf16, [shared_cot, cot_side, cot_other, cot_corner],
            [(index, whole, index) for index in range(HALF)], after=ext_cuts,
        )
        cot_near = links.to_core(cot_mine)
        ext_column = links.column(ordered([ext_copies], [ext_side, ext_other])[0])
        ext_mine = assemble(
            (HALF, PATCHES + EXTRA, width), bf16, [ext, ext_side, ext_other, *ext_corner],
            [(index, whole, index) for index in range(3)]
            + [(3, whole, (3, pl.ds(0, cut))), (4, whole, (3, pl.ds(cut, PATCHES // 2)))],
        )
        ext_near = links.to_core(ext_mine)
        own = (Blocks.apart(ext_mine, cot_mine), Blocks.apart(ext_near, cot_near))
        cot_rest, cots = links.column_rest(cot_column, place, [cot_mine])
        first, second = experts_both(base, own, *feed, (0, 1, 4, 5), after=[cot_rest])
        ext_rest, exts = links.column_rest(ext_column, place, [first])
        moved = links.to_core(second)
        side, other = links.plane_sum_first(first, moved, after=[ext_rest])
        slots = dispatch(base, own, members, after=[side])
        from_side, from_other = links.to_side(side), links.to_other(other)
        routed = routed_grads([slots], expert_up, expert_down, None)
        upper, lower, upper_next, lower_next = links.plane_sum_second(
            first, moved, from_side, from_other, after=[routed[0]]
        )
        upper_more, lower_more = links.to_other(upper_next), links.to_side(lower_next)
        shared = shared_grads(own, HALF, shared_up, shared_down, None, after=[upper, cots])
        output, tokens_grad, small, near, far = backward(
            upper, upper_more, lower, lower_more, after=[shared[0]]
        )
        dense = links.dense_sum(near, far)
        next(dense)
        small_all = lax.all_gather(small, everyone, axis=0)
        *shared, sent = shared_grads_other(exts, cots, 1, shared_up, shared_down, shared, after=[small])
        shared_more = links.to_next(sent)
        step = dense.send([sent])
        slots = dispatch_hops(base, exts, cots, members, after=[step])
        step = dense.send([slots[0]])
        for span in ((0, 2), (2, 3)):
            routed = routed_grads([slots], expert_up, expert_down, routed, after=[step], span=span)
            step = dense.send([routed[0]])
        shared = launch(
            shared_last_kernel, "shared_last", [(shared_up.shape, f32), (shared_down.shape, f32)],
            [*shared, shared_more], after=[step], moved=12 * 10**6,
        )
        routed = routed_grads([slots], expert_up, expert_down, routed, after=[shared[0]], span=(3, members))
        step = dense.send([routed[0]])
        qkv_grad, out_grad = dense.send([step])
        (small_all,) = ordered([small_all], [routed[0]])
        routes_all = jnp.concatenate(
            [value[..., PATCHES, : TOPK * PATCHES].reshape(-1, TOPK * PATCHES) for value in (ext_mine, ext_near, exts)],
            axis=0,
        )
    else:
        shift = lax.axis_index("expert") * links.tensor
        gather = lambda block: jnp.roll(
            lax.all_gather(block, ("expert", "tensor"), axis=0), -shift, axis=0
        )
        all_ext, all_cot = gather(ext), gather(shared_cot)
        planes, sums = [], []
        for start in range(0, links.expert * links.tensor, 2 * HALF):
            spans = [slice(start + HALF * part, start + HALF * (part + 1)) for part in range(2)]
            planes.append(tuple(Blocks.apart(all_ext[span], all_cot[span]) for span in spans))
            shared_ids = tuple(range(links.tensor)) if start == 0 else ()
            sums += experts_both(base, planes[-1], *feed, shared_ids)
        blocks = jnp.roll(jnp.concatenate(sums, axis=0), shift, axis=0)
        total = lax.psum_scatter(blocks, ("expert", "tensor"), scatter_dimension=0, tiled=True)[0]
        upper, lower = total[:PATCHES].astype(f32), total[PATCHES:].astype(f32)
        output, tokens_grad, small, near, far = backward(
            upper, jnp.zeros_like(total[:PATCHES]), lower, jnp.zeros_like(total[PATCHES:])
        )
        small_all = lax.all_gather(small, everyone, axis=0)
        slots = [dispatch(base, plane, members) for plane in planes]
        routed = None
        for start in range(0, len(planes), 2):
            routed = routed_grads(slots[start : start + 2], expert_up, expert_down, routed)
        shared = shared_grads(planes[0][:1], HALF, shared_up, shared_down, None)
        routed = lax.psum(routed, "dp")
        shared = lax.psum(tuple(part[0] for part in shared), ("dp", "expert"))
        routes_all = lax.all_gather(routes.reshape(-1), everyone, axis=0)
        turn = jnp.arange(links.tensor) ^ me
        grads = jnp.stack([near, far], axis=1).reshape((-1,) + near.shape[1:])[turn]
        dense = lax.psum_scatter(grads, "tensor", scatter_dimension=0, tiled=True)[0]
        dense = lax.psum(dense, ("dp", "expert")).astype(f32)
        qkv_grad, out_grad = dense[: 3 * local_width], dense[3 * local_width :]

    condition_all = small_all[:, 6].astype(bf16)
    mod_grad = lax.dynamic_slice_in_dim(small_all[:, 0:6], me * local_width, local_width, axis=2)
    ada_grad = jnp.einsum(
        "id,icf->dcf", condition_all.astype(f32), mod_grad, precision=lax.Precision.HIGHEST
    )
    ada_bias_grad = jnp.sum(mod_grad, axis=0)
    router_grad = jnp.sum(small_all[:, 8:16], axis=0).T
    counts = jnp.sum(
        (routes_all[:, :, None] == jnp.arange(EXPERTS).astype(routes_all.dtype)).astype(jnp.int32),
        axis=(0, 1),
    )
    qkv_grad = qkv_grad.reshape(3, local_width, width).transpose(2, 0, 1)
    return (
        output,
        tokens_grad,
        ada_grad,
        ada_bias_grad,
        qkv_grad,
        out_grad,
        router_grad,
        shared[0],
        shared[1],
        routed[0],
        routed[1],
        counts,
    )


def solution(mesh):
    rows = P(("dp", "expert", "tensor"), None)
    placed = (
        rows,
        rows,
        P(("dp", "expert")),
        P(None, None, "tensor"),
        P(None, "tensor"),
        P(None, None, "tensor"),
        P("tensor", None),
        P(),
        P(None, "tensor"),
        P("tensor", None),
        P("expert", None, "tensor"),
        P("expert", "tensor", None),
        rows,
        rows,
    )
    return jax.shard_map(
        functools.partial(local, Links(mesh)),
        mesh=mesh,
        in_specs=placed,
        out_specs=(
            rows,
            rows,
            P(None, None, "tensor"),
            P(None, "tensor"),
            P(None, None, "tensor"),
            P("tensor", None),
            P(),
            P(None, "tensor"),
            P("tensor", None),
            P("expert", None, "tensor"),
            P("expert", "tensor", None),
            P(),
        ),
        check_vma=False,
    )
```

```python
import functools
import math

import jax
import jax.numpy as jnp
from jax import lax
from jax.experimental import pallas as pl
from jax.experimental.pallas import tpu as pltpu
from jax.sharding import PartitionSpec as P

HD = 64
EXPERTS = 8
TOPK = 2
PATCHES = 256
CAP = 80
EXTRA = 16
EPSILON = 1e-06
HALF = 4
FULL_LIMIT = 32 * 1024 * 1024
VMEM_LIMIT = 63 * 1024 * 1024

f32 = jnp.float32
bf16 = jnp.bfloat16
NN = (((1,), (0,)), ((), ()))
NT = (((1,), (1,)), ((), ()))
TN = (((0,), (0,)), ((), ()))
TT = (((0,), (1,)), ((), ()))


def mm(left, right, dims):
    return lax.dot_general(left, right, dims, preferred_element_type=f32)


def normalize(values):
    center = jnp.mean(values, axis=-1, keepdims=True)
    shifted = values - center
    inverse = lax.rsqrt(jnp.mean(shifted * shifted, axis=-1, keepdims=True) + EPSILON)
    return (shifted * inverse, inverse)


def normalize_back(normed, inverse, upstream):
    return inverse * (
        upstream
        - jnp.mean(upstream, axis=-1, keepdims=True)
        - normed * jnp.mean(upstream * normed, axis=-1, keepdims=True)
    )


def embedding(steps, model_width):
    half_width = model_width // 2
    freqs_all = jnp.exp(-math.log(10000.0) * jnp.arange(half_width, dtype=f32) / half_width)
    angles = steps.astype(f32)[:, None] * freqs_all[None, :]
    return jnp.concatenate([jnp.cos(angles), jnp.sin(angles)], axis=1)


def gelu_both(pre):
    const = math.sqrt(2.0 / math.pi)
    square = pre * pre
    tanh = jnp.tanh(const * pre * (1.0 + 0.044715 * square))
    half = 0.5 + 0.5 * tanh
    value = pre * half
    return value, half + value * (1.0 - tanh) * (const + 3.0 * 0.044715 * const * square)


def launch(
    kernel, name, outs, operands, *, in_specs=None, out_specs=None, grid=(), scalars=(), scratch=(), aliases=None,
    after=(), flops=0, moved=0,
):
    lead = len(scalars)
    count = lead + len(operands)
    waits = len(after)
    on_chip = pl.BlockSpec(memory_space=pltpu.VMEM)
    anywhere = pl.BlockSpec(memory_space=pl.ANY)
    in_specs = list(in_specs or [on_chip] * len(operands)) + [anywhere] * waits
    out_specs = tuple(out_specs or [on_chip] * len(outs))

    def body(*refs):
        kernel(*refs[:count], *refs[count + waits :])

    if scalars and grid:
        shape = dict(
            grid_spec=pltpu.PrefetchScalarGridSpec(
                num_scalar_prefetch=lead, grid=grid, in_specs=in_specs, out_specs=out_specs, scratch_shapes=scratch
            )
        )
    else:
        in_specs = [pl.BlockSpec(memory_space=pltpu.SMEM)] * lead + in_specs
        shape = dict(grid=grid, in_specs=in_specs, out_specs=out_specs, scratch_shapes=scratch)
    return pl.pallas_call(
        body,
        out_shape=tuple(jax.ShapeDtypeStruct(*out) for out in outs),
        input_output_aliases=aliases or {},
        compiler_params=pltpu.CompilerParams(vmem_limit_bytes=VMEM_LIMIT),
        cost_estimate=pl.CostEstimate(flops=int(flops), bytes_accessed=int(moved), transcendentals=0),
        name=name,
        **shape,
    )(*scalars, *operands, *after)


def copy_kernel(plan, count, *refs):
    sources, out, sems = refs[:count], refs[-2], refs[-1]
    copies = [
        pltpu.make_async_copy(sources[index].at[take], out.at[put], sems.at[order])
        for order, (index, take, put) in enumerate(plan)
    ]
    for copy in copies:
        copy.start()
    for copy in copies:
        copy.wait()


def assemble(shape, dtype, sources, plan, after=()):
    size = math.prod(shape) * jnp.dtype(dtype).itemsize
    return launch(
        functools.partial(copy_kernel, plan, len(sources)), "assemble", [(shape, dtype)], sources,
        in_specs=[pl.BlockSpec(memory_space=pl.ANY)] * len(sources),
        scratch=[pltpu.SemaphoreType.DMA((len(plan),))], after=after, moved=2 * size,
    )[0]


def order_kernel(*refs):
    pass


def ordered(values, after):
    anywhere = [pl.BlockSpec(memory_space=pl.ANY)] * len(values)
    return launch(
        order_kernel, "ordered", [(value.shape, value.dtype) for value in values], values, in_specs=anywhere,
        out_specs=anywhere, aliases={index: index for index in range(len(values))}, after=after,
    )


def pair_masks(rows):
    lane = lax.broadcasted_iota(jnp.int32, (rows, 2 * HD), 1)
    return (lane < HD, lane >= HD)


def head_probs(query, key):
    scores = mm(query, key, NT) * (1.0 / math.sqrt(HD))
    weights = jnp.exp(scores - jnp.max(scores, axis=-1, keepdims=True))
    return weights / jnp.sum(weights, axis=-1, keepdims=True)


def shard_rows(shards, part, local_width):
    return jnp.concatenate(
        [shard[part * local_width : (part + 1) * local_width, :] for shard in shards], axis=0
    )


def attention_kernel(
    local_width, tok_ref, mod_ref, router_ref, pairs_ref, w0, w1, w2, w3,
    attn_in_ref, qkv_ref, context_ref, attn_out_ref, ext_ref, column_ref,
):
    shards = (w0, w1, w2, w3)
    rows, width = tok_ref.shape
    mod = mod_ref[...]
    stream = tok_ref[...].astype(f32)
    attn_in = (normalize(stream)[0] * (1.0 + mod[1:2]) + mod[0:1]).astype(bf16)
    attn_in_ref[...] = attn_in
    for part in range(3):
        qkv_ref[part] = mm(attn_in, shard_rows(shards, part, local_width), NT).astype(bf16)
    masks = pair_masks(rows)
    zero = jnp.zeros((rows, 2 * HD), bf16)
    for pair in range(width // (2 * HD)):
        cols = slice(pair * 2 * HD, (pair + 1) * 2 * HD)
        query, key, value = qkv_ref[0, :, cols], qkv_ref[1, :, cols], qkv_ref[2, :, cols]
        parts = []
        for mask in masks:
            probs = head_probs(jnp.where(mask, query, zero), key)
            parts.append(mm(probs.astype(bf16), value, NN))
        context_ref[:, cols] = jnp.where(masks[0], parts[0], parts[1]).astype(bf16)
    attn_out = mm(context_ref[...], shard_rows(shards, 3, local_width), NN)
    attn_out_ref[...] = attn_out
    residual = stream + mod[2:3] * attn_out
    moe_in = (normalize(residual)[0] * (1.0 + mod[4:5]) + mod[3:4]).astype(bf16)
    ext_ref[0:rows, :] = moe_in
    logits = mm(router_ref[...], moe_in, NT)
    pairs = pairs_ref[...]
    expert_id = lax.broadcasted_iota(jnp.int32, (EXPERTS, rows), 0)
    chosen = [
        jnp.sum(jnp.where(expert_id == pairs[k : k + 1], logits, 0.0), axis=0, keepdims=True)
        for k in range(TOPK)
    ]
    top = jnp.maximum(chosen[0], chosen[1])
    powers = [jnp.exp(value - top) for value in chosen]
    gates = [power / (powers[0] + powers[1]) for power in powers]
    high = [gate.astype(bf16).astype(f32) for gate in gates]
    rest = [gate - upper for gate, upper in zip(gates, high)]
    values = pairs.astype(f32)
    packed = (
        jnp.concatenate([values[0:1], values[1:2], values[2:3]], axis=1),
        jnp.concatenate([values[3:4], high[0], high[1]], axis=1),
        jnp.concatenate([rest[0], rest[1], jnp.zeros_like(rest[0])], axis=1),
    )
    row_id = lax.broadcasted_iota(jnp.int32, (EXTRA, width), 0)
    extra = jnp.zeros((EXTRA, width), f32)
    for index, line in enumerate(packed):
        extra = jnp.where(row_id == index, line, extra)
    ext_ref[rows : rows + EXTRA, :] = extra.astype(bf16)
    for copy in range(column_ref.shape[0]):
        column_ref[copy] = ext_ref[...]


def attention_forward(tokens, mod, router_t, pairs, shards, local_width, copies):
    rows, width = tokens.shape
    outs = [
        ((rows, width), bf16),
        ((3, rows, width), bf16),
        ((rows, width), bf16),
        ((rows, width), f32),
        ((rows + EXTRA, width), bf16),
        ((copies, rows + EXTRA, width), bf16),
    ]
    return launch(
        functools.partial(attention_kernel, local_width), "attention_forward", outs,
        [tokens, mod, router_t, pairs, *shards], flops=5 * 10**9, moved=9 * 10**6,
    )


def read_pairs(extra):
    info = extra.astype(f32)
    count = PATCHES
    routes = (info[0:1, 0:count], info[0:1, count : 2 * count])
    places = (info[0:1, 2 * count : 3 * count], info[1:2, 0:count])
    gates = (
        info[1:2, count : 2 * count] + info[2:3, 0:count],
        info[1:2, 2 * count : 3 * count] + info[2:3, count : 2 * count],
    )
    return routes, places, gates


def slot_hits(routes, places, base, slots):
    slot_id = lax.broadcasted_iota(jnp.int32, (slots, PATCHES), 0).astype(f32)
    return [
        slot_id == jnp.where(place < CAP, (route - base) * CAP + place, -1.0)
        for route, place in zip(routes, places)
    ]


def slot_gates(hits, gates):
    return jnp.sum(
        jnp.where(hits[0], gates[0], 0.0) + jnp.where(hits[1], gates[1], 0.0), axis=1, keepdims=True
    )


class Blocks:
    def __init__(self, rows, rows_at, extra_at, cots, cots_at):
        self.rows, self.rows_at, self.extra_at, self.cots, self.cots_at = rows, rows_at, extra_at, cots, cots_at

    @classmethod
    def apart(cls, ext, cots):
        return cls(ext, 0, PATCHES // EXTRA, cots, 0)

    def operands(self):
        return [self.rows, self.rows, self.cots]

    def specs(self, taken=HALF):
        width = self.rows.shape[2]
        places = ((PATCHES, self.rows_at), (EXTRA, self.extra_at), (PATCHES, self.cots_at))
        return [
            pl.BlockSpec((taken, count, width), lambda *_, at=at: (0, at, 0)) for count, at in places
        ]

    def extra(self):
        return self.rows[:, self.extra_at * EXTRA : (self.extra_at + 1) * EXTRA]


def dispatch_kernel(base_ref, *refs):
    rows_ref, cots_ref = refs[-2:]
    members = rows_ref.shape[0]
    base = base_ref[0].astype(f32)
    for part in range(2):
        rows_in, extra_in, cots_in = refs[3 * part : 3 * part + 3]

        @pl.when(pl.program_id(0) == part)
        def _():
            for block in range(HALF):
                dispatch_block(
                    base, members, rows_in[block], extra_in[block], cots_in[block], rows_ref, cots_ref, block
                )


def dispatch_block(base, members, rows, extra, cots, rows_ref, cots_ref, block):
    routes, places, gates = read_pairs(extra)
    hits = slot_hits(routes, places, base, members * CAP)
    hot = (hits[0] | hits[1]).astype(bf16)
    picked = mm(hot, rows, NN).astype(bf16)
    scaled = (mm(hot, cots, NN) * slot_gates(hits, gates)).astype(bf16)
    for member in range(members):
        span = slice(member * CAP, (member + 1) * CAP)
        rows_ref[member, block * CAP : (block + 1) * CAP, :] = picked[span]
        cots_ref[member, block * CAP : (block + 1) * CAP, :] = scaled[span]


def hops_kernel(base_ref, ext, cots, rows_ref, cots_ref):
    base = base_ref[0].astype(f32)
    for block in range(ext.shape[0]):
        dispatch_block(
            base, rows_ref.shape[0], ext[block, 0, :PATCHES], ext[block, 0, PATCHES:], cots[block, 0], rows_ref,
            cots_ref, block,
        )


def dispatch_hops(base, ext, cots, members, after=()):
    blocks, hops, rows, width = ext.shape
    out = ((members, hops * blocks * CAP, width), bf16)
    out_spec = pl.BlockSpec((members, blocks * CAP, width), lambda h, b: (0, h, 0))
    specs = [pl.BlockSpec((blocks, 1, count, width), lambda h, b: (0, h, 0, 0)) for count in (rows, PATCHES)]
    return launch(
        hops_kernel, "dispatch_hops", [out, out], [ext, cots], in_specs=specs, out_specs=[out_spec, out_spec],
        grid=(hops,), scalars=[base], after=after, flops=24 * 10**9, moved=48 * 10**6,
    )


def pick_kernel(place_ref, source, out):
    planes = source.shape[0]
    for hop in range(planes - 1):
        out[hop] = source[lax.rem(place_ref[2] + hop + 1, planes)]


def pick_both_kernel(place_ref, *refs):
    sources, column, rest, stack, sems = refs[:HALF], refs[HALF], refs[-3], refs[-2], refs[-1]
    planes = column.shape[0]
    copies = [
        pltpu.make_async_copy(column.at[lax.rem(place_ref[2] + hop + 1, planes)], rest.at[hop], sems.at[hop])
        for hop in range(planes - 1)
    ]
    copies += [
        pltpu.make_async_copy(source, stack.at[index], sems.at[planes - 1 + index])
        for index, source in enumerate(sources)
    ]
    for copy in copies:
        copy.start()
    for copy in copies:
        copy.wait()


def dispatch(base, blocks, members, after=()):
    width = blocks[0].rows.shape[2]
    out = ((members, 2 * HALF * CAP, width), bf16)
    out_spec = pl.BlockSpec((members, HALF * CAP, width), lambda c, *_: (0, c, 0))
    return launch(
        dispatch_kernel, "dispatch", [out, out], [operand for part in blocks for operand in part.operands()],
        in_specs=[spec for part in blocks for spec in part.specs()], out_specs=[out_spec, out_spec],
        grid=(2,), scalars=[base], after=after, flops=8 * 10**9, moved=16 * 10**6,
    )


def expert_kernel(
    shared_ids, base_ref, rows0, extra0, cots0, rows1, extra1, cots1, sup_ref, sdown_ref, eup_ref, edown_ref,
    first_ref, second_ref, rows_s, cots_s, gate_s, dot_s, shared_s,
):
    step = pl.program_id(0)
    members = rows_s.shape[0]
    width = sup_ref.shape[0]
    base = base_ref[0].astype(f32)
    halves = ((rows0, extra0, cots0), (rows1, extra1, cots1))
    total_rows = 2 * HALF * CAP

    def hits_of(half, place):
        routes, places, gates = read_pairs(halves[half][1][place])
        return slot_hits(routes, places, base, members * CAP), gates

    def start_of(half, place):
        return pl.multiple_of((half * HALF + place) * CAP, CAP)

    def per_block(count, body, first=0):
        for half in range(2):
            lax.fori_loop(first, count, lambda place, _, half=half: (body(half, place), 0)[1], 0)

    @pl.when(step == 0)
    def _():
        def send(half, place):
            rows_in, _, cots_in = halves[half]
            hits, gates = hits_of(half, place)
            hot = (hits[0] | hits[1]).astype(bf16)
            picked = mm(hot, rows_in[place], NN).astype(bf16)
            cots = mm(hot, cots_in[place], NN).astype(bf16)
            gate = slot_gates(hits, gates)
            rows = pl.ds(start_of(half, place), CAP)
            for member in range(members):
                span = slice(member * CAP, (member + 1) * CAP)
                rows_s[member, rows, :] = picked[span]
                cots_s[member, rows, :] = cots[span]
                gate_s[member, rows, :] = gate[span]

        per_block(HALF, send)
        for start in range(0, len(shared_ids), 2):
            pair = shared_ids[start : start + 2]
            inputs = jnp.concatenate([halves[b // HALF][0][b % HALF] for b in pair], axis=0)
            cots = jnp.concatenate([halves[b // HALF][2][b % HALF] for b in pair], axis=0)
            value, slope = gelu_both(mm(inputs, sup_ref[...], NN))
            pre_grad = (mm(cots, sdown_ref[...], NT) * slope).astype(bf16)
            result = mm(value.astype(bf16), sdown_ref[...], NN)
            back = mm(pre_grad, sup_ref[...], NT)
            for place in range(len(pair)):
                span = slice(place * PATCHES, (place + 1) * PATCHES)
                shared_s[start + place, :, 0:width] = result[span]
                shared_s[start + place, :, width:] = back[span]

    @pl.when(step > 0)
    def _():
        member = step - 1
        tile = total_rows // 2

        for part in range(2):
            span = slice(part * tile, (part + 1) * tile)
            inputs, cots, gate = rows_s[member, span, :], cots_s[member, span, :], gate_s[member, span, :]
            value, slope = gelu_both(mm(inputs, eup_ref[0], NN))
            act_grad = mm(cots, edown_ref[0], NT)
            dot_s[member, span, :] = jnp.sum(value * act_grad, axis=1, keepdims=True)
            active = (gate * value).astype(bf16)
            pre_grad = (gate * act_grad * slope).astype(bf16)
            rows_s[member, span, :] = mm(active, edown_ref[0], NN).astype(bf16)
            cots_s[member, span, :] = mm(pre_grad, eup_ref[0], NT).astype(bf16)

    @pl.when(step == members)
    def _():
        per_half = [sum(1 for b in shared_ids if b // HALF == half) for half in range(2)]

        def combine(half, place, shared):
            out_ref = (first_ref, second_ref)[half]
            hits, _ = hits_of(half, place)
            hot = (hits[0] | hits[1]).astype(bf16)
            span = pl.ds(start_of(half, place), CAP)
            dots = jnp.concatenate([dot_s[m, span, :] for m in range(members)], axis=0)
            sums = [jnp.sum(jnp.where(hit, dots, 0.0), axis=0, keepdims=True) for hit in hits]
            line = jnp.concatenate(sums + [jnp.zeros_like(sums[0])], axis=1)
            row_id = lax.broadcasted_iota(jnp.int32, (EXTRA, width), 0)
            out_ref[place, 2 * PATCHES :, :] = jnp.where(row_id == 0, line, 0.0).astype(bf16)
            for index, source in enumerate((rows_s, cots_s)):
                slots = jnp.concatenate([source[m, span, :] for m in range(members)], axis=0)
                total = mm(hot, slots, TN)
                if shared:
                    where = half * per_half[0] + place
                    total = total + shared_s[where, :, index * width : (index + 1) * width]
                out_ref[place, index * PATCHES : (index + 1) * PATCHES, :] = total.astype(bf16)

        for half in range(2):
            for first, last, shared in ((0, per_half[half], True), (per_half[half], HALF, False)):
                if last > first:
                    lax.fori_loop(
                        first, last,
                        lambda place, _, half=half, shared=shared: (combine(half, place, shared), 0)[1], 0,
                    )


def experts_both(base, blocks, shared_up, shared_down, expert_up, expert_down, shared_ids, after=()):
    members, width, hidden = expert_up.shape
    shape = (HALF, 2 * PATCHES + EXTRA, width)
    out_spec = pl.BlockSpec(shape, lambda e, b: (0, 0, 0))
    slots = (members, 2 * HALF * CAP)
    return launch(
        functools.partial(expert_kernel, shared_ids), "experts_both", [(shape, bf16)] * 2,
        [operand for part in blocks for operand in part.operands()]
        + [shared_up, shared_down, expert_up, expert_down],
        in_specs=[spec for part in blocks for spec in part.specs()]
        + [
            pl.BlockSpec((width, hidden), lambda e, b: (0, 0)),
            pl.BlockSpec((hidden, width), lambda e, b: (0, 0)),
            pl.BlockSpec((1, width, hidden), lambda e, b: (jnp.maximum(e - 1, 0), 0, 0)),
            pl.BlockSpec((1, hidden, width), lambda e, b: (jnp.maximum(e - 1, 0), 0, 0)),
        ],
        out_specs=[out_spec, out_spec],
        grid=(members + 1,),
        scalars=[base],
        after=after,
        scratch=[
            pltpu.VMEM((*slots, width), bf16),
            pltpu.VMEM((*slots, width), bf16),
            pltpu.VMEM((*slots, 1), f32),
            pltpu.VMEM((*slots, 1), f32),
            pltpu.VMEM((max(len(shared_ids), 1), PATCHES, 2 * width), f32),
        ], flops=30 * 10**9, moved=30 * 10**6,
    )


def both_grads(inputs, cots, up, down):
    value, slope = gelu_both(mm(up, inputs, TT))
    pre_grad = (mm(down, cots, NT) * slope).astype(bf16)
    return mm(inputs, pre_grad, TT), mm(value.astype(bf16), cots, NN)


def grads_kernel(count, tile, started, *refs):
    row_refs, cot_refs = refs[:count], refs[count : 2 * count]
    up_ref, down_ref = refs[2 * count : 2 * count + 2]
    up_grad_ref, down_grad_ref = refs[-2:]
    width = up_ref.shape[1]
    inputs = [ref[...].reshape(-1, width) for ref in row_refs]
    cots = [ref[...].reshape(-1, width) for ref in cot_refs]
    groups = max(1, count * inputs[0].shape[0] // tile)
    each = count // groups
    for group in range(groups):
        part = slice(group * each, (group + 1) * each)
        rows, cot = jnp.concatenate(inputs[part], axis=0), jnp.concatenate(cots[part], axis=0)
        up_grad, down_grad = both_grads(rows, cot, up_ref[0], down_ref[0])
        if group == 0 and started:
            up_grad_ref[0] = refs[2 * count + 2][0] + up_grad
            down_grad_ref[0] = refs[2 * count + 3][0] + down_grad
        elif group == 0:
            up_grad_ref[0] = up_grad
            down_grad_ref[0] = down_grad
        else:
            up_grad_ref[0] += up_grad
            down_grad_ref[0] += down_grad


def shared_other_kernel(rows, cots, up, down, up_before, down_before, up_out, down_out, low_out):
    width = up.shape[0]
    grads = both_grads(rows[...].reshape(-1, width), cots[...].reshape(-1, width), up[...], down[...])
    step = pl.program_id(0)
    for grad, before, out in zip(grads, (up_before, down_before), (up_out, down_out)):

        @pl.when(step == 0)
        def _():
            out[...] = before[0] + grad

        @pl.when(step > 0)
        def _():
            out[...] += grad

    @pl.when(step == pl.num_programs(0) - 1)
    def _():
        low_out[0] = up_out[...].astype(bf16)
        low_out[1] = down_out[...].astype(bf16)


def weight_grads(rows, cots, specs, up, down, before, tile, total, after=(), span=None):
    members, width, hidden = up.shape
    start, stop = span or (0, members)
    up_spec = pl.BlockSpec((1, width, hidden), lambda e: (e + start, 0, 0))
    down_spec = pl.BlockSpec((1, hidden, width), lambda e: (e + start, 0, 0))
    started = before is not None
    count = len(rows)
    first = 2 * count + 2
    return launch(
        functools.partial(grads_kernel, count, tile, started), "weight_grads", [(up.shape, f32), (down.shape, f32)],
        [*rows, *cots, up, down, *(before or ())],
        in_specs=specs + [up_spec, down_spec] * (2 if started else 1), out_specs=[up_spec, down_spec],
        grid=(stop - start,), aliases={first: 0, first + 1: 1} if started else None, after=after,
        flops=12 * total * width * hidden, moved=total * width * 4,
    )


def routed_grads(slots, up, down, before, after=(), span=None):
    members, count, width = slots[0][0].shape
    start, stop = span or (0, members)
    spec = pl.BlockSpec((1, count, width), lambda e: (e + start, 0, 0))
    rows, cots = [pair[0] for pair in slots], [pair[1] for pair in slots]
    specs = [spec] * (2 * len(slots))
    each = len(slots) * count
    return weight_grads(
        rows, cots, specs, up, down, before, each, (stop - start) * each, after=after, span=span
    )


def shared_grads(blocks, taken, up, down, before, after=()):
    rows, cots = [part.rows for part in blocks], [part.cots for part in blocks]
    all_specs = [part.specs(taken) for part in blocks]
    specs = [spec[0] for spec in all_specs] + [spec[2] for spec in all_specs]
    total = len(blocks) * taken * PATCHES
    tile = total if total <= 8 * PATCHES else total // 2
    return weight_grads(rows, cots, specs, up[None], down[None], before, tile, total, after)


def shared_grads_other(ext, cots, hop, up, down, before, after=()):
    blocks, _, _, width = ext.shape
    steps = 2
    spec = pl.BlockSpec((blocks // steps, 1, PATCHES, width), lambda t: (t, hop, 0, 0))
    up_spec = pl.BlockSpec(up.shape, lambda t: (0, 0))
    down_spec = pl.BlockSpec(down.shape, lambda t: (0, 0))
    before_specs = [pl.BlockSpec((1, *part.shape), lambda t: (0, 0, 0)) for part in (up, down)]
    low = (2, *up.shape)
    total = blocks * PATCHES
    return launch(
        shared_other_kernel, "shared_grads_other", [(up.shape, f32), (down.shape, f32), (low, bf16)],
        [ext, cots, up, down, *before], in_specs=[spec, spec, up_spec, down_spec] + before_specs,
        out_specs=[up_spec, down_spec, pl.BlockSpec(low, lambda t: (0, 0, 0))],
        grid=(steps,), after=after, flops=12 * total * up.size, moved=total * width * 4,
    )


def shared_last_kernel(up, down, more, up_out, down_out):
    up_out[...] = up[...] + more[0].astype(f32)
    down_out[...] = down[...] + more[1].astype(f32)


def backward_kernel(
    local_width, moe_ref, moe_more_ref, back_ref, back_more_ref, cond_ref, tok_ref, cot_ref, mod_ref, router_ref, pairs_ref, attn_in_ref,
    qkv_ref, context_ref, attn_out_ref, ext_ref, w0, w1, w2, w3,
    output_ref, tok_grad_ref, small_ref, near_ref, far_ref, grad_s,
):
    def put_weight_grad(first, grad):
        for index in range(len(shards)):
            out_ref = (near_ref, far_ref)[index % 2]
            out_ref[index // 2, first : first + local_width, :] = grad[
                index * local_width : (index + 1) * local_width
            ]

    shards = (w0, w1, w2, w3)
    rows, width = tok_ref.shape
    mod = mod_ref[...]
    stream = tok_ref[...].astype(f32)
    attn_out = attn_out_ref[...]
    residual = stream + mod[2:3] * attn_out
    second_norm, second_inv = normalize(residual)
    moe_out = moe_ref[...] + moe_more_ref[...].astype(f32)
    back = back_ref[...] + back_more_ref[...].astype(f32)
    upstream = cot_ref[...].astype(f32)
    output_ref[...] = (residual + mod[5:6] * moe_out).astype(bf16)
    gate_two_grad = jnp.sum(upstream * moe_out, axis=0, keepdims=True)
    routes, places, gates = read_pairs(ext_ref[rows:, :])
    dots = (back[rows : rows + 1, 0:PATCHES], back[rows : rows + 1, PATCHES : 2 * PATCHES])
    mean_dot = gates[0] * dots[0] + gates[1] * dots[1]
    pairs = pairs_ref[...]
    expert_id = lax.broadcasted_iota(jnp.int32, (EXPERTS, rows), 0)
    logits_grad = jnp.zeros((EXPERTS, rows), f32)
    for k in range(TOPK):
        logits_grad += jnp.where(expert_id == pairs[k : k + 1], gates[k] * (dots[k] - mean_dot), 0.0)
    logits_grad = logits_grad.astype(bf16)
    moe_in_grad = back[0:rows] + mm(logits_grad, router_ref[...], TN)
    shift_two_grad = jnp.sum(moe_in_grad, axis=0, keepdims=True)
    scale_two_grad = jnp.sum(moe_in_grad * second_norm, axis=0, keepdims=True)
    residual_grad = upstream + normalize_back(
        second_norm, second_inv, moe_in_grad * (1.0 + mod[4:5])
    )
    gate_one_grad = jnp.sum(residual_grad * attn_out, axis=0, keepdims=True)
    attn_grad = (mod[2:3] * residual_grad).astype(bf16)
    out_grad = mm(context_ref[...], attn_grad, TN).astype(bf16)
    put_weight_grad(3 * local_width, out_grad)
    context_grad = mm(attn_grad, shard_rows(shards, 3, local_width), NT).astype(bf16)
    masks = pair_masks(rows)
    zero = jnp.zeros((rows, 2 * HD), bf16)
    scale = 1.0 / math.sqrt(HD)
    for pair in range(width // (2 * HD)):
        cols = slice(pair * 2 * HD, (pair + 1) * 2 * HD)
        query, key, value = qkv_ref[0, :, cols], qkv_ref[1, :, cols], qkv_ref[2, :, cols]
        upper = context_grad[:, cols]
        sums = []
        for mask in masks:
            probs = head_probs(jnp.where(mask, query, zero), key)
            probs_grad = mm(jnp.where(mask, upper, zero), value, NT)
            value_grad = mm(probs.astype(bf16), upper, TN)
            score_grad = (
                probs * (probs_grad - jnp.sum(probs_grad * probs, axis=-1, keepdims=True))
            ).astype(bf16)
            sums.append((mm(score_grad, key, NN) * scale, mm(score_grad, query, TN) * scale, value_grad))
        for part in range(3):
            grad_s[part, :, cols] = jnp.where(masks[0], sums[0][part], sums[1][part]).astype(bf16)
    attn_in = attn_in_ref[...]
    attn_in_grad = jnp.zeros((rows, width), f32)
    for part in range(3):
        grad = grad_s[part]
        attn_in_grad += mm(grad, shard_rows(shards, part, local_width), NN)
        put_weight_grad(part * local_width, mm(grad, attn_in, TN).astype(bf16))
    first_norm, first_inv = normalize(stream)
    shift_one_grad = jnp.sum(attn_in_grad, axis=0, keepdims=True)
    scale_one_grad = jnp.sum(attn_in_grad * first_norm, axis=0, keepdims=True)
    tok_grad_ref[...] = residual_grad + normalize_back(
        first_norm, first_inv, attn_in_grad * (1.0 + mod[1:2])
    )
    lines = (
        shift_one_grad, scale_one_grad, gate_one_grad, shift_two_grad, scale_two_grad, gate_two_grad,
        cond_ref[...],
    )
    row_id = lax.broadcasted_iota(jnp.int32, (8, width), 0)
    stacked = jnp.zeros((8, width), f32)
    for index, line in enumerate(lines):
        stacked = jnp.where(row_id == index, line, stacked)
    small_ref[0:8, :] = stacked
    small_ref[8:16, :] = mm(logits_grad, ext_ref[0:rows, :], NN)


def attention_backward(
    moe, moe_more, back, back_more, cond, tokens, cotangent, mod, router_t, pairs, attn_in, qkv, context,
    attn_out, ext, shards, local_width, after=(),
):
    rows, width = tokens.shape
    halves = ((len(shards) // 2, 4 * local_width, width), bf16)
    return launch(
        functools.partial(backward_kernel, local_width), "attention_backward",
        [((rows, width), bf16), ((rows, width), f32), ((16, width), f32), halves, halves],
        [
            moe, moe_more, back, back_more, cond, tokens, cotangent, mod, router_t, pairs, attn_in, qkv,
            context, attn_out, ext, *shards,
        ],
        scratch=[pltpu.VMEM((3, rows, width), bf16)], after=after, flops=10 * 10**9, moved=16 * 10**6,
    )


def take_all(copies):
    for copy in copies:
        copy.start()
    for copy in copies:
        copy.wait()


def plane_first_kernel(first, more, side, other, upper_s, lower_s, sems):
    cut = PATCHES
    low = first.shape[1] - cut
    copies = []
    for index, source in enumerate((first, more)):
        for place, (upper, lower) in enumerate(((1, 2), (3, 3))):
            at = 4 * index + 2 * place
            copies += [
                pltpu.make_async_copy(source.at[upper, pl.ds(0, cut)], upper_s.at[index, place], sems.at[at]),
                pltpu.make_async_copy(source.at[lower, pl.ds(cut, low)], lower_s.at[index, place], sems.at[at + 1]),
            ]
    take_all(copies)
    side[...] = (upper_s[0].astype(f32) + upper_s[1].astype(f32)).astype(bf16)
    other[...] = (lower_s[0].astype(f32) + lower_s[1].astype(f32)).astype(bf16)


def plane_second_kernel(first, more, side, other, upper, lower, upper_next, lower_next, upper_s, lower_s, sems):
    cut = PATCHES
    low = first.shape[1] - cut
    copies = []
    for index, source in enumerate((first, more)):
        for place, (up, down) in enumerate(((0, 0), (2, 1))):
            at = 4 * index + 2 * place
            copies += [
                pltpu.make_async_copy(source.at[up, pl.ds(0, cut)], upper_s.at[index, place], sems.at[at]),
                pltpu.make_async_copy(source.at[down, pl.ds(cut, low)], lower_s.at[index, place], sems.at[at + 1]),
            ]
    take_all(copies)
    uppers = [upper_s[0, p].astype(f32) + upper_s[1, p].astype(f32) + side[p].astype(f32) for p in range(2)]
    lowers = [lower_s[0, p].astype(f32) + lower_s[1, p].astype(f32) + other[p].astype(f32) for p in range(2)]
    upper[...] = uppers[0]
    upper_next[...] = uppers[1].astype(bf16)
    lower[...] = lowers[0]
    lower_next[...] = lowers[1].astype(bf16)


def span_of(index, size):
    return pl.ds(pl.multiple_of(index * size, size), size)


def dense_copies(near, more, index, who, whole_s, half_s, sems):
    cut = whole_s.shape[1]
    half = half_s.shape[2]
    rows = pl.ds(pl.multiple_of(cut + who * half, half), half)
    copies = []
    for term, source in enumerate((near, more)):
        copies.append(pltpu.make_async_copy(source.at[index, pl.ds(0, cut)], whole_s.at[term], sems.at[3 * term]))
        for shard in range(2):
            copies.append(
                pltpu.make_async_copy(source.at[shard, rows], half_s.at[term, shard], sems.at[3 * term + 1 + shard])
            )
    take_all(copies)


def dense_first_kernel(place, near, more, side, other, whole_s, half_s, sems):
    dense_copies(near, more, 1, 1 - place[0], whole_s, half_s, sems)
    side[...] = (whole_s[0].astype(f32) + whole_s[1].astype(f32)).astype(bf16)
    other[...] = (half_s[0].astype(f32) + half_s[1].astype(f32)).astype(bf16)


def dense_second_kernel(place, near, more, from_side, from_other, side, other, upper, lower, whole_s, half_s, sems):
    mine = place[0]
    dense_copies(near, more, 0, mine, whole_s, half_s, sems)
    half = upper.shape[0]
    for out, who in ((upper, mine), (other, 1 - mine)):
        rows = span_of(who, half)
        total = whole_s[0, rows, :].astype(f32) + whole_s[1, rows, :].astype(f32) + from_side[rows, :].astype(f32)
        out[...] = total.astype(out.dtype)
    total = half_s[0].astype(f32) + half_s[1].astype(f32) + from_other[...].astype(f32)
    lower[...] = total[0]
    side[...] = total[1].astype(bf16)


def dense_third_kernel(size, place, upper, lower, from_side, from_other, own, *outs):
    sent, total = outs[:-1], outs[-1]
    half = upper.shape[0]
    share = 2 * half // size
    total[0:half, :] = upper[...] + from_other[...].astype(f32)
    total[half:, :] = lower[...] + from_side[...].astype(f32)
    own[...] = total[span_of(place[1], share), :]
    for hop in range(1, size):
        sent[hop - 1][...] = total[span_of(lax.rem(place[1] + hop, size), share), :].astype(bf16)


def dense_fourth_kernel(own, *refs):
    out = refs[-1]
    total = own[...]
    for ref in refs[:-1]:
        total = total + ref[...].astype(f32)
    out[...] = total.astype(bf16)


def dense_fifth_kernel(size, place, own, *refs):
    out = refs[-1]
    share = own.shape[0]
    out[span_of(place[1], share), :] = own[...]
    for hop in range(1, size):
        out[span_of(lax.rem(place[1] + size - hop, size), share), :] = refs[hop - 1][...]


def dense_last_kernel(place, own, more, qkv_out, out_out, total):
    half = own.shape[0] // 2
    for ref, who in ((own, place[0]), (more, 1 - place[0])):
        for index in range(2):
            rows = pl.ds(pl.multiple_of(2 * half * index + who * half, half), half)
            total[rows, :] = ref[index * half : (index + 1) * half, :].astype(f32)
    count = qkv_out.shape[0]
    qkv_out[...] = total[0:count, :]
    out_out[...] = total[count:, :]


class Links:
    def __init__(self, mesh):
        self.dp, self.expert, self.tensor = (mesh.shape[name] for name in ("dp", "expert", "tensor"))
        self.paired = self.expert == 2 and self.tensor == 4
        self.core = [(i, i ^ 1) for i in range(self.tensor)]
        self.side = [(i, i ^ 2) for i in range(self.tensor)]
        self.other = [(0, 1), (1, 0)]

    def to_core(self, value):
        return lax.ppermute(value, "tensor", self.core)

    def to_side(self, value):
        return lax.ppermute(value, "tensor", self.side)

    def to_other(self, value):
        return lax.ppermute(value, "expert", self.other)

    def to_next(self, value):
        return lax.ppermute(value, "dp", [(i, i ^ 1) for i in range(self.dp)])

    def along(self, value, hop):
        return lax.ppermute(value, "dp", [(i, (i + hop) % self.dp) for i in range(self.dp)])

    def column(self, copies):
        return lax.all_to_all(copies, "dp", split_axis=0, concat_axis=0)

    def column_rest(self, column, place, after):
        planes, rows, width = column.shape
        (rest,) = launch(
            pick_kernel, "pick", [((planes - 1, rows, width), column.dtype)], [column], scalars=[place], after=after,
            moved=3 * 10**6,
        )
        return rest, lax.all_gather(rest, ("expert", "tensor"), axis=0)

    def plane_sum_first(self, first, more, after):
        width = first.shape[2]
        low = first.shape[1] - PATCHES
        return launch(
            plane_first_kernel, "plane_first", [((2, PATCHES, width), bf16), ((2, low, width), bf16)],
            [first, more], in_specs=[pl.BlockSpec(memory_space=pl.ANY)] * 2,
            scratch=[
                pltpu.VMEM((2, 2, PATCHES, width), bf16),
                pltpu.VMEM((2, 2, low, width), bf16),
                pltpu.SemaphoreType.DMA((8,)),
            ],
            after=after, moved=5 * 10**6,
        )

    def plane_sum_second(self, first, more, side, other, after):
        width = first.shape[2]
        low = first.shape[1] - PATCHES
        return launch(
            plane_second_kernel, "plane_second",
            [((PATCHES, width), f32), ((low, width), f32), ((PATCHES, width), bf16), ((low, width), bf16)],
            [first, more, side, other],
            in_specs=[pl.BlockSpec(memory_space=pl.ANY)] * 2 + [pl.BlockSpec(memory_space=pltpu.VMEM)] * 2,
            scratch=[
                pltpu.VMEM((2, 2, PATCHES, width), bf16),
                pltpu.VMEM((2, 2, low, width), bf16),
                pltpu.SemaphoreType.DMA((8,)),
            ],
            after=after, moved=7 * 10**6,
        )

    def dense_sum(self, near, far):
        _, rows, width = near.shape
        cut, half, share = rows // 2, rows // 4, rows // 2 // self.dp
        place = [jnp.stack([lax.axis_index("expert"), lax.axis_index("dp")]).astype(jnp.int32)]
        more = self.to_core(far)
        after = yield None
        anywhere, on_chip = pl.BlockSpec(memory_space=pl.ANY), pl.BlockSpec(memory_space=pltpu.VMEM)
        scratch = [
            pltpu.VMEM((2, cut, width), bf16), pltpu.VMEM((2, 2, half, width), bf16), pltpu.SemaphoreType.DMA((6,)),
        ]
        side, other = launch(
            dense_first_kernel, "dense_first", [((cut, width), bf16), ((2, half, width), bf16)], [near, more],
            in_specs=[anywhere] * 2, scalars=place, scratch=scratch, after=after, moved=4 * 10**6,
        )
        from_side, from_other = self.to_side(side), self.to_other(other)
        after = yield side
        side, other, upper, lower = launch(
            dense_second_kernel, "dense_second",
            [((half, width), bf16), ((half, width), bf16), ((half, width), f32), ((half, width), f32)],
            [near, more, from_side, from_other], in_specs=[anywhere] * 2 + [on_chip] * 2, scalars=place,
            scratch=scratch, after=after, moved=5 * 10**6,
        )
        from_side, from_other = self.to_side(side), self.to_other(other)
        after = yield upper
        hops = range(1, self.dp)
        outs = launch(
            functools.partial(dense_third_kernel, self.dp), "dense_third",
            [((share, width), f32)] + [((share, width), bf16)] * len(hops),
            [upper, lower, from_side, from_other], scalars=place, scratch=[pltpu.VMEM((cut, width), f32)],
            after=after, moved=3 * 10**6,
        )
        moved = [self.along(outs[hop], hop) for hop in hops]
        after = yield outs[0]
        (total,) = launch(
            dense_fourth_kernel, "dense_fourth", [((share, width), bf16)], [outs[0], *moved], after=after,
            moved=10**6,
        )
        moved = [self.along(total, hop) for hop in hops]
        after = yield total
        (column,) = launch(
            functools.partial(dense_fifth_kernel, self.dp), "dense_fifth", [((cut, width), bf16)], [total, *moved],
            scalars=place, after=after, moved=10**6,
        )
        more = self.to_other(column)
        after = yield column
        yield launch(
            dense_last_kernel, "dense_last", [((rows * 3 // 4, width), f32), ((rows // 4, width), f32)],
            [column, more], scalars=place, scratch=[pltpu.VMEM((rows, width), f32)], after=after,
            moved=4 * 10**6,
        )


def local(
    links,
    tokens,
    cotangent,
    timesteps,
    ada_weight,
    ada_bias,
    qkv_weight,
    out_weight,
    router_weight,
    shared_up,
    shared_down,
    expert_up,
    expert_down,
    routes,
    places,
):
    rows, width = tokens.shape
    local_width = qkv_weight.shape[2]
    members = expert_up.shape[0]
    me = lax.axis_index("tensor")
    base = (lax.axis_index("expert") * members).astype(jnp.int32).reshape(1)
    everyone = ("dp", "expert", "tensor")
    total_blocks = links.dp * links.expert * links.tensor
    full = links.paired and links.dp == 4 and total_blocks * rows * width * 2 <= FULL_LIMIT

    condition = jax.nn.silu(embedding(timesteps, width)).astype(bf16)
    mod_cols = jnp.einsum("id,dcf->icf", condition, ada_weight, preferred_element_type=f32) + ada_bias[None]
    mod = lax.all_to_all(mod_cols, "tensor", split_axis=0, concat_axis=2, tiled=True)[0]
    own_condition = lax.dynamic_slice_in_dim(condition.astype(f32), me, 1, axis=0)
    shared_cot = (mod[5][None] * cotangent.astype(f32)).astype(bf16)

    weight = jnp.concatenate(
        [qkv_weight.transpose(1, 2, 0).reshape(3 * local_width, width), out_weight], axis=0
    )
    if full:
        (weight,) = ordered([weight], [shared_cot])
    across = links.to_side(weight)
    near_shard = links.to_core(weight)
    if full:
        place = jnp.stack([base[0], *(lax.axis_index(axis) for axis in ("expert", "dp"))]).astype(jnp.int32)
        cot_column = links.column(jnp.broadcast_to(shared_cot[None], (links.dp, *shared_cot.shape)))
        cot_other = links.to_other(shared_cot)
        across, cot_other = ordered([across, cot_other], [mod])
        cot_side = links.to_side(ordered([shared_cot], [across])[0])
        cot_corner = links.to_other(cot_side)
    else:
        (across,) = ordered([across], [mod])
    shards = (weight, near_shard, across, links.to_core(across))
    router_t = router_weight.T
    pairs = jnp.concatenate([routes.T, places.T], axis=0)

    whole = slice(None)
    attn_in, qkv, context, attn_out, ext, ext_copies = attention_forward(
        tokens, mod, router_t, pairs, shards, local_width, links.dp if full else 1
    )
    feed = (shared_up, shared_down, expert_up, expert_down)
    backward = functools.partial(
        attention_backward, cond=own_condition, tokens=tokens, cotangent=cotangent, mod=mod, router_t=router_t,
        pairs=pairs, attn_in=attn_in, qkv=qkv, context=context, attn_out=attn_out, ext=ext, shards=shards,
        local_width=local_width,
    )
    if full:
        ext_side, ext_other = links.to_side(ext), links.to_other(ext)
        cut = PATCHES // 2 + EXTRA
        ext_cuts = (ext_other[:cut], ext_side[cut:])
        ext_corner = (links.to_side(ext_cuts[0]), links.to_other(ext_cuts[1]))
        ext_mine = assemble(
            (HALF, PATCHES + EXTRA, width), bf16, [ext, ext_side, ext_other, *ext_corner],
            [(index, whole, index) for index in range(3)]
            + [(3, whole, (3, pl.ds(0, cut))), (4, whole, (3, pl.ds(cut, PATCHES // 2)))],
        )
        ext_near = links.to_core(ext_mine)
        pieces = [shared_cot, cot_side, cot_other, cot_corner]
        cot_rest, cot_mine = launch(
            pick_both_kernel, "pick_both",
            [((links.dp - 1, PATCHES, width), bf16), ((HALF, PATCHES, width), bf16)], [*pieces, cot_column],
            in_specs=[pl.BlockSpec(memory_space=pl.ANY)] * (HALF + 1), scalars=[place],
            scratch=[pltpu.SemaphoreType.DMA((links.dp - 1 + HALF,))], after=[ext_mine], moved=5 * 10**6,
        )
        cots = lax.all_gather(cot_rest, ("expert", "tensor"), axis=0)
        cot_near = links.to_core(cot_mine)
        ext_column = links.column(ordered([ext_copies], [ext_side, ext_other])[0])
        own = (Blocks.apart(ext_mine, cot_mine), Blocks.apart(ext_near, cot_near))
        first, second = experts_both(base, own, *feed, (0, 1, 4, 5), after=[cot_rest])
        ext_rest, exts = links.column_rest(ext_column, place, [first])
        moved = links.to_core(second)
        side, other = links.plane_sum_first(first, moved, after=[ext_rest])
        slots = dispatch(base, own, members, after=[side])
        from_side, from_other = links.to_side(side), links.to_other(other)
        routed = routed_grads([slots], expert_up, expert_down, None)
        upper, lower, upper_next, lower_next = links.plane_sum_second(
            first, moved, from_side, from_other, after=[routed[0]]
        )
        upper_more, lower_more = links.to_other(upper_next), links.to_side(lower_next)
        shared = shared_grads(own, HALF, shared_up, shared_down, None, after=[upper, cots])
        output, tokens_grad, small, near, far = backward(
            upper, upper_more, lower, lower_more, after=[shared[0]]
        )
        dense = links.dense_sum(near, far)
        next(dense)
        small_all = lax.all_gather(small, everyone, axis=0)
        *shared, sent = shared_grads_other(exts, cots, 1, shared_up, shared_down, shared, after=[small])
        shared_more = links.to_next(sent)
        step = dense.send([sent])
        slots = dispatch_hops(base, exts, cots, members, after=[step])
        step = dense.send([slots[0]])
        for span in ((0, 2), (2, 3)):
            routed = routed_grads([slots], expert_up, expert_down, routed, after=[step], span=span)
            step = dense.send([routed[0]])
        shared = launch(
            shared_last_kernel, "shared_last", [(shared_up.shape, f32), (shared_down.shape, f32)],
            [*shared, shared_more], after=[step], moved=12 * 10**6,
        )
        routed = routed_grads([slots], expert_up, expert_down, routed, after=[shared[0]], span=(3, members))
        step = dense.send([routed[0]])
        qkv_grad, out_grad = dense.send([step])
        (small_all,) = ordered([small_all], [routed[0]])
        routes_all = jnp.concatenate(
            [value[..., PATCHES, : TOPK * PATCHES].reshape(-1, TOPK * PATCHES) for value in (ext_mine, ext_near, exts)],
            axis=0,
        )
    else:
        shift = lax.axis_index("expert") * links.tensor
        gather = lambda block: jnp.roll(
            lax.all_gather(block, ("expert", "tensor"), axis=0), -shift, axis=0
        )
        all_ext, all_cot = gather(ext), gather(shared_cot)
        planes, sums = [], []
        for start in range(0, links.expert * links.tensor, 2 * HALF):
            spans = [slice(start + HALF * part, start + HALF * (part + 1)) for part in range(2)]
            planes.append(tuple(Blocks.apart(all_ext[span], all_cot[span]) for span in spans))
            shared_ids = tuple(range(links.tensor)) if start == 0 else ()
            sums += experts_both(base, planes[-1], *feed, shared_ids)
        blocks = jnp.roll(jnp.concatenate(sums, axis=0), shift, axis=0)
        total = lax.psum_scatter(blocks, ("expert", "tensor"), scatter_dimension=0, tiled=True)[0]
        upper, lower = total[:PATCHES].astype(f32), total[PATCHES:].astype(f32)
        output, tokens_grad, small, near, far = backward(
            upper, jnp.zeros_like(total[:PATCHES]), lower, jnp.zeros_like(total[PATCHES:])
        )
        small_all = lax.all_gather(small, everyone, axis=0)
        slots = [dispatch(base, plane, members) for plane in planes]
        routed = None
        for start in range(0, len(planes), 2):
            routed = routed_grads(slots[start : start + 2], expert_up, expert_down, routed)
        shared = shared_grads(planes[0][:1], HALF, shared_up, shared_down, None)
        routed = lax.psum(routed, "dp")
        shared = lax.psum(tuple(part[0] for part in shared), ("dp", "expert"))
        routes_all = lax.all_gather(routes.reshape(-1), everyone, axis=0)
        turn = jnp.arange(links.tensor) ^ me
        grads = jnp.stack([near, far], axis=1).reshape((-1,) + near.shape[1:])[turn]
        dense = lax.psum_scatter(grads, "tensor", scatter_dimension=0, tiled=True)[0]
        dense = lax.psum(dense, ("dp", "expert")).astype(f32)
        qkv_grad, out_grad = dense[: 3 * local_width], dense[3 * local_width :]

    condition_all = small_all[:, 6].astype(bf16)
    mod_grad = lax.dynamic_slice_in_dim(small_all[:, 0:6], me * local_width, local_width, axis=2)
    ada_grad = jnp.einsum(
        "id,icf->dcf", condition_all.astype(f32), mod_grad, precision=lax.Precision.HIGHEST
    )
    ada_bias_grad = jnp.sum(mod_grad, axis=0)
    router_grad = jnp.sum(small_all[:, 8:16], axis=0).T
    counts = jnp.sum(
        (routes_all[:, :, None] == jnp.arange(EXPERTS).astype(routes_all.dtype)).astype(jnp.int32),
        axis=(0, 1),
    )
    qkv_grad = qkv_grad.reshape(3, local_width, width).transpose(2, 0, 1)
    return (
        output,
        tokens_grad,
        ada_grad,
        ada_bias_grad,
        qkv_grad,
        out_grad,
        router_grad,
        shared[0],
        shared[1],
        routed[0],
        routed[1],
        counts,
    )


def solution(mesh):
    rows = P(("dp", "expert", "tensor"), None)
    placed = (
        rows,
        rows,
        P(("dp", "expert")),
        P(None, None, "tensor"),
        P(None, "tensor"),
        P(None, None, "tensor"),
        P("tensor", None),
        P(),
        P(None, "tensor"),
        P("tensor", None),
        P("expert", None, "tensor"),
        P("expert", "tensor", None),
        rows,
        rows,
    )
    return jax.shard_map(
        functools.partial(local, Links(mesh)),
        mesh=mesh,
        in_specs=placed,
        out_specs=(
            rows,
            rows,
            P(None, None, "tensor"),
            P(None, "tensor"),
            P(None, None, "tensor"),
            P("tensor", None),
            P(),
            P(None, "tensor"),
            P("tensor", None),
            P("expert", None, "tensor"),
            P("expert", "tensor", None),
            P(),
        ),
        check_vma=False,
    )
```

```python
import functools
import math

import jax
import jax.numpy as jnp
from jax import lax
from jax.experimental import pallas as pl
from jax.experimental.pallas import tpu as pltpu
from jax.sharding import PartitionSpec as P

HD = 64
EXPERTS = 8
TOPK = 2
PATCHES = 256
CAP = 80
EXTRA = 16
EPSILON = 1e-06
HALF = 4
FULL_LIMIT = 32 * 1024 * 1024
VMEM_LIMIT = 63 * 1024 * 1024

f32 = jnp.float32
bf16 = jnp.bfloat16
NN = (((1,), (0,)), ((), ()))
NT = (((1,), (1,)), ((), ()))
TN = (((0,), (0,)), ((), ()))
TT = (((0,), (1,)), ((), ()))


def mm(left, right, dims):
    return lax.dot_general(left, right, dims, preferred_element_type=f32)


def normalize(values):
    center = jnp.mean(values, axis=-1, keepdims=True)
    shifted = values - center
    inverse = lax.rsqrt(jnp.mean(shifted * shifted, axis=-1, keepdims=True) + EPSILON)
    return (shifted * inverse, inverse)


def normalize_back(normed, inverse, upstream):
    return inverse * (
        upstream
        - jnp.mean(upstream, axis=-1, keepdims=True)
        - normed * jnp.mean(upstream * normed, axis=-1, keepdims=True)
    )


def embedding(steps, model_width):
    half_width = model_width // 2
    freqs_all = jnp.exp(-math.log(10000.0) * jnp.arange(half_width, dtype=f32) / half_width)
    angles = steps.astype(f32)[:, None] * freqs_all[None, :]
    return jnp.concatenate([jnp.cos(angles), jnp.sin(angles)], axis=1)


def gelu_both(pre):
    const = math.sqrt(2.0 / math.pi)
    square = pre * pre
    tanh = jnp.tanh(const * pre * (1.0 + 0.044715 * square))
    half = 0.5 + 0.5 * tanh
    value = pre * half
    return value, half + value * (1.0 - tanh) * (const + 3.0 * 0.044715 * const * square)


def launch(
    kernel, name, outs, operands, *, in_specs=None, out_specs=None, grid=(), scalars=(), scratch=(), aliases=None,
    after=(), flops=0, moved=0,
):
    lead = len(scalars)
    count = lead + len(operands)
    waits = len(after)
    on_chip = pl.BlockSpec(memory_space=pltpu.VMEM)
    anywhere = pl.BlockSpec(memory_space=pl.ANY)
    in_specs = list(in_specs or [on_chip] * len(operands)) + [anywhere] * waits
    out_specs = tuple(out_specs or [on_chip] * len(outs))

    def body(*refs):
        kernel(*refs[:count], *refs[count + waits :])

    if scalars and grid:
        shape = dict(
            grid_spec=pltpu.PrefetchScalarGridSpec(
                num_scalar_prefetch=lead, grid=grid, in_specs=in_specs, out_specs=out_specs, scratch_shapes=scratch
            )
        )
    else:
        in_specs = [pl.BlockSpec(memory_space=pltpu.SMEM)] * lead + in_specs
        shape = dict(grid=grid, in_specs=in_specs, out_specs=out_specs, scratch_shapes=scratch)
    return pl.pallas_call(
        body,
        out_shape=tuple(jax.ShapeDtypeStruct(*out) for out in outs),
        input_output_aliases=aliases or {},
        compiler_params=pltpu.CompilerParams(vmem_limit_bytes=VMEM_LIMIT),
        cost_estimate=pl.CostEstimate(flops=int(flops), bytes_accessed=int(moved), transcendentals=0),
        name=name,
        **shape,
    )(*scalars, *operands, *after)


def copy_kernel(plan, count, *refs):
    sources, out, sems = refs[:count], refs[-2], refs[-1]
    copies = [
        pltpu.make_async_copy(sources[index].at[take], out.at[put], sems.at[order])
        for order, (index, take, put) in enumerate(plan)
    ]
    for copy in copies:
        copy.start()
    for copy in copies:
        copy.wait()


def assemble(shape, dtype, sources, plan, after=()):
    size = math.prod(shape) * jnp.dtype(dtype).itemsize
    return launch(
        functools.partial(copy_kernel, plan, len(sources)), "assemble", [(shape, dtype)], sources,
        in_specs=[pl.BlockSpec(memory_space=pl.ANY)] * len(sources),
        scratch=[pltpu.SemaphoreType.DMA((len(plan),))], after=after, moved=2 * size,
    )[0]


def order_kernel(*refs):
    pass


def ordered(values, after):
    anywhere = [pl.BlockSpec(memory_space=pl.ANY)] * len(values)
    return launch(
        order_kernel, "ordered", [(value.shape, value.dtype) for value in values], values, in_specs=anywhere,
        out_specs=anywhere, aliases={index: index for index in range(len(values))}, after=after,
    )


def pair_masks(rows):
    lane = lax.broadcasted_iota(jnp.int32, (rows, 2 * HD), 1)
    return (lane < HD, lane >= HD)


def head_probs(query, key):
    scores = mm(query, key, NT) * (1.0 / math.sqrt(HD))
    weights = jnp.exp(scores - jnp.max(scores, axis=-1, keepdims=True))
    return weights / jnp.sum(weights, axis=-1, keepdims=True)


def shard_rows(shards, part, local_width):
    return jnp.concatenate(
        [shard[part * local_width : (part + 1) * local_width, :] for shard in shards], axis=0
    )


def attention_kernel(
    local_width, tok_ref, mod_ref, router_ref, pairs_ref, w0, w1, w2, w3,
    attn_in_ref, qkv_ref, context_ref, attn_out_ref, ext_ref, column_ref,
):
    shards = (w0, w1, w2, w3)
    rows, width = tok_ref.shape
    mod = mod_ref[...]
    stream = tok_ref[...].astype(f32)
    attn_in = (normalize(stream)[0] * (1.0 + mod[1:2]) + mod[0:1]).astype(bf16)
    attn_in_ref[...] = attn_in
    for part in range(3):
        qkv_ref[part] = mm(attn_in, shard_rows(shards, part, local_width), NT).astype(bf16)
    masks = pair_masks(rows)
    zero = jnp.zeros((rows, 2 * HD), bf16)
    for pair in range(width // (2 * HD)):
        cols = slice(pair * 2 * HD, (pair + 1) * 2 * HD)
        query, key, value = qkv_ref[0, :, cols], qkv_ref[1, :, cols], qkv_ref[2, :, cols]
        parts = []
        for mask in masks:
            probs = head_probs(jnp.where(mask, query, zero), key)
            parts.append(mm(probs.astype(bf16), value, NN))
        context_ref[:, cols] = jnp.where(masks[0], parts[0], parts[1]).astype(bf16)
    attn_out = mm(context_ref[...], shard_rows(shards, 3, local_width), NN)
    attn_out_ref[...] = attn_out
    residual = stream + mod[2:3] * attn_out
    moe_in = (normalize(residual)[0] * (1.0 + mod[4:5]) + mod[3:4]).astype(bf16)
    ext_ref[0:rows, :] = moe_in
    logits = mm(router_ref[...], moe_in, NT)
    pairs = pairs_ref[...]
    expert_id = lax.broadcasted_iota(jnp.int32, (EXPERTS, rows), 0)
    chosen = [
        jnp.sum(jnp.where(expert_id == pairs[k : k + 1], logits, 0.0), axis=0, keepdims=True)
        for k in range(TOPK)
    ]
    top = jnp.maximum(chosen[0], chosen[1])
    powers = [jnp.exp(value - top) for value in chosen]
    gates = [power / (powers[0] + powers[1]) for power in powers]
    high = [gate.astype(bf16).astype(f32) for gate in gates]
    rest = [gate - upper for gate, upper in zip(gates, high)]
    values = pairs.astype(f32)
    packed = (
        jnp.concatenate([values[0:1], values[1:2], values[2:3]], axis=1),
        jnp.concatenate([values[3:4], high[0], high[1]], axis=1),
        jnp.concatenate([rest[0], rest[1], jnp.zeros_like(rest[0])], axis=1),
    )
    row_id = lax.broadcasted_iota(jnp.int32, (EXTRA, width), 0)
    extra = jnp.zeros((EXTRA, width), f32)
    for index, line in enumerate(packed):
        extra = jnp.where(row_id == index, line, extra)
    ext_ref[rows : rows + EXTRA, :] = extra.astype(bf16)
    for copy in range(column_ref.shape[0]):
        column_ref[copy] = ext_ref[...]


def attention_forward(tokens, mod, router_t, pairs, shards, local_width, copies):
    rows, width = tokens.shape
    outs = [
        ((rows, width), bf16),
        ((3, rows, width), bf16),
        ((rows, width), bf16),
        ((rows, width), f32),
        ((rows + EXTRA, width), bf16),
        ((copies, rows + EXTRA, width), bf16),
    ]
    return launch(
        functools.partial(attention_kernel, local_width), "attention_forward", outs,
        [tokens, mod, router_t, pairs, *shards], flops=5 * 10**9, moved=9 * 10**6,
    )


def read_pairs(extra):
    info = extra.astype(f32)
    count = PATCHES
    routes = (info[0:1, 0:count], info[0:1, count : 2 * count])
    places = (info[0:1, 2 * count : 3 * count], info[1:2, 0:count])
    gates = (
        info[1:2, count : 2 * count] + info[2:3, 0:count],
        info[1:2, 2 * count : 3 * count] + info[2:3, count : 2 * count],
    )
    return routes, places, gates


def slot_hits(routes, places, base, slots):
    slot_id = lax.broadcasted_iota(jnp.int32, (slots, PATCHES), 0).astype(f32)
    return [
        slot_id == jnp.where(place < CAP, (route - base) * CAP + place, -1.0)
        for route, place in zip(routes, places)
    ]


def slot_gates(hits, gates):
    return jnp.sum(
        jnp.where(hits[0], gates[0], 0.0) + jnp.where(hits[1], gates[1], 0.0), axis=1, keepdims=True
    )


class Blocks:
    def __init__(self, rows, rows_at, extra_at, cots, cots_at):
        self.rows, self.rows_at, self.extra_at, self.cots, self.cots_at = rows, rows_at, extra_at, cots, cots_at

    @classmethod
    def apart(cls, ext, cots):
        return cls(ext, 0, PATCHES // EXTRA, cots, 0)

    def operands(self):
        return [self.rows, self.rows, self.cots]

    def specs(self, taken=HALF):
        width = self.rows.shape[2]
        places = ((PATCHES, self.rows_at), (EXTRA, self.extra_at), (PATCHES, self.cots_at))
        return [
            pl.BlockSpec((taken, count, width), lambda *_, at=at: (0, at, 0)) for count, at in places
        ]

    def extra(self):
        return self.rows[:, self.extra_at * EXTRA : (self.extra_at + 1) * EXTRA]


def dispatch_kernel(base_ref, *refs):
    rows_ref, cots_ref = refs[-2:]
    members = rows_ref.shape[0]
    base = base_ref[0].astype(f32)
    for part in range(2):
        rows_in, extra_in, cots_in = refs[3 * part : 3 * part + 3]

        @pl.when(pl.program_id(0) == part)
        def _():
            for block in range(HALF):
                dispatch_block(
                    base, members, rows_in[block], extra_in[block], cots_in[block], rows_ref, cots_ref, block
                )


def dispatch_block(base, members, rows, extra, cots, rows_ref, cots_ref, block):
    routes, places, gates = read_pairs(extra)
    hits = slot_hits(routes, places, base, members * CAP)
    hot = (hits[0] | hits[1]).astype(bf16)
    picked = mm(hot, rows, NN).astype(bf16)
    scaled = (mm(hot, cots, NN) * slot_gates(hits, gates)).astype(bf16)
    for member in range(members):
        span = slice(member * CAP, (member + 1) * CAP)
        rows_ref[member, block * CAP : (block + 1) * CAP, :] = picked[span]
        cots_ref[member, block * CAP : (block + 1) * CAP, :] = scaled[span]


def hops_kernel(base_ref, ext, cots, rows_ref, cots_ref):
    base = base_ref[0].astype(f32)
    for block in range(ext.shape[0]):
        dispatch_block(
            base, rows_ref.shape[0], ext[block, 0, :PATCHES], ext[block, 0, PATCHES:], cots[block, 0], rows_ref,
            cots_ref, block,
        )


def dispatch_hops(base, ext, cots, members, after=()):
    blocks, hops, rows, width = ext.shape
    out = ((members, hops * blocks * CAP, width), bf16)
    out_spec = pl.BlockSpec((members, blocks * CAP, width), lambda h, b: (0, h, 0))
    specs = [pl.BlockSpec((blocks, 1, count, width), lambda h, b: (0, h, 0, 0)) for count in (rows, PATCHES)]
    return launch(
        hops_kernel, "dispatch_hops", [out, out], [ext, cots], in_specs=specs, out_specs=[out_spec, out_spec],
        grid=(hops,), scalars=[base], after=after, flops=24 * 10**9, moved=48 * 10**6,
    )


def pick_kernel(place_ref, source, out):
    planes = source.shape[0]
    for hop in range(planes - 1):
        out[hop] = source[lax.rem(place_ref[2] + hop + 1, planes)]


def pick_both_kernel(place_ref, *refs):
    sources, column, rest, stack, sems = refs[:HALF], refs[HALF], refs[-3], refs[-2], refs[-1]
    planes = column.shape[0]
    copies = [
        pltpu.make_async_copy(column.at[lax.rem(place_ref[2] + hop + 1, planes)], rest.at[hop], sems.at[hop])
        for hop in range(planes - 1)
    ]
    copies += [
        pltpu.make_async_copy(source, stack.at[index], sems.at[planes - 1 + index])
        for index, source in enumerate(sources)
    ]
    for copy in copies:
        copy.start()
    for copy in copies:
        copy.wait()


def dispatch(base, blocks, members, after=()):
    width = blocks[0].rows.shape[2]
    out = ((members, 2 * HALF * CAP, width), bf16)
    out_spec = pl.BlockSpec((members, HALF * CAP, width), lambda c, *_: (0, c, 0))
    return launch(
        dispatch_kernel, "dispatch", [out, out], [operand for part in blocks for operand in part.operands()],
        in_specs=[spec for part in blocks for spec in part.specs()], out_specs=[out_spec, out_spec],
        grid=(2,), scalars=[base], after=after, flops=8 * 10**9, moved=16 * 10**6,
    )


def expert_kernel(
    shared_ids, base_ref, rows0, extra0, cots0, rows1, extra1, cots1, sup_ref, sdown_ref, eup_ref, edown_ref,
    first_ref, second_ref, rows_s, cots_s, gate_s, dot_s, shared_s,
):
    step = pl.program_id(0)
    members = rows_s.shape[0]
    width = sup_ref.shape[0]
    base = base_ref[0].astype(f32)
    halves = ((rows0, extra0, cots0), (rows1, extra1, cots1))
    total_rows = 2 * HALF * CAP

    def hits_of(half, place):
        routes, places, gates = read_pairs(halves[half][1][place])
        return slot_hits(routes, places, base, members * CAP), gates

    def start_of(half, place):
        return pl.multiple_of((half * HALF + place) * CAP, CAP)

    def per_block(count, body, first=0):
        for half in range(2):
            lax.fori_loop(first, count, lambda place, _, half=half: (body(half, place), 0)[1], 0)

    @pl.when(step == 0)
    def _():
        def send(half, place):
            rows_in, _, cots_in = halves[half]
            hits, gates = hits_of(half, place)
            hot = (hits[0] | hits[1]).astype(bf16)
            picked = mm(hot, rows_in[place], NN).astype(bf16)
            cots = mm(hot, cots_in[place], NN).astype(bf16)
            gate = slot_gates(hits, gates)
            rows = pl.ds(start_of(half, place), CAP)
            for member in range(members):
                span = slice(member * CAP, (member + 1) * CAP)
                rows_s[member, rows, :] = picked[span]
                cots_s[member, rows, :] = cots[span]
                gate_s[member, rows, :] = gate[span]

        per_block(HALF, send)
        for start in range(0, len(shared_ids), 2):
            pair = shared_ids[start : start + 2]
            inputs = jnp.concatenate([halves[b // HALF][0][b % HALF] for b in pair], axis=0)
            cots = jnp.concatenate([halves[b // HALF][2][b % HALF] for b in pair], axis=0)
            value, slope = gelu_both(mm(inputs, sup_ref[...], NN))
            pre_grad = (mm(cots, sdown_ref[...], NT) * slope).astype(bf16)
            result = mm(value.astype(bf16), sdown_ref[...], NN)
            back = mm(pre_grad, sup_ref[...], NT)
            for place in range(len(pair)):
                span = slice(place * PATCHES, (place + 1) * PATCHES)
                shared_s[start + place, :, 0:width] = result[span]
                shared_s[start + place, :, width:] = back[span]

    @pl.when(step > 0)
    def _():
        member = step - 1
        tile = total_rows // 2

        for part in range(2):
            span = slice(part * tile, (part + 1) * tile)
            inputs, cots, gate = rows_s[member, span, :], cots_s[member, span, :], gate_s[member, span, :]
            value, slope = gelu_both(mm(inputs, eup_ref[0], NN))
            act_grad = mm(cots, edown_ref[0], NT)
            dot_s[member, span, :] = jnp.sum(value * act_grad, axis=1, keepdims=True)
            active = (gate * value).astype(bf16)
            pre_grad = (gate * act_grad * slope).astype(bf16)
            rows_s[member, span, :] = mm(active, edown_ref[0], NN).astype(bf16)
            cots_s[member, span, :] = mm(pre_grad, eup_ref[0], NT).astype(bf16)

    @pl.when(step == members)
    def _():
        per_half = [sum(1 for b in shared_ids if b // HALF == half) for half in range(2)]

        def combine(half, place, shared):
            out_ref = (first_ref, second_ref)[half]
            hits, _ = hits_of(half, place)
            hot = (hits[0] | hits[1]).astype(bf16)
            span = pl.ds(start_of(half, place), CAP)
            dots = jnp.concatenate([dot_s[m, span, :] for m in range(members)], axis=0)
            sums = [jnp.sum(jnp.where(hit, dots, 0.0), axis=0, keepdims=True) for hit in hits]
            line = jnp.concatenate(sums + [jnp.zeros_like(sums[0])], axis=1)
            row_id = lax.broadcasted_iota(jnp.int32, (EXTRA, width), 0)
            out_ref[place, 2 * PATCHES :, :] = jnp.where(row_id == 0, line, 0.0).astype(bf16)
            for index, source in enumerate((rows_s, cots_s)):
                slots = jnp.concatenate([source[m, span, :] for m in range(members)], axis=0)
                total = mm(hot, slots, TN)
                if shared:
                    where = half * per_half[0] + place
                    total = total + shared_s[where, :, index * width : (index + 1) * width]
                out_ref[place, index * PATCHES : (index + 1) * PATCHES, :] = total.astype(bf16)

        for half in range(2):
            for first, last, shared in ((0, per_half[half], True), (per_half[half], HALF, False)):
                if last > first:
                    lax.fori_loop(
                        first, last,
                        lambda place, _, half=half, shared=shared: (combine(half, place, shared), 0)[1], 0,
                    )


def experts_both(base, blocks, shared_up, shared_down, expert_up, expert_down, shared_ids, after=()):
    members, width, hidden = expert_up.shape
    shape = (HALF, 2 * PATCHES + EXTRA, width)
    out_spec = pl.BlockSpec(shape, lambda e, b: (0, 0, 0))
    slots = (members, 2 * HALF * CAP)
    return launch(
        functools.partial(expert_kernel, shared_ids), "experts_both", [(shape, bf16)] * 2,
        [operand for part in blocks for operand in part.operands()]
        + [shared_up, shared_down, expert_up, expert_down],
        in_specs=[spec for part in blocks for spec in part.specs()]
        + [
            pl.BlockSpec((width, hidden), lambda e, b: (0, 0)),
            pl.BlockSpec((hidden, width), lambda e, b: (0, 0)),
            pl.BlockSpec((1, width, hidden), lambda e, b: (jnp.maximum(e - 1, 0), 0, 0)),
            pl.BlockSpec((1, hidden, width), lambda e, b: (jnp.maximum(e - 1, 0), 0, 0)),
        ],
        out_specs=[out_spec, out_spec],
        grid=(members + 1,),
        scalars=[base],
        after=after,
        scratch=[
            pltpu.VMEM((*slots, width), bf16),
            pltpu.VMEM((*slots, width), bf16),
            pltpu.VMEM((*slots, 1), f32),
            pltpu.VMEM((*slots, 1), f32),
            pltpu.VMEM((max(len(shared_ids), 1), PATCHES, 2 * width), f32),
        ], flops=30 * 10**9, moved=30 * 10**6,
    )


def both_grads(inputs, cots, up, down):
    value, slope = gelu_both(mm(up, inputs, TT))
    pre_grad = (mm(down, cots, NT) * slope).astype(bf16)
    return mm(inputs, pre_grad, TT), mm(value.astype(bf16), cots, NN)


def grads_kernel(count, tile, started, *refs):
    row_refs, cot_refs = refs[:count], refs[count : 2 * count]
    up_ref, down_ref = refs[2 * count : 2 * count + 2]
    up_grad_ref, down_grad_ref = refs[-2:]
    width = up_ref.shape[1]
    inputs = [ref[...].reshape(-1, width) for ref in row_refs]
    cots = [ref[...].reshape(-1, width) for ref in cot_refs]
    groups = max(1, count * inputs[0].shape[0] // tile)
    each = count // groups
    for group in range(groups):
        part = slice(group * each, (group + 1) * each)
        rows, cot = jnp.concatenate(inputs[part], axis=0), jnp.concatenate(cots[part], axis=0)
        up_grad, down_grad = both_grads(rows, cot, up_ref[0], down_ref[0])
        if group == 0 and started:
            up_grad_ref[0] = refs[2 * count + 2][0] + up_grad
            down_grad_ref[0] = refs[2 * count + 3][0] + down_grad
        elif group == 0:
            up_grad_ref[0] = up_grad
            down_grad_ref[0] = down_grad
        else:
            up_grad_ref[0] += up_grad
            down_grad_ref[0] += down_grad


def shared_other_kernel(rows, cots, up, down, up_before, down_before, up_out, down_out, low_out):
    width = up.shape[0]
    grads = both_grads(rows[...].reshape(-1, width), cots[...].reshape(-1, width), up[...], down[...])
    step = pl.program_id(0)
    for grad, before, out in zip(grads, (up_before, down_before), (up_out, down_out)):

        @pl.when(step == 0)
        def _():
            out[...] = before[0] + grad

        @pl.when(step > 0)
        def _():
            out[...] += grad

    @pl.when(step == pl.num_programs(0) - 1)
    def _():
        low_out[0] = up_out[...].astype(bf16)
        low_out[1] = down_out[...].astype(bf16)


def weight_grads(rows, cots, specs, up, down, before, tile, total, after=(), span=None):
    members, width, hidden = up.shape
    start, stop = span or (0, members)
    up_spec = pl.BlockSpec((1, width, hidden), lambda e: (e + start, 0, 0))
    down_spec = pl.BlockSpec((1, hidden, width), lambda e: (e + start, 0, 0))
    started = before is not None
    count = len(rows)
    first = 2 * count + 2
    return launch(
        functools.partial(grads_kernel, count, tile, started), "weight_grads", [(up.shape, f32), (down.shape, f32)],
        [*rows, *cots, up, down, *(before or ())],
        in_specs=specs + [up_spec, down_spec] * (2 if started else 1), out_specs=[up_spec, down_spec],
        grid=(stop - start,), aliases={first: 0, first + 1: 1} if started else None, after=after,
        flops=12 * total * width * hidden, moved=total * width * 4,
    )


def routed_grads(slots, up, down, before, after=(), span=None):
    members, count, width = slots[0][0].shape
    start, stop = span or (0, members)
    spec = pl.BlockSpec((1, count, width), lambda e: (e + start, 0, 0))
    rows, cots = [pair[0] for pair in slots], [pair[1] for pair in slots]
    specs = [spec] * (2 * len(slots))
    each = len(slots) * count
    return weight_grads(
        rows, cots, specs, up, down, before, each, (stop - start) * each, after=after, span=span
    )


def shared_grads(blocks, taken, up, down, before, after=()):
    rows, cots = [part.rows for part in blocks], [part.cots for part in blocks]
    all_specs = [part.specs(taken) for part in blocks]
    specs = [spec[0] for spec in all_specs] + [spec[2] for spec in all_specs]
    total = len(blocks) * taken * PATCHES
    tile = total if total <= 8 * PATCHES else total // 2
    return weight_grads(rows, cots, specs, up[None], down[None], before, tile, total, after)


def shared_grads_other(ext, cots, hop, up, down, before, after=()):
    blocks, _, _, width = ext.shape
    steps = 2
    spec = pl.BlockSpec((blocks // steps, 1, PATCHES, width), lambda t: (t, hop, 0, 0))
    up_spec = pl.BlockSpec(up.shape, lambda t: (0, 0))
    down_spec = pl.BlockSpec(down.shape, lambda t: (0, 0))
    before_specs = [pl.BlockSpec((1, *part.shape), lambda t: (0, 0, 0)) for part in (up, down)]
    low = (2, *up.shape)
    total = blocks * PATCHES
    return launch(
        shared_other_kernel, "shared_grads_other", [(up.shape, f32), (down.shape, f32), (low, bf16)],
        [ext, cots, up, down, *before], in_specs=[spec, spec, up_spec, down_spec] + before_specs,
        out_specs=[up_spec, down_spec, pl.BlockSpec(low, lambda t: (0, 0, 0))],
        grid=(steps,), after=after, flops=12 * total * up.size, moved=total * width * 4,
    )


def shared_last_kernel(up, down, more, up_out, down_out):
    up_out[...] = up[...] + more[0].astype(f32)
    down_out[...] = down[...] + more[1].astype(f32)


def backward_kernel(
    local_width, moe_ref, moe_more_ref, back_ref, back_more_ref, cond_ref, tok_ref, cot_ref, mod_ref, router_ref, pairs_ref, attn_in_ref,
    qkv_ref, context_ref, attn_out_ref, ext_ref, w0, w1, w2, w3,
    output_ref, tok_grad_ref, small_ref, near_ref, far_ref, grad_s,
):
    def put_weight_grad(first, grad):
        for index in range(len(shards)):
            out_ref = (near_ref, far_ref)[index % 2]
            out_ref[index // 2, first : first + local_width, :] = grad[
                index * local_width : (index + 1) * local_width
            ]

    shards = (w0, w1, w2, w3)
    rows, width = tok_ref.shape
    mod = mod_ref[...]
    stream = tok_ref[...].astype(f32)
    attn_out = attn_out_ref[...]
    residual = stream + mod[2:3] * attn_out
    second_norm, second_inv = normalize(residual)
    moe_out = moe_ref[...] + moe_more_ref[...].astype(f32)
    back = back_ref[...] + back_more_ref[...].astype(f32)
    upstream = cot_ref[...].astype(f32)
    output_ref[...] = (residual + mod[5:6] * moe_out).astype(bf16)
    gate_two_grad = jnp.sum(upstream * moe_out, axis=0, keepdims=True)
    routes, places, gates = read_pairs(ext_ref[rows:, :])
    dots = (back[rows : rows + 1, 0:PATCHES], back[rows : rows + 1, PATCHES : 2 * PATCHES])
    mean_dot = gates[0] * dots[0] + gates[1] * dots[1]
    pairs = pairs_ref[...]
    expert_id = lax.broadcasted_iota(jnp.int32, (EXPERTS, rows), 0)
    logits_grad = jnp.zeros((EXPERTS, rows), f32)
    for k in range(TOPK):
        logits_grad += jnp.where(expert_id == pairs[k : k + 1], gates[k] * (dots[k] - mean_dot), 0.0)
    logits_grad = logits_grad.astype(bf16)
    moe_in_grad = back[0:rows] + mm(logits_grad, router_ref[...], TN)
    shift_two_grad = jnp.sum(moe_in_grad, axis=0, keepdims=True)
    scale_two_grad = jnp.sum(moe_in_grad * second_norm, axis=0, keepdims=True)
    residual_grad = upstream + normalize_back(
        second_norm, second_inv, moe_in_grad * (1.0 + mod[4:5])
    )
    gate_one_grad = jnp.sum(residual_grad * attn_out, axis=0, keepdims=True)
    attn_grad = (mod[2:3] * residual_grad).astype(bf16)
    out_grad = mm(context_ref[...], attn_grad, TN).astype(bf16)
    put_weight_grad(3 * local_width, out_grad)
    context_grad = mm(attn_grad, shard_rows(shards, 3, local_width), NT).astype(bf16)
    masks = pair_masks(rows)
    zero = jnp.zeros((rows, 2 * HD), bf16)
    scale = 1.0 / math.sqrt(HD)
    for pair in range(width // (2 * HD)):
        cols = slice(pair * 2 * HD, (pair + 1) * 2 * HD)
        query, key, value = qkv_ref[0, :, cols], qkv_ref[1, :, cols], qkv_ref[2, :, cols]
        upper = context_grad[:, cols]
        sums = []
        for mask in masks:
            probs = head_probs(jnp.where(mask, query, zero), key)
            probs_grad = mm(jnp.where(mask, upper, zero), value, NT)
            value_grad = mm(probs.astype(bf16), upper, TN)
            score_grad = (
                probs * (probs_grad - jnp.sum(probs_grad * probs, axis=-1, keepdims=True))
            ).astype(bf16)
            sums.append((mm(score_grad, key, NN) * scale, mm(score_grad, query, TN) * scale, value_grad))
        for part in range(3):
            grad_s[part, :, cols] = jnp.where(masks[0], sums[0][part], sums[1][part]).astype(bf16)
    attn_in = attn_in_ref[...]
    attn_in_grad = jnp.zeros((rows, width), f32)
    for part in range(3):
        grad = grad_s[part]
        attn_in_grad += mm(grad, shard_rows(shards, part, local_width), NN)
        put_weight_grad(part * local_width, mm(grad, attn_in, TN).astype(bf16))
    first_norm, first_inv = normalize(stream)
    shift_one_grad = jnp.sum(attn_in_grad, axis=0, keepdims=True)
    scale_one_grad = jnp.sum(attn_in_grad * first_norm, axis=0, keepdims=True)
    tok_grad_ref[...] = residual_grad + normalize_back(
        first_norm, first_inv, attn_in_grad * (1.0 + mod[1:2])
    )
    lines = (
        shift_one_grad, scale_one_grad, gate_one_grad, shift_two_grad, scale_two_grad, gate_two_grad,
        cond_ref[...],
    )
    row_id = lax.broadcasted_iota(jnp.int32, (8, width), 0)
    stacked = jnp.zeros((8, width), f32)
    for index, line in enumerate(lines):
        stacked = jnp.where(row_id == index, line, stacked)
    small_ref[0:8, :] = stacked
    small_ref[8:16, :] = mm(logits_grad, ext_ref[0:rows, :], NN)


def attention_backward(
    moe, moe_more, back, back_more, cond, tokens, cotangent, mod, router_t, pairs, attn_in, qkv, context,
    attn_out, ext, shards, local_width, after=(),
):
    rows, width = tokens.shape
    halves = ((len(shards) // 2, 4 * local_width, width), bf16)
    return launch(
        functools.partial(backward_kernel, local_width), "attention_backward",
        [((rows, width), bf16), ((rows, width), f32), ((16, width), f32), halves, halves],
        [
            moe, moe_more, back, back_more, cond, tokens, cotangent, mod, router_t, pairs, attn_in, qkv,
            context, attn_out, ext, *shards,
        ],
        scratch=[pltpu.VMEM((3, rows, width), bf16)], after=after, flops=10 * 10**9, moved=16 * 10**6,
    )


def take_all(copies):
    for copy in copies:
        copy.start()
    for copy in copies:
        copy.wait()


def plane_first_kernel(first, more, side, other, upper_s, lower_s, sems):
    cut = PATCHES
    low = first.shape[1] - cut
    copies = []
    for index, source in enumerate((first, more)):
        for place, (upper, lower) in enumerate(((1, 2), (3, 3))):
            at = 4 * index + 2 * place
            copies += [
                pltpu.make_async_copy(source.at[upper, pl.ds(0, cut)], upper_s.at[index, place], sems.at[at]),
                pltpu.make_async_copy(source.at[lower, pl.ds(cut, low)], lower_s.at[index, place], sems.at[at + 1]),
            ]
    take_all(copies)
    side[...] = (upper_s[0].astype(f32) + upper_s[1].astype(f32)).astype(bf16)
    other[...] = (lower_s[0].astype(f32) + lower_s[1].astype(f32)).astype(bf16)


def plane_second_kernel(first, more, side, other, upper, lower, upper_next, lower_next, upper_s, lower_s, sems):
    cut = PATCHES
    low = first.shape[1] - cut
    copies = []
    for index, source in enumerate((first, more)):
        for place, (up, down) in enumerate(((0, 0), (2, 1))):
            at = 4 * index + 2 * place
            copies += [
                pltpu.make_async_copy(source.at[up, pl.ds(0, cut)], upper_s.at[index, place], sems.at[at]),
                pltpu.make_async_copy(source.at[down, pl.ds(cut, low)], lower_s.at[index, place], sems.at[at + 1]),
            ]
    take_all(copies)
    uppers = [upper_s[0, p].astype(f32) + upper_s[1, p].astype(f32) + side[p].astype(f32) for p in range(2)]
    lowers = [lower_s[0, p].astype(f32) + lower_s[1, p].astype(f32) + other[p].astype(f32) for p in range(2)]
    upper[...] = uppers[0]
    upper_next[...] = uppers[1].astype(bf16)
    lower[...] = lowers[0]
    lower_next[...] = lowers[1].astype(bf16)


def span_of(index, size):
    return pl.ds(pl.multiple_of(index * size, size), size)


def dense_copies(near, more, index, who, whole_s, half_s, sems):
    cut = whole_s.shape[1]
    half = half_s.shape[2]
    rows = pl.ds(pl.multiple_of(cut + who * half, half), half)
    copies = []
    for term, source in enumerate((near, more)):
        copies.append(pltpu.make_async_copy(source.at[index, pl.ds(0, cut)], whole_s.at[term], sems.at[3 * term]))
        for shard in range(2):
            copies.append(
                pltpu.make_async_copy(source.at[shard, rows], half_s.at[term, shard], sems.at[3 * term + 1 + shard])
            )
    take_all(copies)


def dense_first_kernel(place, near, more, side, other, whole_s, half_s, sems):
    dense_copies(near, more, 1, 1 - place[0], whole_s, half_s, sems)
    side[...] = (whole_s[0].astype(f32) + whole_s[1].astype(f32)).astype(bf16)
    other[...] = (half_s[0].astype(f32) + half_s[1].astype(f32)).astype(bf16)


def dense_second_kernel(place, near, more, from_side, from_other, side, other, upper, lower, whole_s, half_s, sems):
    mine = place[0]
    dense_copies(near, more, 0, mine, whole_s, half_s, sems)
    half = upper.shape[0]
    for out, who in ((upper, mine), (other, 1 - mine)):
        rows = span_of(who, half)
        total = whole_s[0, rows, :].astype(f32) + whole_s[1, rows, :].astype(f32) + from_side[rows, :].astype(f32)
        out[...] = total.astype(out.dtype)
    total = half_s[0].astype(f32) + half_s[1].astype(f32) + from_other[...].astype(f32)
    lower[...] = total[0]
    side[...] = total[1].astype(bf16)


def dense_third_kernel(size, place, upper, lower, from_side, from_other, own, *outs):
    sent, total = outs[:-1], outs[-1]
    half = upper.shape[0]
    share = 2 * half // size
    total[0:half, :] = upper[...] + from_other[...].astype(f32)
    total[half:, :] = lower[...] + from_side[...].astype(f32)
    own[...] = total[span_of(place[1], share), :]
    for hop in range(1, size):
        sent[hop - 1][...] = total[span_of(lax.rem(place[1] + hop, size), share), :].astype(bf16)


def dense_fourth_kernel(own, *refs):
    out = refs[-1]
    total = own[...]
    for ref in refs[:-1]:
        total = total + ref[...].astype(f32)
    out[...] = total.astype(bf16)


def dense_fifth_kernel(size, place, own, *refs):
    out = refs[-1]
    share = own.shape[0]
    out[span_of(place[1], share), :] = own[...]
    for hop in range(1, size):
        out[span_of(lax.rem(place[1] + size - hop, size), share), :] = refs[hop - 1][...]


def dense_last_kernel(place, own, more, qkv_out, out_out, total):
    half = own.shape[0] // 2
    for ref, who in ((own, place[0]), (more, 1 - place[0])):
        for index in range(2):
            rows = pl.ds(pl.multiple_of(2 * half * index + who * half, half), half)
            total[rows, :] = ref[index * half : (index + 1) * half, :].astype(f32)
    count = qkv_out.shape[0]
    qkv_out[...] = total[0:count, :]
    out_out[...] = total[count:, :]


class Links:
    def __init__(self, mesh):
        self.dp, self.expert, self.tensor = (mesh.shape[name] for name in ("dp", "expert", "tensor"))
        self.paired = self.expert == 2 and self.tensor == 4
        self.core = [(i, i ^ 1) for i in range(self.tensor)]
        self.side = [(i, i ^ 2) for i in range(self.tensor)]
        self.other = [(0, 1), (1, 0)]

    def to_core(self, value):
        return lax.ppermute(value, "tensor", self.core)

    def to_side(self, value):
        return lax.ppermute(value, "tensor", self.side)

    def to_other(self, value):
        return lax.ppermute(value, "expert", self.other)

    def to_next(self, value):
        return lax.ppermute(value, "dp", [(i, i ^ 1) for i in range(self.dp)])

    def along(self, value, hop):
        return lax.ppermute(value, "dp", [(i, (i + hop) % self.dp) for i in range(self.dp)])

    def column(self, copies):
        return lax.all_to_all(copies, "dp", split_axis=0, concat_axis=0)

    def column_rest(self, column, place, after):
        planes, rows, width = column.shape
        (rest,) = launch(
            pick_kernel, "pick", [((planes - 1, rows, width), column.dtype)], [column], scalars=[place], after=after,
            moved=3 * 10**6,
        )
        return rest, lax.all_gather(rest, ("expert", "tensor"), axis=0)

    def plane_sum_first(self, first, more, after):
        width = first.shape[2]
        low = first.shape[1] - PATCHES
        return launch(
            plane_first_kernel, "plane_first", [((2, PATCHES, width), bf16), ((2, low, width), bf16)],
            [first, more], in_specs=[pl.BlockSpec(memory_space=pl.ANY)] * 2,
            scratch=[
                pltpu.VMEM((2, 2, PATCHES, width), bf16),
                pltpu.VMEM((2, 2, low, width), bf16),
                pltpu.SemaphoreType.DMA((8,)),
            ],
            after=after, moved=5 * 10**6,
        )

    def plane_sum_second(self, first, more, side, other, after):
        width = first.shape[2]
        low = first.shape[1] - PATCHES
        return launch(
            plane_second_kernel, "plane_second",
            [((PATCHES, width), f32), ((low, width), f32), ((PATCHES, width), bf16), ((low, width), bf16)],
            [first, more, side, other],
            in_specs=[pl.BlockSpec(memory_space=pl.ANY)] * 2 + [pl.BlockSpec(memory_space=pltpu.VMEM)] * 2,
            scratch=[
                pltpu.VMEM((2, 2, PATCHES, width), bf16),
                pltpu.VMEM((2, 2, low, width), bf16),
                pltpu.SemaphoreType.DMA((8,)),
            ],
            after=after, moved=7 * 10**6,
        )

    def dense_sum(self, near, far):
        _, rows, width = near.shape
        cut, half, share = rows // 2, rows // 4, rows // 2 // self.dp
        place = [jnp.stack([lax.axis_index("expert"), lax.axis_index("dp")]).astype(jnp.int32)]
        more = self.to_core(far)
        after = yield None
        anywhere, on_chip = pl.BlockSpec(memory_space=pl.ANY), pl.BlockSpec(memory_space=pltpu.VMEM)
        scratch = [
            pltpu.VMEM((2, cut, width), bf16), pltpu.VMEM((2, 2, half, width), bf16), pltpu.SemaphoreType.DMA((6,)),
        ]
        side, other = launch(
            dense_first_kernel, "dense_first", [((cut, width), bf16), ((2, half, width), bf16)], [near, more],
            in_specs=[anywhere] * 2, scalars=place, scratch=scratch, after=after, moved=4 * 10**6,
        )
        from_side, from_other = self.to_side(side), self.to_other(other)
        after = yield side
        side, other, upper, lower = launch(
            dense_second_kernel, "dense_second",
            [((half, width), bf16), ((half, width), bf16), ((half, width), f32), ((half, width), f32)],
            [near, more, from_side, from_other], in_specs=[anywhere] * 2 + [on_chip] * 2, scalars=place,
            scratch=scratch, after=after, moved=5 * 10**6,
        )
        from_side, from_other = self.to_side(side), self.to_other(other)
        after = yield upper
        hops = range(1, self.dp)
        outs = launch(
            functools.partial(dense_third_kernel, self.dp), "dense_third",
            [((share, width), f32)] + [((share, width), bf16)] * len(hops),
            [upper, lower, from_side, from_other], scalars=place, scratch=[pltpu.VMEM((cut, width), f32)],
            after=after, moved=3 * 10**6,
        )
        moved = [self.along(outs[hop], hop) for hop in hops]
        after = yield outs[0]
        (total,) = launch(
            dense_fourth_kernel, "dense_fourth", [((share, width), bf16)], [outs[0], *moved], after=after,
            moved=10**6,
        )
        moved = [self.along(total, hop) for hop in hops]
        after = yield total
        (column,) = launch(
            functools.partial(dense_fifth_kernel, self.dp), "dense_fifth", [((cut, width), bf16)], [total, *moved],
            scalars=place, after=after, moved=10**6,
        )
        more = self.to_other(column)
        after = yield column
        yield launch(
            dense_last_kernel, "dense_last", [((rows * 3 // 4, width), f32), ((rows // 4, width), f32)],
            [column, more], scalars=place, scratch=[pltpu.VMEM((rows, width), f32)], after=after,
            moved=4 * 10**6,
        )


def local(
    links,
    tokens,
    cotangent,
    timesteps,
    ada_weight,
    ada_bias,
    qkv_weight,
    out_weight,
    router_weight,
    shared_up,
    shared_down,
    expert_up,
    expert_down,
    routes,
    places,
):
    rows, width = tokens.shape
    local_width = qkv_weight.shape[2]
    members = expert_up.shape[0]
    me = lax.axis_index("tensor")
    base = (lax.axis_index("expert") * members).astype(jnp.int32).reshape(1)
    everyone = ("dp", "expert", "tensor")
    total_blocks = links.dp * links.expert * links.tensor
    full = links.paired and links.dp == 4 and total_blocks * rows * width * 2 <= FULL_LIMIT

    condition = jax.nn.silu(embedding(timesteps, width)).astype(bf16)
    mod_cols = jnp.einsum("id,dcf->icf", condition, ada_weight, preferred_element_type=f32) + ada_bias[None]
    mod = lax.all_to_all(mod_cols, "tensor", split_axis=0, concat_axis=2, tiled=True)[0]
    own_condition = lax.dynamic_slice_in_dim(condition.astype(f32), me, 1, axis=0)
    shared_cot = (mod[5][None] * cotangent.astype(f32)).astype(bf16)

    weight = jnp.concatenate(
        [qkv_weight.transpose(1, 2, 0).reshape(3 * local_width, width), out_weight], axis=0
    )
    if full:
        (weight,) = ordered([weight], [mod])
    across = links.to_side(weight)
    near_shard = links.to_core(weight)
    if full:
        place = jnp.stack([base[0], *(lax.axis_index(axis) for axis in ("expert", "dp"))]).astype(jnp.int32)
        cot_column = links.column(jnp.broadcast_to(shared_cot[None], (links.dp, *shared_cot.shape)))
        cot_other = links.to_other(shared_cot)
        across, cot_other = ordered([across, cot_other], [mod])
        cot_side = links.to_side(ordered([shared_cot], [across])[0])
        cot_corner = links.to_other(cot_side)
    else:
        (across,) = ordered([across], [mod])
    shards = (weight, near_shard, across, links.to_core(across))
    router_t = router_weight.T
    pairs = jnp.concatenate([routes.T, places.T], axis=0)

    whole = slice(None)
    attn_in, qkv, context, attn_out, ext, ext_copies = attention_forward(
        tokens, mod, router_t, pairs, shards, local_width, links.dp if full else 1
    )
    feed = (shared_up, shared_down, expert_up, expert_down)

    def small_grads(small_all):
        condition_all = small_all[:, 6].astype(bf16)
        mod_grad = lax.dynamic_slice_in_dim(small_all[:, 0:6], me * local_width, local_width, axis=2)
        ada_grad = jnp.einsum(
            "id,icf->dcf", condition_all.astype(f32), mod_grad, precision=lax.Precision.HIGHEST
        )
        return ada_grad, jnp.sum(mod_grad, axis=0), jnp.sum(small_all[:, 8:16], axis=0).T

    backward = functools.partial(
        attention_backward, cond=own_condition, tokens=tokens, cotangent=cotangent, mod=mod, router_t=router_t,
        pairs=pairs, attn_in=attn_in, qkv=qkv, context=context, attn_out=attn_out, ext=ext, shards=shards,
        local_width=local_width,
    )
    if full:
        ext_side, ext_other = links.to_side(ext), links.to_other(ext)
        cut = PATCHES // 2 + EXTRA
        ext_cuts = (ext_other[:cut], ext_side[cut:])
        ext_corner = (links.to_side(ext_cuts[0]), links.to_other(ext_cuts[1]))
        ext_mine = assemble(
            (HALF, PATCHES + EXTRA, width), bf16, [ext, ext_side, ext_other, *ext_corner],
            [(index, whole, index) for index in range(3)]
            + [(3, whole, (3, pl.ds(0, cut))), (4, whole, (3, pl.ds(cut, PATCHES // 2)))],
        )
        ext_near = links.to_core(ext_mine)
        pieces = [shared_cot, cot_side, cot_other, cot_corner]
        cot_rest, cot_mine = launch(
            pick_both_kernel, "pick_both",
            [((links.dp - 1, PATCHES, width), bf16), ((HALF, PATCHES, width), bf16)], [*pieces, cot_column],
            in_specs=[pl.BlockSpec(memory_space=pl.ANY)] * (HALF + 1), scalars=[place],
            scratch=[pltpu.SemaphoreType.DMA((links.dp - 1 + HALF,))], after=[ext_mine], moved=5 * 10**6,
        )
        cots = lax.all_gather(cot_rest, ("expert", "tensor"), axis=0)
        cot_near = links.to_core(cot_mine)
        ext_column = links.column(ordered([ext_copies], [ext_side, ext_other])[0])
        own = (Blocks.apart(ext_mine, cot_mine), Blocks.apart(ext_near, cot_near))
        first, second = experts_both(base, own, *feed, (0, 1, 4, 5), after=[cot_rest])
        ext_rest, exts = links.column_rest(ext_column, place, [first])
        moved = links.to_core(second)
        side, other = links.plane_sum_first(first, moved, after=[ext_rest])
        slots = dispatch(base, own, members, after=[side])
        from_side, from_other = links.to_side(side), links.to_other(other)
        routed = routed_grads([slots], expert_up, expert_down, None)
        upper, lower, upper_next, lower_next = links.plane_sum_second(
            first, moved, from_side, from_other, after=[routed[0]]
        )
        upper_more, lower_more = links.to_other(upper_next), links.to_side(lower_next)
        shared = shared_grads(own, HALF, shared_up, shared_down, None, after=[upper, cots])
        output, tokens_grad, small, near, far = backward(
            upper, upper_more, lower, lower_more, after=[shared[0]]
        )
        dense = links.dense_sum(near, far)
        next(dense)
        small_all = lax.all_gather(small, everyone, axis=0)
        *shared, sent = shared_grads_other(exts, cots, 1, shared_up, shared_down, shared, after=[small])
        shared_more = links.to_next(sent)
        step = dense.send([sent])
        slots = dispatch_hops(base, exts, cots, members, after=[step])
        step = dense.send([slots[0]])
        for span in ((0, 2), (2, 3)):
            routed = routed_grads([slots], expert_up, expert_down, routed, after=[step], span=span)
            step = dense.send([routed[0]])
        shared = launch(
            shared_last_kernel, "shared_last", [(shared_up.shape, f32), (shared_down.shape, f32)],
            [*shared, shared_more], after=[step], moved=12 * 10**6,
        )
        ada_grad, ada_bias_grad, router_grad = small_grads(ordered([small_all], [shared[0]])[0])
        step = dense.send([shared[0], ada_grad.transpose(1, 2, 0)])
        routed = routed_grads([slots], expert_up, expert_down, routed, after=[step], span=(3, members))
        qkv_grad, out_grad = dense.send([routed[0]])
        routes_all = jnp.concatenate(
            [value[..., PATCHES, : TOPK * PATCHES].reshape(-1, TOPK * PATCHES) for value in (ext_mine, ext_near, exts)],
            axis=0,
        )
    else:
        shift = lax.axis_index("expert") * links.tensor
        gather = lambda block: jnp.roll(
            lax.all_gather(block, ("expert", "tensor"), axis=0), -shift, axis=0
        )
        all_ext, all_cot = gather(ext), gather(shared_cot)
        planes, sums = [], []
        for start in range(0, links.expert * links.tensor, 2 * HALF):
            spans = [slice(start + HALF * part, start + HALF * (part + 1)) for part in range(2)]
            planes.append(tuple(Blocks.apart(all_ext[span], all_cot[span]) for span in spans))
            shared_ids = tuple(range(links.tensor)) if start == 0 else ()
            sums += experts_both(base, planes[-1], *feed, shared_ids)
        blocks = jnp.roll(jnp.concatenate(sums, axis=0), shift, axis=0)
        total = lax.psum_scatter(blocks, ("expert", "tensor"), scatter_dimension=0, tiled=True)[0]
        upper, lower = total[:PATCHES].astype(f32), total[PATCHES:].astype(f32)
        output, tokens_grad, small, near, far = backward(
            upper, jnp.zeros_like(total[:PATCHES]), lower, jnp.zeros_like(total[PATCHES:])
        )
        small_all = lax.all_gather(small, everyone, axis=0)
        slots = [dispatch(base, plane, members) for plane in planes]
        routed = None
        for start in range(0, len(planes), 2):
            routed = routed_grads(slots[start : start + 2], expert_up, expert_down, routed)
        shared = shared_grads(planes[0][:1], HALF, shared_up, shared_down, None)
        routed = lax.psum(routed, "dp")
        shared = lax.psum(tuple(part[0] for part in shared), ("dp", "expert"))
        routes_all = lax.all_gather(routes.reshape(-1), everyone, axis=0)
        turn = jnp.arange(links.tensor) ^ me
        grads = jnp.stack([near, far], axis=1).reshape((-1,) + near.shape[1:])[turn]
        dense = lax.psum_scatter(grads, "tensor", scatter_dimension=0, tiled=True)[0]
        dense = lax.psum(dense, ("dp", "expert")).astype(f32)
        qkv_grad, out_grad = dense[: 3 * local_width], dense[3 * local_width :]
        ada_grad, ada_bias_grad, router_grad = small_grads(small_all)

    counts = jnp.sum(
        (routes_all[:, :, None] == jnp.arange(EXPERTS).astype(routes_all.dtype)).astype(jnp.int32),
        axis=(0, 1),
    )
    qkv_grad = qkv_grad.reshape(3, local_width, width).transpose(2, 0, 1)
    return (
        output,
        tokens_grad,
        ada_grad,
        ada_bias_grad,
        qkv_grad,
        out_grad,
        router_grad,
        shared[0],
        shared[1],
        routed[0],
        routed[1],
        counts,
    )


def solution(mesh):
    rows = P(("dp", "expert", "tensor"), None)
    placed = (
        rows,
        rows,
        P(("dp", "expert")),
        P(None, None, "tensor"),
        P(None, "tensor"),
        P(None, None, "tensor"),
        P("tensor", None),
        P(),
        P(None, "tensor"),
        P("tensor", None),
        P("expert", None, "tensor"),
        P("expert", "tensor", None),
        rows,
        rows,
    )
    return jax.shard_map(
        functools.partial(local, Links(mesh)),
        mesh=mesh,
        in_specs=placed,
        out_specs=(
            rows,
            rows,
            P(None, None, "tensor"),
            P(None, "tensor"),
            P(None, None, "tensor"),
            P("tensor", None),
            P(),
            P(None, "tensor"),
            P("tensor", None),
            P("expert", None, "tensor"),
            P("expert", "tensor", None),
            P(),
        ),
        check_vma=False,
    )
```
